32 devices in a mesh: box: 16 (over z, y, x), samp: 2 (over core).
Axes of the slice: x: 2, y: 2, z: 4, core: 2. Of those that a mesh axis runs over, the one named last changes fastest.
Arguments:
- currents: bfloat16 [128, 8, 128], P(('box', 'samp')), may hold values from -6 to 6
- radiation: bfloat16 [128, 2, 2, 512, 128], P(('box', 'samp')), may hold values from -0.1875 to 0.1875
- near_blocks: bfloat16 [128, 8, 2, 128, 128], P(('box', 'samp')), may hold values from -0.125 to 0.125
- near_src: int32 [128, 8], P(('box', 'samp')), may hold values from 0 to 127, as said below
- leaf_parent: int32 [128], P('box'), may hold values from 0 to 255, as said below
- leaf_shift: int32 [128], P('box'), may hold values from 0 to 7
- shift_table: bfloat16 [8, 2, 8192], P(None, None, 'samp'), may hold values from -4 to 4
- interp_idx: int32 [64, 2], P('samp'), may hold values from 0 to 3, as said below
- interp_val: bfloat16 [64, 2, 128, 128], P('samp'), may hold values from -0.375 to 0.375
- top_src: int32 [256, 16], P('box'), may hold values from 0 to 255, as said below
- top_disp: int32 [256, 16], P('box'), may hold values from 0 to 31
- trans_table: bfloat16 [32, 2, 8192], P(None, None, 'samp'), may hold values from -1 to 1
Outputs:
- matvec: float32 [128, 8, 128], P(('box', 'samp'))
The draws below stay inside these ranges and needn't reach their ends.
Inputs may be any that keep to these rules, and one draw needn't show every extreme that they name: `near_src`: entry 0 of a leaf's row is the leaf itself; every entry lies in the 4 leaves of the leaf's own device or of the devices just before and after it in box+samp order (leaves numbered box-major), and these ends are reached. `leaf_parent`: the parent of leaf l lies in its box group: its value divided by 16 equals l divided by 8. `interp_idx`: the 2 entries of a row differ. `top_src`: a source of top box t is another box of t's group (t // 16), or one of the last 8 boxes of the group before it, or one of the first 8 boxes of the group after it; both rims are reached.
All inputs are finite; a program needn't handle non-finite values.
Results may differ from the reference program's by a relative error of at most 0.013.
Values may be sent and summed in bfloat16 or wider, within the bound.
No kernel may reach another device: no remote copies, remote signals or barrier semaphores. Data moves between devices by JAX's collectives and lax.ppermute only.
A program may use at most 64 MiB of HBM per device.

```python
import jax
import jax.numpy as jnp
from jax import lax

EXC = 4
UNK = 128
KL = 512
KT = 8192
BLK = 128
IBLK = 2
NEAR = 8
ILIST = 16
NSHIFT = 8
NDISP = 32
LEAF_DEV = 4
TOP_DEV = 16
RIM = 8
GROUP_LEAVES = 8
NL = 128
NT = 256
N_SAMP = 2


def draw_near_src(key, part):
    leaves = jnp.arange(NL)
    first = leaves // LEAF_DEV * LEAF_DEV
    offsets = jax.random.randint(jax.random.fold_in(key, 11), (NL, NEAR - 1), -LEAF_DEV, 2 * LEAF_DEV)
    lowest = leaves % LEAF_DEV == 0
    highest = leaves % LEAF_DEV == LEAF_DEV - 1
    column_low = jnp.where(lowest, -LEAF_DEV, offsets[:, 0])
    column_high = jnp.where(highest, 2 * LEAF_DEV - 1, offsets[:, 1])
    flipped = jax.random.randint(jax.random.fold_in(key, 13), (NL,), 0, 2) == 1
    column_one = jnp.where(flipped, column_high, column_low)
    column_two = jnp.where(flipped, column_low, column_high)
    offsets = jnp.concatenate([column_one[:, None], column_two[:, None], offsets[:, 2:]], axis=1)
    sources = jnp.clip(first[:, None] + offsets, 0, NL - 1)
    return jnp.concatenate([leaves[:, None], sources], axis=1).astype(jnp.int32)


def draw_leaf_parent(key, part):
    leaves = jnp.arange(NL)
    group_index = leaves // GROUP_LEAVES
    choice_top = jax.random.randint(jax.random.fold_in(key, 23), (NL,), 0, TOP_DEV)
    return (group_index * TOP_DEV + choice_top).astype(jnp.int32)


def draw_interp_idx(key, part):
    block_rows = KT // BLK
    in_blocks = KL // BLK
    scores = jax.random.randint(jax.random.fold_in(key, 37), (block_rows, in_blocks), 0, 4096) * 64 + jnp.arange(in_blocks)[None, :]
    order = jnp.argsort(scores, axis=1, stable=True)
    return order[:, :IBLK].astype(jnp.int32)


def draw_top_src(key, part):
    targets = jnp.arange(NT)
    group_index = targets // TOP_DEV
    local = targets % TOP_DEV
    group_total = NT // TOP_DEV
    side = jax.random.randint(jax.random.fold_in(key, 41), (NT, ILIST), 0, 3) - 1
    side = jnp.where((group_index[:, None] == 0) & (side == -1), 0, side)
    side = jnp.where((group_index[:, None] == group_total - 1) & (side == 1), 0, side)
    step_own = jax.random.randint(jax.random.fold_in(key, 43), (NT, ILIST), 0, TOP_DEV - 1)
    own = group_index[:, None] * TOP_DEV + (local[:, None] + 1 + step_own) % TOP_DEV
    picks = jax.random.randint(jax.random.fold_in(key, 47), (NT, ILIST), 0, RIM)
    lower = (group_index[:, None] - 1) * TOP_DEV + TOP_DEV - RIM + picks
    upper = (group_index[:, None] + 1) * TOP_DEV + picks
    sources = jnp.where(side == -1, lower, jnp.where(side == 1, upper, own))
    force_low = (local == 0) & (group_index > 0)
    force_high = (local == TOP_DEV - 1) & (group_index < group_total - 1)
    column_low = jnp.where(force_low, (group_index - 1) * TOP_DEV + TOP_DEV - RIM, sources[:, 0])
    column_high = jnp.where(force_high, (group_index + 1) * TOP_DEV + RIM - 1, sources[:, 1])
    sources = jnp.concatenate([column_low[:, None], column_high[:, None], sources[:, 2:]], axis=1)
    return sources.astype(jnp.int32)


def place_ends(entries, key, smallest, high):
    extent = entries.shape
    place = [jax.random.randint(jax.random.fold_in(key, axis), (), 0, extent[axis]) for axis in range(len(extent))]
    entries = entries.at[tuple(place)].set(smallest)
    longest = extent.index(max(extent))
    place[longest] = (place[longest] + 1) % extent[longest]
    return entries.at[tuple(place)].set(high)


def steps_of(rng, extent, split, low, high):
    factor_of, own = 1.0, jax.random.fold_in(rng, 6)
    for position, blocks in split:
        draws = jnp.exp(jax.random.uniform(jax.random.fold_in(own, position), (blocks,), jnp.float32, low / len(split), high / len(split)))
        factor_of = factor_of * jnp.repeat(draws, extent[position] // blocks).reshape([-1 if axis == position else 1 for axis in range(len(extent))])
    return factor_of


def centred(key, shape, scale, most, split=(), dtype=jnp.bfloat16):
    level = steps_of(key, shape, split, -0.22, 0.18) if split else 1.0
    drawn = jax.random.normal(key, shape, jnp.float32) * scale * level
    return jnp.minimum(jnp.maximum(drawn, -most), most).astype(dtype)


def setup_inputs(seed: int = 0) -> dict:
    key_list = jax.random.split(jax.random.key(seed), 13)
    currents = centred(key_list[0], (NL, 2 * EXC, UNK), 1.0, 6.0, ((0, 32),))
    radiation = centred(key_list[1], (NL, 2, 2, KL, UNK), (2 * KL) ** -0.5, 0.1875, ((0, 32),))
    near_blocks = centred(key_list[2], (NL, NEAR, 2, UNK, UNK), (2 * NEAR * UNK) ** -0.5, 0.125, ((0, 32),))
    near_src = draw_near_src(jax.random.fold_in(key_list[12], 71), 0)
    leaf_parent = draw_leaf_parent(jax.random.fold_in(key_list[12], 71), 0)
    leaf_shift = place_ends(jax.random.randint(key_list[5], (NL,), 0, NSHIFT), jax.random.fold_in(key_list[5], 1), 0, NSHIFT - 1).astype(jnp.int32)
    shift_table = centred(key_list[6], (NSHIFT, 2, KT), 0.5, 4.0, ((2, 2),))
    interp_idx = draw_interp_idx(jax.random.fold_in(key_list[12], 71), 0)
    interp_val = centred(key_list[8], (KT // BLK, IBLK, BLK, BLK), (IBLK * BLK) ** -0.5, 0.375, ((0, 2),))
    top_src = draw_top_src(jax.random.fold_in(key_list[12], 71), 0)
    top_disp = place_ends(jax.random.randint(key_list[10], (NT, ILIST), 0, NDISP), jax.random.fold_in(key_list[10], 1), 0, NDISP - 1).astype(jnp.int32)
    trans_table = centred(key_list[11], (NDISP, 2, KT), (2 * ILIST) ** -0.5, 1.0, ((2, 2),))
    return {"currents": currents, "radiation": radiation, "near_blocks": near_blocks, "near_src": near_src, "leaf_parent": leaf_parent, "leaf_shift": leaf_shift, "shift_table": shift_table, "interp_idx": interp_idx, "interp_val": interp_val, "top_src": top_src, "top_disp": top_disp, "trans_table": trans_table}


HIGHEST = lax.Precision.HIGHEST


def complex_mul(a_real, a_imag, b_real, b_imag):
    return a_real * b_real - a_imag * b_imag, a_real * b_imag + a_imag * b_real


def reference(currents, radiation, near_blocks, near_src, leaf_parent, leaf_shift, shift_table, interp_idx, interp_val, top_src, top_disp, trans_table):
    comps = 4 * EXC
    half_comp = 2 * EXC
    groups = NT // TOP_DEV
    in_blocks = KL // BLK
    range_blocks = KT // BLK // N_SAMP

    def radiate_one(packed):
        rad_leaf, cur_leaf = packed
        rad_leaf = rad_leaf.astype(jnp.float32)
        cur_leaf = cur_leaf.astype(jnp.float32)
        rad_real = rad_leaf[:, 0]
        rad_imag = rad_leaf[:, 1]
        cur_real = cur_leaf[:EXC]
        cur_imag = cur_leaf[EXC:]
        form = "pqu,eu->peq"
        out_real = jnp.einsum(form, rad_real, cur_real) - jnp.einsum(form, rad_imag, cur_imag)
        out_imag = jnp.einsum(form, rad_real, cur_imag) + jnp.einsum(form, rad_imag, cur_real)
        return jnp.concatenate([out_real.reshape(half_comp, KL), out_imag.reshape(half_comp, KL)], axis=0).astype(jnp.bfloat16)

    leaf_pat = lax.map(radiate_one, (radiation, currents))
    val_float = interp_val.astype(jnp.float32)

    def up_group(packed):
        patterns, parents, shifts, group_index = packed
        picked = patterns.reshape(GROUP_LEAVES, comps, in_blocks, BLK)[:, :, interp_idx, :].astype(jnp.float32)
        moved = jnp.einsum("lcbri,brki->lcbk", picked, val_float).reshape(GROUP_LEAVES, comps, KT)
        shift_rows = shift_table[shifts].astype(jnp.float32)
        up_real, up_imag = complex_mul(moved[:, :half_comp], moved[:, half_comp:], shift_rows[:, 0:1], shift_rows[:, 1:2])
        shifted = jnp.concatenate([up_real, up_imag], axis=1)
        member = (parents[None, :] - group_index * TOP_DEV == jnp.arange(TOP_DEV)[:, None]).astype(jnp.float32)
        return jnp.einsum("tl,lck->tck", member, shifted, precision=HIGHEST).astype(jnp.bfloat16)

    group_ids = jnp.arange(groups).astype(jnp.int32)
    top_pat = lax.map(up_group, (leaf_pat.reshape(groups, GROUP_LEAVES, comps, KL), leaf_parent.reshape(groups, GROUP_LEAVES), leaf_shift.reshape(groups, GROUP_LEAVES), group_ids))
    top_pat = top_pat.reshape(NT, comps, KT)
    block_onehot = (interp_idx[:, :, None] == jnp.arange(in_blocks)[None, None, :]).astype(jnp.float32).reshape(N_SAMP, range_blocks, IBLK, in_blocks)
    val_ranges = val_float.reshape(N_SAMP, range_blocks, IBLK, BLK, BLK)

    def down_group(packed):
        sources, displace, parents, shifts, group_index = packed

        def add_entry(entry, total):
            source_rows = top_pat[sources[:, entry]].astype(jnp.float32)
            coeff = trans_table[displace[:, entry]].astype(jnp.float32)
            part_real, part_imag = complex_mul(coeff[:, 0:1], coeff[:, 1:2], source_rows[:, :half_comp], source_rows[:, half_comp:])
            return total + jnp.concatenate([part_real, part_imag], axis=1)

        incoming = lax.fori_loop(0, ILIST, add_entry, jnp.zeros((TOP_DEV, comps, KT), jnp.float32)).astype(jnp.bfloat16)
        spread = incoming[parents - group_index * TOP_DEV].astype(jnp.float32)
        shift_rows = shift_table[shifts].astype(jnp.float32)
        down_real, down_imag = complex_mul(shift_rows[:, 0:1], -shift_rows[:, 1:2], spread[:, :half_comp], spread[:, half_comp:])
        down = jnp.concatenate([down_real, down_imag], axis=1).astype(jnp.bfloat16).astype(jnp.float32)
        parts = jnp.einsum("lcsbk,sbrki->lcsbri", down.reshape(GROUP_LEAVES, comps, N_SAMP, range_blocks, BLK), val_ranges)
        folded = jnp.einsum("lcsbri,sbrq->lcsqi", parts, block_onehot, precision=HIGHEST)
        rounded = lax.optimization_barrier(folded.astype(jnp.bfloat16)).astype(jnp.float32)
        return jnp.sum(rounded, axis=2).reshape(GROUP_LEAVES, comps, KL).astype(jnp.bfloat16)

    far = lax.map(down_group, (top_src.reshape(groups, TOP_DEV, ILIST), top_disp.reshape(groups, TOP_DEV, ILIST), leaf_parent.reshape(groups, GROUP_LEAVES), leaf_shift.reshape(groups, GROUP_LEAVES), group_ids))
    far = far.reshape(NL, comps, KL)

    def leaf_out(packed):
        rad_leaf, far_leaf, blocks, sources = packed
        rad_leaf = rad_leaf.astype(jnp.float32)
        far_leaf = far_leaf.astype(jnp.float32)
        rad_real = rad_leaf[:, 0]
        rad_imag = rad_leaf[:, 1]
        far_real = far_leaf[:half_comp].reshape(2, EXC, KL)
        far_imag = far_leaf[half_comp:].reshape(2, EXC, KL)
        form = "pqu,peq->eu"
        recv_real = jnp.einsum(form, rad_real, far_real) + jnp.einsum(form, rad_imag, far_imag)
        recv_imag = jnp.einsum(form, rad_real, far_imag) - jnp.einsum(form, rad_imag, far_real)
        near_rows = currents[sources].astype(jnp.float32)
        blocks = blocks.astype(jnp.float32)
        form_near = "nuv,nev->eu"
        near_real = jnp.einsum(form_near, blocks[:, 0], near_rows[:, :EXC]) - jnp.einsum(form_near, blocks[:, 1], near_rows[:, EXC:])
        near_imag = jnp.einsum(form_near, blocks[:, 0], near_rows[:, EXC:]) + jnp.einsum(form_near, blocks[:, 1], near_rows[:, :EXC])
        return jnp.concatenate([recv_real + near_real, recv_imag + near_imag], axis=0)

    return lax.map(leaf_out, (radiation, far, near_blocks, near_src))
```

```python
import functools

import jax
import jax.numpy as jnp
from jax import lax
from jax.experimental import pallas as pl
from jax.experimental.pallas import tpu as pltpu
from jax.sharding import PartitionSpec as P

F32 = jnp.float32
BF16 = jnp.bfloat16
ANY = pl.BlockSpec(memory_space=pl.ANY)
VMEM = pl.BlockSpec(memory_space=pltpu.VMEM)
SMEM = pl.BlockSpec(memory_space=pltpu.SMEM)
NT = (((1,), (1,)), ((), ()))
LIMIT = 48 * 1024 * 1024


def params():
    return pltpu.CompilerParams(vmem_limit_bytes=LIMIT)


def radiate_kernel(cur_ref, meta_ref, rad_hbm, msg_ref, rad_ref, sem):
    leaf_count, in_blocks = cur_ref.shape[0], msg_ref.shape[0]
    block = msg_ref.shape[2]
    half = cur_ref.shape[1] // 2
    copies = [
        pltpu.make_async_copy(rad_hbm.at[leaf], rad_ref.at[leaf], sem.at[leaf])
        for leaf in range(leaf_count)
    ]
    for copy in copies:
        copy.start()
    base = leaf_count * 4 * half
    meta = meta_ref[...]
    zero = jnp.zeros((half, cur_ref.shape[2]), F32)
    left = []
    for leaf in range(leaf_count):
        cur = cur_ref[leaf].astype(F32)
        real, imag = cur[:half], cur[half:]
        pieces = [
            jnp.concatenate(rows, axis=0).astype(BF16)
            for rows in (
                (real, zero, imag, zero),
                (-imag, zero, real, zero),
                (zero, real, zero, imag),
                (zero, -imag, zero, real),
            )
        ]
        left.append(jnp.concatenate(pieces, axis=1))
        row = base + leaf // in_blocks * 4 * half
        msg_ref[leaf % in_blocks, row : row + 4 * half, :] = jnp.concatenate(
            [cur, meta], axis=0
        ).astype(BF16)
    for leaf in range(leaf_count):
        copies[leaf].wait()
        right = jnp.concatenate(
            [rad_ref[leaf, p, r] for p in range(2) for r in range(2)], axis=1
        )
        out = lax.dot_general(left[leaf], right, NT, preferred_element_type=F32).astype(BF16)
        for b in range(in_blocks):
            msg_ref[b, leaf * 4 * half : (leaf + 1) * 4 * half, :] = out[
                :, b * block : (b + 1) * block
            ]


def field_kernel(
    idx_ref,
    rep_ref,
    sid_ref,
    own_ref,
    slot_ref,
    disp_ref,
    me_ref,
    prev_hbm,
    here_hbm,
    next_hbm,
    val_ref,
    shift_ref,
    trans_ref,
    *rest,
    n_samp,
    leaf_count,
    entries,
):
    outs = rest[:n_samp]
    msg_ref, top_ref, down_ref, acc_ref, sem = rest[n_samp:]
    step = pl.program_id(0)
    tile = val_ref.shape[0]
    block = val_ref.shape[2]
    leaves = top_ref.shape[0] - 1
    group = leaves // 3
    rows = 16 * leaf_count

    @pl.when(step == 0)
    def _():
        copies = [
            pltpu.make_async_copy(src, msg_ref.at[pl.ds(g * n_samp, n_samp)], sem.at[g])
            for g, src in enumerate((prev_hbm, here_hbm, next_hbm))
        ]
        for copy in copies:
            copy.start()
        acc_ref[...] = jnp.zeros_like(acc_ref)
        top_ref[leaves] = jnp.zeros(top_ref.shape[1:], F32)
        for copy in copies:
            copy.wait()

    def row(ref, index, b):
        return jnp.broadcast_to(ref[index, b : b + 1, :], (8, block))

    for b in range(tile):
        first, second = idx_ref[(step * tile + b) * 2], idx_ref[(step * tile + b) * 2 + 1]
        left = jnp.concatenate(
            [msg_ref[:, first, :rows, :], msg_ref[:, second, :rows, :]], axis=2
        ).reshape(leaves * 16, 2 * block)
        right = jnp.concatenate([val_ref[b, 0], val_ref[b, 1]], axis=1)
        moved = lax.dot_general(left, right, NT, preferred_element_type=F32)
        for s in range(leaves):
            real, imag = moved[s * 16 : s * 16 + 8], moved[s * 16 + 8 : s * 16 + 16]
            shift_real = row(shift_ref, 2 * sid_ref[s], b)
            shift_imag = row(shift_ref, 2 * sid_ref[s] + 1, b)
            up_real = real * shift_real - imag * shift_imag
            up_imag = real * shift_imag + imag * shift_real
            rep = rep_ref[s]
            fresh = rep == s
            top_ref[rep, 0, b] = jnp.where(fresh, 0.0, top_ref[rep, 0, b]) + up_real
            top_ref[rep, 1, b] = jnp.where(fresh, 0.0, top_ref[rep, 1, b]) + up_imag

    def target(leaf, carry):
        real = [jnp.zeros((8, block), F32) for _ in range(tile)]
        imag = [jnp.zeros((8, block), F32) for _ in range(tile)]
        for j in range(entries):
            slot, disp = slot_ref[leaf * entries + j], disp_ref[leaf * entries + j]
            for b in range(tile):
                coef_real = row(trans_ref, 2 * disp, b)
                coef_imag = row(trans_ref, 2 * disp + 1, b)
                src_real, src_imag = top_ref[slot, 0, b], top_ref[slot, 1, b]
                real[b] += coef_real * src_real - coef_imag * src_imag
                imag[b] += coef_real * src_imag + coef_imag * src_real
        sid = own_ref[leaf]
        for b in range(tile):
            shift_real = row(shift_ref, 2 * sid, b)
            shift_imag = row(shift_ref, 2 * sid + 1, b)
            down = jnp.concatenate(
                [
                    shift_real * real[b] + shift_imag * imag[b],
                    shift_real * imag[b] - shift_imag * real[b],
                ],
                axis=0,
            )
            down_ref[b, pl.ds(pl.multiple_of(leaf * 16, 16), 16), :] = down.astype(BF16)
        return carry

    lax.fori_loop(0, group, target, 0)

    for b in range(tile):
        first, second = idx_ref[(step * tile + b) * 2], idx_ref[(step * tile + b) * 2 + 1]
        right = jnp.concatenate([val_ref[b, 0], val_ref[b, 1]], axis=1)
        part = jnp.dot(down_ref[b], right, preferred_element_type=F32)
        acc_ref[first] += part[:, :block]
        acc_ref[second] += part[:, block:]

    @pl.when(step == pl.num_programs(0) - 1)
    def _():
        me = me_ref[0]
        for d, out in enumerate(outs):
            owner = lax.rem(me + d, n_samp)
            start = pl.multiple_of(owner * rows, rows)
            out[...] = acc_ref[:, pl.ds(start, rows), :].astype(BF16)


def near_kernel(src_ref, prev_hbm, here_hbm, next_hbm, near_hbm, out_ref, cur_ref, near_ref, sem):
    leaf_count, near = near_ref.shape[:2]
    n_samp = prev_hbm.shape[0]
    in_blocks = prev_hbm.shape[1]
    extra = cur_ref.shape[2]
    base = prev_hbm.shape[2] - extra
    copies = [
        pltpu.make_async_copy(
            src.at[:, :, pl.ds(base, extra), :], cur_ref.at[pl.ds(g * n_samp, n_samp)], sem.at[g]
        )
        for g, src in enumerate((prev_hbm, here_hbm, next_hbm))
    ] + [
        pltpu.make_async_copy(near_hbm.at[leaf], near_ref.at[leaf], sem.at[3 + leaf])
        for leaf in range(leaf_count)
    ]
    for copy in copies:
        copy.start()
    for copy in copies[:3]:
        copy.wait()
    for leaf in range(leaf_count):
        left = []
        right = []
        for n in range(near):
            src = src_ref[leaf * near + n]
            piece, inner = src // leaf_count, lax.rem(src, leaf_count)
            start = pl.multiple_of(inner // in_blocks * 16, 16)
            both = cur_ref[piece, lax.rem(inner, in_blocks), pl.ds(start, 16), :].astype(F32)
            real, imag = both[:4], both[4:8]
            left.append(both[:8].astype(BF16))
            left.append(jnp.concatenate([-imag, real], axis=0).astype(BF16))
        copies[3 + leaf].wait()
        for n in range(near):
            right += [near_ref[leaf, n, 0], near_ref[leaf, n, 1]]
        out_ref[leaf] = lax.dot_general(
            jnp.concatenate(left, axis=1),
            jnp.concatenate(right, axis=1),
            NT,
            preferred_element_type=F32,
        )


def receive_kernel(near_ref, rad_hbm, *rest, n_samp):
    far_refs = rest[:n_samp]
    out_ref, rad_ref, sem = rest[n_samp:]
    leaf_count = out_ref.shape[0]
    copies = [
        pltpu.make_async_copy(rad_hbm.at[leaf], rad_ref.at[leaf], sem.at[leaf])
        for leaf in range(leaf_count)
    ]
    for copy in copies:
        copy.start()
    far = far_refs[0][...].astype(F32)
    for ref in far_refs[1:]:
        far = far + ref[...].astype(F32)
    in_blocks = far.shape[0]
    unknowns = rad_ref.shape[4]
    depth = rad_ref.shape[1] * rad_ref.shape[2] * rad_ref.shape[3]
    for leaf in range(leaf_count):
        left = []
        for p in range(2):
            real = [far[b, leaf * 16 + p * 4 : leaf * 16 + p * 4 + 4] for b in range(in_blocks)]
            imag = [
                far[b, leaf * 16 + 8 + p * 4 : leaf * 16 + 12 + p * 4] for b in range(in_blocks)
            ]
            left += [jnp.concatenate(pair, axis=0) for pair in zip(real, imag)]
            left += [jnp.concatenate([i, -r], axis=0) for r, i in zip(real, imag)]
        wide = jnp.concatenate(left, axis=1).astype(BF16)
        copies[leaf].wait()
        right = rad_ref[leaf].reshape(depth, unknowns)
        out_ref[leaf] = near_ref[leaf] + jnp.dot(wide, right, preferred_element_type=F32)


def per_device(
    currents,
    radiation,
    near_blocks,
    near_src,
    leaf_parent,
    leaf_shift,
    shift_table,
    interp_idx,
    interp_val,
    top_src,
    top_disp,
    trans_table,
):
    n_samp = lax.axis_size("samp")
    n_box = lax.axis_size("box")
    group_index = lax.axis_index("box")
    me = lax.axis_index("samp")
    leaf_count, comps, unknowns = currents.shape
    group = leaf_parent.shape[0]
    top_count, entries = top_src.shape
    local_blocks, _, block, _ = interp_val.shape
    in_blocks = radiation.shape[3] // block
    near = near_src.shape[1]
    leaves = 3 * group
    rows = 16 * leaf_count
    extra = 16 * -(-leaf_count // in_blocks)
    tile = min(8, local_blocks)
    steps = local_blocks // tile

    parent_local = leaf_parent - group_index * top_count
    meta = jnp.zeros((8, block), F32)
    meta = meta.at[0, :group].set(parent_local.astype(F32))
    meta = meta.at[1, :group].set(leaf_shift.astype(F32))

    message = pl.pallas_call(
        radiate_kernel,
        out_shape=jax.ShapeDtypeStruct((in_blocks, rows + extra, block), BF16),
        in_specs=[VMEM, VMEM, ANY],
        out_specs=VMEM,
        scratch_shapes=[
            pltpu.VMEM(radiation.shape, BF16),
            pltpu.SemaphoreType.DMA((leaf_count,)),
        ],
        compiler_params=params(),
        name="radiate",
    )(currents, meta, radiation)
    here = lax.all_gather(message, "samp", axis=0)
    before = lax.ppermute(here, "box", [(i, i + 1) for i in range(n_box - 1)])
    after = lax.ppermute(here, "box", [(i + 1, i) for i in range(n_box - 1)])

    def numbers(piece):
        found = piece[0, 0, rows + 8 : rows + 10, :group].astype(jnp.int32)
        return found[0], found[1]

    parent_before, shift_before = numbers(before)
    parent_after, shift_after = numbers(after)
    parents = jnp.concatenate(
        [parent_before, parent_local + top_count, parent_after + 2 * top_count]
    )
    shifts = jnp.concatenate([shift_before, leaf_shift, shift_after])
    order = jnp.arange(leaves, dtype=jnp.int32)
    rep = jnp.min(
        jnp.where(parents[:, None] == parents[None, :], order[None, :], leaves), axis=1
    )
    chosen = (parent_local[:, None] == jnp.arange(top_count)[None, :])[:, :, None]
    sources = jnp.sum(jnp.where(chosen, top_src[None], 0), axis=1)
    sources = sources - (group_index - 1) * top_count
    displace = jnp.sum(jnp.where(chosen, top_disp[None], 0), axis=1)
    slots = jnp.min(
        jnp.where(sources[:, :, None] == parents[None, None, :], order[None, None, :], leaves),
        axis=2,
    )
    shift_rows = shift_table.astype(F32).reshape(-1, local_blocks, block)
    trans_rows = trans_table.astype(F32).reshape(-1, local_blocks, block)

    fars = pl.pallas_call(
        functools.partial(
            field_kernel, n_samp=n_samp, leaf_count=leaf_count, entries=entries
        ),
        out_shape=[jax.ShapeDtypeStruct((in_blocks, rows, block), BF16)] * n_samp,
        grid=(steps,),
        in_specs=[SMEM] * 7
        + [ANY] * 3
        + [
            pl.BlockSpec((tile, 2, block, block), lambda t: (t, 0, 0, 0)),
            pl.BlockSpec((shift_rows.shape[0], tile, block), lambda t: (0, t, 0)),
            pl.BlockSpec((trans_rows.shape[0], tile, block), lambda t: (0, t, 0)),
        ],
        out_specs=[pl.BlockSpec((in_blocks, rows, block), lambda t: (0, 0, 0))] * n_samp,
        scratch_shapes=[
            pltpu.VMEM((3 * n_samp,) + message.shape, BF16),
            pltpu.VMEM((leaves + 1, 2, tile, 8, block), F32),
            pltpu.VMEM((tile, group * 16, block), BF16),
            pltpu.VMEM((in_blocks, group * 16, block), F32),
            pltpu.SemaphoreType.DMA((3,)),
        ],
        compiler_params=params(),
        name="field",
    )(
        interp_idx.reshape(-1),
        rep,
        shifts,
        leaf_shift,
        slots.reshape(-1),
        displace.reshape(-1),
        me[None],
        before,
        here,
        after,
        interp_val,
        shift_rows,
        trans_rows,
    )
    received = [fars[0]] + [
        lax.ppermute(fars[d], "samp", [(i, (i + d) % n_samp) for i in range(n_samp)])
        for d in range(1, n_samp)
    ]
    near_out = pl.pallas_call(
        near_kernel,
        out_shape=jax.ShapeDtypeStruct((leaf_count, comps, unknowns), F32),
        in_specs=[SMEM] + [ANY] * 4,
        out_specs=VMEM,
        scratch_shapes=[
            pltpu.VMEM((3 * n_samp, in_blocks, extra, block), BF16),
            pltpu.VMEM(near_blocks.shape, BF16),
            pltpu.SemaphoreType.DMA((3 + leaf_count,)),
        ],
        compiler_params=params(),
        name="near",
    )(
        (near_src - (group_index - 1) * group).reshape(-1),
        before,
        here,
        after,
        near_blocks,
    )
    return pl.pallas_call(
        functools.partial(receive_kernel, n_samp=n_samp),
        out_shape=jax.ShapeDtypeStruct((leaf_count, comps, unknowns), F32),
        in_specs=[VMEM, ANY] + [VMEM] * n_samp,
        out_specs=VMEM,
        scratch_shapes=[
            pltpu.VMEM(radiation.shape, BF16),
            pltpu.SemaphoreType.DMA((leaf_count,)),
        ],
        compiler_params=params(),
        name="receive",
    )(near_out, radiation, *received)


def solution(mesh):
    placed = (
        P(("box", "samp"), None, None),
        P(("box", "samp"), None, None, None, None),
        P(("box", "samp"), None, None, None, None),
        P(("box", "samp"), None),
        P("box"),
        P("box"),
        P(None, None, "samp"),
        P("samp", None),
        P("samp", None, None, None),
        P("box", None),
        P("box", None),
        P(None, None, "samp"),
    )
    return jax.shard_map(
        per_device,
        mesh=mesh,
        in_specs=placed,
        out_specs=P(("box", "samp"), None, None),
        check_vma=False,
    )
```

```python
import functools

import jax
import jax.numpy as jnp
from jax import lax
from jax.experimental import pallas as pl
from jax.experimental.pallas import tpu as pltpu
from jax.sharding import PartitionSpec as P

F32 = jnp.float32
BF16 = jnp.bfloat16
HBM = pl.BlockSpec(memory_space=pltpu.HBM)
VMEM = pl.BlockSpec(memory_space=pltpu.VMEM)
SMEM = pl.BlockSpec(memory_space=pltpu.SMEM)
NT = (((1,), (1,)), ((), ()))
LIMIT = 24 * 1024 * 1024


def params():
    return pltpu.CompilerParams(vmem_limit_bytes=LIMIT)


def radiate_kernel(parent_ref, shift_ref, cur_hbm, rad_hbm, msg_ref, cur_ref, rad_ref, sem, *, top_count):
    leaf_count, in_blocks = cur_ref.shape[0], msg_ref.shape[0]
    block = msg_ref.shape[2]
    half = cur_ref.shape[1] // 2
    group = parent_ref.shape[0]
    first = pltpu.make_async_copy(cur_hbm, cur_ref, sem.at[leaf_count])
    first.start()
    copies = [
        pltpu.make_async_copy(rad_hbm.at[leaf], rad_ref.at[leaf], sem.at[leaf])
        for leaf in range(leaf_count)
    ]
    for copy in copies:
        copy.start()
    base = leaf_count * 4 * half
    lane = lax.broadcasted_iota(jnp.int32, (8, block), 1)
    line = lax.broadcasted_iota(jnp.int32, (8, block), 0)
    meta = jnp.zeros((8, block), jnp.int32)
    for member in range(group):
        pair = jnp.where(
            line == 0, lax.rem(parent_ref[member], top_count), shift_ref[member]
        )
        meta = jnp.where(lane == member, pair, meta)
    meta = meta.astype(F32)
    zero = jnp.zeros((half, cur_ref.shape[2]), F32)
    first.wait()
    left = []
    for leaf in range(leaf_count):
        cur = cur_ref[leaf].astype(F32)
        real, imag = cur[:half], cur[half:]
        pieces = [
            jnp.concatenate(rows, axis=0).astype(BF16)
            for rows in (
                (real, zero, imag, zero),
                (-imag, zero, real, zero),
                (zero, real, zero, imag),
                (zero, -imag, zero, real),
            )
        ]
        left.append(jnp.concatenate(pieces, axis=1))
        row = base + leaf // in_blocks * 4 * half
        msg_ref[leaf % in_blocks, row : row + 4 * half, :] = jnp.concatenate(
            [cur, meta], axis=0
        ).astype(BF16)
    for leaf in range(leaf_count):
        copies[leaf].wait()
        right = jnp.concatenate(
            [rad_ref[leaf, p, r] for p in range(2) for r in range(2)], axis=1
        )
        out = lax.dot_general(left[leaf], right, NT, preferred_element_type=F32).astype(BF16)
        for b in range(in_blocks):
            msg_ref[b, leaf * 4 * half : (leaf + 1) * 4 * half, :] = out[
                :, b * block : (b + 1) * block
            ]


def field_kernel(
    idx_ref,
    parent_ref,
    sid_ref,
    src_ref,
    disp_ref,
    pair_ref,
    side_ref,
    val_ref,
    shift_ref,
    trans_ref,
    *rest,
    n_samp,
    leaf_count,
):
    outs = rest[:n_samp]
    (
        top_ref,
        inc_ref,
        down_ref,
        acc_ref,
        meta_ref,
        num_ref,
        box_ref,
        rep_ref,
        count_ref,
        slot_ref,
        coef_ref,
        sem,
    ) = rest[n_samp:]
    tile = top_ref.shape[2]
    block = val_ref.shape[2]
    leaves = top_ref.shape[0]
    group = leaves // 3
    rows = 16 * leaf_count
    top_count, entries = src_ref.shape
    where = lax.axis_index("box")
    odd = lax.rem(where, 2)
    bases = (1 - odd, 2 - odd, 2 * odd)

    lines = []
    for both in (
        pair_ref[0, 0, rows : rows + 16, :],
        pair_ref[n_samp, 0, rows : rows + 16, :],
        side_ref[odd * n_samp, 0, rows : rows + 16, :],
    ):
        lines.append(both.astype(F32)[8:10])
    lines.append(lines[0])
    meta_ref[...] = jnp.concatenate(lines, axis=0).astype(jnp.int32)
    fetch = pltpu.make_async_copy(meta_ref, num_ref, sem)
    fetch.start()
    acc_ref[...] = jnp.zeros_like(acc_ref)
    for box in range(3 * top_count):
        box_ref[box] = -1
    fetch.wait()
    boxes = [num_ref[2 * (s // group), s % group] + bases[s // group] * top_count for s in range(leaves)]
    for s in reversed(range(leaves)):
        box_ref[boxes[s]] = s
    for s in range(leaves):
        rep_ref[s] = box_ref[boxes[s]]

    def listing(leaf, carry):
        parent = parent_ref[leaf] - where * top_count
        count = jnp.int32(0)
        for j in range(entries):
            slot = box_ref[src_ref[parent, j] - (where - 1) * top_count]
            slot_ref[leaf, count] = slot
            coef_ref[leaf, count] = 2 * disp_ref[parent, j]
            count += (slot >= 0).astype(jnp.int32)
        count_ref[leaf] = count
        return carry

    lax.fori_loop(0, group, listing, 0)

    def row(ref, index, t, b):
        return jnp.broadcast_to(ref[index, t, b : b + 1, :], (8, block))

    def slab(t, carry):
        for b in range(tile):
            first, second = idx_ref[t * tile + b, 0], idx_ref[t * tile + b, 1]
            left = jnp.concatenate(
                [
                    jnp.concatenate(
                        [
                            pair_ref[:, use, :rows, :],
                            side_ref[pl.ds(odd * n_samp, n_samp), use, :rows, :],
                        ],
                        axis=0,
                    ).reshape(leaves * 16, block)
                    for use in (first, second)
                ],
                axis=1,
            )
            right = jnp.concatenate([val_ref[t * tile + b, 0], val_ref[t * tile + b, 1]], axis=1)
            moved = lax.dot_general(left, right, NT, preferred_element_type=F32)
            for s in range(leaves):
                real, imag = moved[s * 16 : s * 16 + 8], moved[s * 16 + 8 : s * 16 + 16]
                sid = num_ref[2 * (s // group) + 1, s % group]
                shift_real = row(shift_ref, 2 * sid, t, b)
                shift_imag = row(shift_ref, 2 * sid + 1, t, b)
                top_ref[s, 0, b] = real * shift_real - imag * shift_imag
                top_ref[s, 1, b] = real * shift_imag + imag * shift_real

        def merge(s, carry):
            rep = rep_ref[s]

            @pl.when(rep != s)
            def _():
                top_ref[rep] = top_ref[rep] + top_ref[s]

            return carry

        lax.fori_loop(0, leaves, merge, 0)

        def target(leaf, carry):
            @pl.when(rep_ref[odd * group + leaf] == odd * group + leaf)
            def _():
                def entry(n, total):
                    slot, coef = slot_ref[leaf, n], coef_ref[leaf, n]
                    real, imag = list(total[:tile]), list(total[tile:])
                    for b in range(tile):
                        coef_real = row(trans_ref, coef, t, b)
                        coef_imag = row(trans_ref, coef + 1, t, b)
                        src_real, src_imag = top_ref[slot, 0, b], top_ref[slot, 1, b]
                        real[b] += coef_real * src_real - coef_imag * src_imag
                        imag[b] += coef_real * src_imag + coef_imag * src_real
                    return tuple(real + imag)

                zero = jnp.zeros((8, block), F32)
                total = lax.fori_loop(0, count_ref[leaf], entry, (zero,) * (2 * tile))
                for b in range(tile):
                    inc_ref[leaf, 0, b] = total[b]
                    inc_ref[leaf, 1, b] = total[tile + b]

            return carry

        lax.fori_loop(0, group, target, 0)

        for leaf in range(group):
            sid = 2 * sid_ref[leaf]
            rep = rep_ref[odd * group + leaf] - odd * group
            for b in range(tile):
                shift_real = row(shift_ref, sid, t, b)
                shift_imag = row(shift_ref, sid + 1, t, b)
                real, imag = inc_ref[rep, 0, b], inc_ref[rep, 1, b]
                down = jnp.concatenate(
                    [
                        shift_real * real + shift_imag * imag,
                        shift_real * imag - shift_imag * real,
                    ],
                    axis=0,
                )
                down_ref[b, leaf * 16 : leaf * 16 + 16, :] = down.astype(BF16)

        for b in range(tile):
            first, second = idx_ref[t * tile + b, 0], idx_ref[t * tile + b, 1]
            right = jnp.concatenate([val_ref[t * tile + b, 0], val_ref[t * tile + b, 1]], axis=1)
            part = jnp.dot(down_ref[b], right, preferred_element_type=F32)
            acc_ref[first] += part[:, :block]
            acc_ref[second] += part[:, block:]
        return carry

    lax.fori_loop(0, val_ref.shape[0] // tile, slab, 0)

    me = lax.axis_index("samp")
    for d, out in enumerate(outs):
        owner = lax.rem(me + d, n_samp)
        start = pl.multiple_of(owner * rows, rows)
        out[...] = acc_ref[:, pl.ds(start, rows), :].astype(BF16)


def near_kernel(src_ref, pair_ref, side_ref, near_hbm, out_ref, cur_ref, near_ref, sem, *, rows, n_samp):
    leaf_count, near = near_ref.shape[:2]
    in_blocks = pair_ref.shape[1]
    group = n_samp * leaf_count
    copies = [
        pltpu.make_async_copy(near_hbm.at[leaf], near_ref.at[leaf], sem.at[leaf])
        for leaf in range(leaf_count)
    ]
    for copy in copies:
        copy.start()
    where = lax.axis_index("box")
    odd = lax.rem(where, 2)
    for ref, base, place in (
        (pair_ref, 0, 1 - odd),
        (pair_ref, n_samp, 2 - odd),
        (side_ref, odd * n_samp, 2 * odd),
    ):
        for leaf in range(group):
            samp, inner = leaf // leaf_count, leaf % leaf_count
            line = rows + inner // in_blocks * 16
            cur = ref[base + samp, inner % in_blocks, line : line + 16, :].astype(F32)
            cur_ref[place * group + leaf] = jnp.concatenate(
                [cur[:8], -cur[4:8], cur[:4]], axis=0
            ).astype(BF16)
    for leaf in range(leaf_count):
        left = jnp.concatenate(
            [cur_ref[src_ref[leaf, n] - (where - 1) * group] for n in range(near)], axis=1
        )
        copies[leaf].wait()
        out = [
            lax.dot_general(
                left,
                jnp.concatenate([near_ref[leaf, n, r] for n in range(near)], axis=1),
                NT,
                preferred_element_type=F32,
            )
            for r in range(2)
        ]
        out_ref[leaf] = out[0][:8] + out[1][8:]


def receive_kernel(near_ref, rad_ref, *rest):
    far_refs, out_ref = rest[:-1], rest[-1]
    leaf_count = out_ref.shape[0]
    far = far_refs[0][...].astype(F32)
    for ref in far_refs[1:]:
        far = far + ref[...].astype(F32)
    in_blocks = far.shape[0]
    unknowns = rad_ref.shape[4]
    depth = rad_ref.shape[1] * rad_ref.shape[2] * rad_ref.shape[3]
    for leaf in range(leaf_count):
        left = []
        for p in range(2):
            real = [far[b, leaf * 16 + p * 4 : leaf * 16 + p * 4 + 4] for b in range(in_blocks)]
            imag = [
                far[b, leaf * 16 + 8 + p * 4 : leaf * 16 + 12 + p * 4] for b in range(in_blocks)
            ]
            left += [jnp.concatenate(pair, axis=0) for pair in zip(real, imag)]
            left += [jnp.concatenate([i, -r], axis=0) for r, i in zip(real, imag)]
        wide = jnp.concatenate(left, axis=1).astype(BF16)
        right = rad_ref[leaf].reshape(depth, unknowns)
        out_ref[leaf] = near_ref[leaf] + jnp.dot(wide, right, preferred_element_type=F32)


def per_device(
    currents,
    radiation,
    near_blocks,
    near_src,
    leaf_parent,
    leaf_shift,
    shift_table,
    interp_idx,
    interp_val,
    top_src,
    top_disp,
    trans_table,
):
    n_samp = lax.axis_size("samp")
    n_box = lax.axis_size("box")
    leaf_count, comps, unknowns = currents.shape
    group = leaf_parent.shape[0]
    top_count, entries = top_src.shape
    local_blocks, _, block, _ = interp_val.shape
    in_blocks = radiation.shape[3] // block
    leaves = 3 * group
    rows = 16 * leaf_count
    extra = 16 * -(-leaf_count // in_blocks)
    tile = min(16, local_blocks)
    slabs = local_blocks // tile

    message = pl.pallas_call(
        functools.partial(radiate_kernel, top_count=top_count),
        out_shape=jax.ShapeDtypeStruct((in_blocks, rows + extra, block), BF16),
        in_specs=[SMEM, SMEM, HBM, HBM],
        out_specs=VMEM,
        scratch_shapes=[
            pltpu.VMEM(currents.shape, BF16),
            pltpu.VMEM(radiation.shape, BF16),
            pltpu.SemaphoreType.DMA((leaf_count + 1,)),
        ],
        compiler_params=params(),
        name="radiate",
    )(leaf_parent, leaf_shift, currents, radiation)

    def around(start):
        members = [
            [(box + step) % n_box * n_samp + samp for step in range(2) for samp in range(n_samp)]
            for box in range(start, n_box, 2)
        ]
        return lax.all_gather(message, ("box", "samp"), axis=0, axis_index_groups=members)

    pair, side = around(0), around(1)
    shift_rows = shift_table.astype(F32).reshape(-1, slabs, tile, block)
    trans_rows = trans_table.astype(F32).reshape(-1, slabs, tile, block)

    fars = pl.pallas_call(
        functools.partial(field_kernel, n_samp=n_samp, leaf_count=leaf_count),
        out_shape=[jax.ShapeDtypeStruct((in_blocks, rows, block), BF16)] * n_samp,
        in_specs=[SMEM] * 5 + [VMEM] * 5,
        out_specs=[VMEM] * n_samp,
        scratch_shapes=[
            pltpu.VMEM((leaves, 2, tile, 8, block), F32),
            pltpu.VMEM((group, 2, tile, 8, block), F32),
            pltpu.VMEM((tile, group * 16, block), BF16),
            pltpu.VMEM((in_blocks, group * 16, block), F32),
            pltpu.VMEM((8, block), jnp.int32),
            pltpu.SMEM((8, block), jnp.int32),
            pltpu.SMEM((3 * top_count,), jnp.int32),
            pltpu.SMEM((leaves,), jnp.int32),
            pltpu.SMEM((group,), jnp.int32),
            pltpu.SMEM((group, entries), jnp.int32),
            pltpu.SMEM((group, entries), jnp.int32),
            pltpu.SemaphoreType.DMA,
        ],
        compiler_params=params(),
        name="field",
    )(
        interp_idx,
        leaf_parent,
        leaf_shift,
        top_src,
        top_disp,
        pair,
        side,
        interp_val,
        shift_rows,
        trans_rows,
    )
    received = [fars[0]] + [
        lax.ppermute(fars[d], "samp", [(i, (i + d) % n_samp) for i in range(n_samp)])
        for d in range(1, n_samp)
    ]
    near_out = pl.pallas_call(
        functools.partial(near_kernel, rows=rows, n_samp=n_samp),
        out_shape=jax.ShapeDtypeStruct((leaf_count, comps, unknowns), F32),
        in_specs=[SMEM, VMEM, VMEM, HBM],
        out_specs=VMEM,
        scratch_shapes=[
            pltpu.VMEM((leaves, 16, block), BF16),
            pltpu.VMEM(near_blocks.shape, BF16),
            pltpu.SemaphoreType.DMA((leaf_count,)),
        ],
        compiler_params=params(),
        name="near",
    )(near_src, pair, side, near_blocks)
    return pl.pallas_call(
        receive_kernel,
        out_shape=jax.ShapeDtypeStruct((leaf_count, comps, unknowns), F32),
        in_specs=[VMEM] * (2 + n_samp),
        out_specs=VMEM,
        compiler_params=params(),
        name="receive",
    )(near_out, radiation, *received)


def solution(mesh):
    placed = (
        P(("box", "samp"), None, None),
        P(("box", "samp"), None, None, None, None),
        P(("box", "samp"), None, None, None, None),
        P(("box", "samp"), None),
        P("box"),
        P("box"),
        P(None, None, "samp"),
        P("samp", None),
        P("samp", None, None, None),
        P("box", None),
        P("box", None),
        P(None, None, "samp"),
    )
    return jax.shard_map(
        per_device,
        mesh=mesh,
        in_specs=placed,
        out_specs=P(("box", "samp"), None, None),
        check_vma=False,
    )
```

```python
import functools

import jax
import jax.numpy as jnp
from jax import lax
from jax.experimental import pallas as pl
from jax.experimental.pallas import tpu as pltpu
from jax.sharding import PartitionSpec as P

F32 = jnp.float32
BF16 = jnp.bfloat16
HBM = pl.BlockSpec(memory_space=pltpu.HBM)
VMEM = pl.BlockSpec(memory_space=pltpu.VMEM)
SMEM = pl.BlockSpec(memory_space=pltpu.SMEM)
NT = (((1,), (1,)), ((), ()))
LIMIT = 24 * 1024 * 1024


def params():
    return pltpu.CompilerParams(vmem_limit_bytes=LIMIT)


def pinned(*arrays):
    return [pltpu.with_memory_space_constraint(array, pltpu.HBM) for array in arrays]


def radiate_kernel(
    parent_hbm, shift_hbm, cur_hbm, rad_hbm, msg_ref, parent_ref, shift_ref, cur_ref, rad_ref, sem, *, top_count
):
    leaf_count, in_blocks = cur_ref.shape[0], msg_ref.shape[0]
    block = msg_ref.shape[2]
    half = cur_ref.shape[1] // 2
    group = parent_ref.shape[0]
    firsts = [
        pltpu.make_async_copy(src, dst, sem.at[leaf_count + n])
        for n, (src, dst) in enumerate(
            ((parent_hbm, parent_ref), (shift_hbm, shift_ref), (cur_hbm, cur_ref))
        )
    ]
    for copy in firsts:
        copy.start()
    copies = [
        pltpu.make_async_copy(rad_hbm.at[leaf], rad_ref.at[leaf], sem.at[leaf])
        for leaf in range(leaf_count)
    ]
    for copy in copies:
        copy.start()
    base = leaf_count * 4 * half
    lane = lax.broadcasted_iota(jnp.int32, (8, block), 1)
    line = lax.broadcasted_iota(jnp.int32, (8, block), 0)
    meta = jnp.zeros((8, block), jnp.int32)
    for copy in firsts:
        copy.wait()
    for member in range(group):
        pair = jnp.where(
            line == 0, lax.rem(parent_ref[member], top_count), shift_ref[member]
        )
        meta = jnp.where(lane == member, pair, meta)
    meta = meta.astype(F32)
    zero = jnp.zeros((half, cur_ref.shape[2]), F32)
    left = []
    for leaf in range(leaf_count):
        cur = cur_ref[leaf].astype(F32)
        real, imag = cur[:half], cur[half:]
        pieces = [
            jnp.concatenate(rows, axis=0).astype(BF16)
            for rows in (
                (real, zero, imag, zero),
                (-imag, zero, real, zero),
                (zero, real, zero, imag),
                (zero, -imag, zero, real),
            )
        ]
        left.append(jnp.concatenate(pieces, axis=1))
        row = base + leaf // in_blocks * 4 * half
        msg_ref[leaf % in_blocks, row : row + 4 * half, :] = jnp.concatenate(
            [cur, meta], axis=0
        ).astype(BF16)
    for leaf in range(leaf_count):
        copies[leaf].wait()
        right = jnp.concatenate(
            [rad_ref[leaf, p, r] for p in range(2) for r in range(2)], axis=1
        )
        out = lax.dot_general(left[leaf], right, NT, preferred_element_type=F32).astype(BF16)
        for b in range(in_blocks):
            msg_ref[b, leaf * 4 * half : (leaf + 1) * 4 * half, :] = out[
                :, b * block : (b + 1) * block
            ]


def field_kernel(
    idx_ref,
    parent_ref,
    sid_ref,
    src_ref,
    disp_ref,
    here_ref,
    ends_ref,
    val_hbm,
    shift_ref,
    trans_ref,
    *rest,
    n_samp,
    leaf_count,
):
    outs = rest[:n_samp]
    (
        top_ref,
        inc_ref,
        down_ref,
        acc_ref,
        meta_ref,
        num_ref,
        box_ref,
        rep_ref,
        count_ref,
        slot_ref,
        coef_ref,
        val_ref,
        sem,
        val_sem,
    ) = rest[n_samp:]
    tile = top_ref.shape[2]
    block = val_ref.shape[2]
    leaves = top_ref.shape[0]
    group = leaves // 3
    rows = 16 * leaf_count
    top_count, entries = src_ref.shape
    where = lax.axis_index("box")
    slabs = val_ref.shape[0] // tile
    loads = [
        pltpu.make_async_copy(
            val_hbm.at[pl.ds(t * tile, tile)], val_ref.at[pl.ds(t * tile, tile)], val_sem.at[t]
        )
        for t in range(slabs)
    ]
    for load in loads:
        load.start()

    lines = [
        both.astype(F32)[8:10]
        for both in (
            ends_ref[0, 0, 0, rows : rows + 16, :],
            here_ref[0, 0, rows : rows + 16, :],
            ends_ref[n_samp - 1, 0, 0, rows : rows + 16, :],
        )
    ]
    lines.append(lines[0])
    meta_ref[...] = jnp.concatenate(lines, axis=0).astype(jnp.int32)
    fetch = pltpu.make_async_copy(meta_ref, num_ref, sem)
    fetch.start()
    acc_ref[...] = jnp.zeros_like(acc_ref)
    for box in range(3 * top_count):
        box_ref[box] = -1
    fetch.wait()
    boxes = [num_ref[2 * (s // group), s % group] + s // group * top_count for s in range(leaves)]
    for s in reversed(range(leaves)):
        box_ref[boxes[s]] = s
    for s in range(leaves):
        rep_ref[s] = box_ref[boxes[s]]

    def listing(leaf, carry):
        parent = parent_ref[leaf] - where * top_count
        count = jnp.int32(0)
        slots = [box_ref[src_ref[parent, j] - (where - 1) * top_count] for j in range(entries)]
        coefs = [2 * disp_ref[parent, j] for j in range(entries)]
        for slot, coef in zip(slots, coefs):
            slot_ref[leaf, count] = slot
            coef_ref[leaf, count] = coef
            count += (slot >= 0).astype(jnp.int32)
        count_ref[leaf] = count
        return carry

    lax.fori_loop(0, group, listing, 0)

    def row(ref, index, t, b):
        return jnp.broadcast_to(ref[index, t, b : b + 1, :], (8, block))

    def slab(t, carry):
        pltpu.make_async_copy(
            val_hbm.at[pl.ds(t * tile, tile)], val_ref.at[pl.ds(t * tile, tile)], val_sem.at[t]
        ).wait()
        for b in range(tile):
            first, second = idx_ref[t * tile + b, 0], idx_ref[t * tile + b, 1]
            left = jnp.concatenate(
                [
                    jnp.concatenate(
                        [
                            ends_ref[0, :, use, :rows, :],
                            here_ref[:, use, :rows, :],
                            ends_ref[n_samp - 1, :, use, :rows, :],
                        ],
                        axis=0,
                    ).reshape(leaves * 16, block)
                    for use in (first, second)
                ],
                axis=1,
            )
            right = jnp.concatenate([val_ref[t * tile + b, 0], val_ref[t * tile + b, 1]], axis=1)
            moved = lax.dot_general(left, right, NT, preferred_element_type=F32)
            for s in range(leaves):
                real, imag = moved[s * 16 : s * 16 + 8], moved[s * 16 + 8 : s * 16 + 16]
                sid = num_ref[2 * (s // group) + 1, s % group]
                shift_real = row(shift_ref, 2 * sid, t, b)
                shift_imag = row(shift_ref, 2 * sid + 1, t, b)
                top_ref[s, 0, b] = real * shift_real - imag * shift_imag
                top_ref[s, 1, b] = real * shift_imag + imag * shift_real

        def merge(s, carry):
            rep = rep_ref[s]

            @pl.when(rep != s)
            def _():
                top_ref[rep] = top_ref[rep] + top_ref[s]

            return carry

        lax.fori_loop(0, leaves, merge, 0)

        def target(leaf, carry):
            @pl.when(rep_ref[group + leaf] == group + leaf)
            def _():
                def entry(n, total):
                    slot, coef = slot_ref[leaf, n], coef_ref[leaf, n]
                    real, imag = list(total[:tile]), list(total[tile:])
                    for b in range(tile):
                        coef_real = row(trans_ref, coef, t, b)
                        coef_imag = row(trans_ref, coef + 1, t, b)
                        src_real, src_imag = top_ref[slot, 0, b], top_ref[slot, 1, b]
                        real[b] += coef_real * src_real - coef_imag * src_imag
                        imag[b] += coef_real * src_imag + coef_imag * src_real
                    return tuple(real + imag)

                zero = jnp.zeros((8, block), F32)
                total = lax.fori_loop(0, count_ref[leaf], entry, (zero,) * (2 * tile))
                for b in range(tile):
                    inc_ref[leaf, 0, b] = total[b]
                    inc_ref[leaf, 1, b] = total[tile + b]

            return carry

        lax.fori_loop(0, group, target, 0)

        for leaf in range(group):
            sid = 2 * sid_ref[leaf]
            rep = rep_ref[group + leaf] - group
            for b in range(tile):
                shift_real = row(shift_ref, sid, t, b)
                shift_imag = row(shift_ref, sid + 1, t, b)
                real, imag = inc_ref[rep, 0, b], inc_ref[rep, 1, b]
                down = jnp.concatenate(
                    [
                        shift_real * real + shift_imag * imag,
                        shift_real * imag - shift_imag * real,
                    ],
                    axis=0,
                )
                down_ref[b, leaf * 16 : leaf * 16 + 16, :] = down.astype(BF16)

        for b in range(tile):
            first, second = idx_ref[t * tile + b, 0], idx_ref[t * tile + b, 1]
            right = jnp.concatenate([val_ref[t * tile + b, 0], val_ref[t * tile + b, 1]], axis=1)
            part = jnp.dot(down_ref[b], right, preferred_element_type=F32)
            acc_ref[first] += part[:, :block]
            acc_ref[second] += part[:, block:]
        return carry

    lax.fori_loop(0, slabs, slab, 0)

    me = lax.axis_index("samp")
    for d, out in enumerate(outs):
        owner = lax.rem(me + d, n_samp)
        start = pl.multiple_of(owner * rows, rows)
        out[...] = acc_ref[:, pl.ds(start, rows), :].astype(BF16)


def near_kernel(src_ref, here_ref, ends_ref, near_hbm, out_ref, cur_ref, near_ref, sem, *, rows, n_samp):
    leaf_count, near = near_ref.shape[:2]
    in_blocks = here_ref.shape[1]
    group = n_samp * leaf_count
    copies = [
        pltpu.make_async_copy(near_hbm.at[leaf], near_ref.at[leaf], sem.at[leaf])
        for leaf in range(leaf_count)
    ]
    for copy in copies:
        copy.start()
    where = lax.axis_index("box")
    for place, ref in enumerate((ends_ref.at[0], here_ref, ends_ref.at[n_samp - 1])):
        for leaf in range(group):
            samp, inner = leaf // leaf_count, leaf % leaf_count
            line = rows + inner // in_blocks * 16
            cur = ref[samp, inner % in_blocks, line : line + 16, :].astype(F32)
            cur_ref[place * group + leaf] = jnp.concatenate(
                [cur[:8], -cur[4:8], cur[:4]], axis=0
            ).astype(BF16)
    for leaf in range(leaf_count):
        left = jnp.concatenate(
            [cur_ref[src_ref[leaf, n] - (where - 1) * group] for n in range(near)], axis=1
        )
        copies[leaf].wait()
        out = [
            lax.dot_general(
                left,
                jnp.concatenate([near_ref[leaf, n, r] for n in range(near)], axis=1),
                NT,
                preferred_element_type=F32,
            )
            for r in range(2)
        ]
        out_ref[leaf] = out[0][:8] + out[1][8:]


def receive_kernel(near_ref, rad_ref, *rest):
    far_refs, out_ref = rest[:-1], rest[-1]
    leaf_count = out_ref.shape[0]
    far = far_refs[0][...].astype(F32)
    for ref in far_refs[1:]:
        far = far + ref[...].astype(F32)
    in_blocks = far.shape[0]
    unknowns = rad_ref.shape[4]
    depth = rad_ref.shape[1] * rad_ref.shape[2] * rad_ref.shape[3]
    for leaf in range(leaf_count):
        left = []
        for p in range(2):
            real = [far[b, leaf * 16 + p * 4 : leaf * 16 + p * 4 + 4] for b in range(in_blocks)]
            imag = [
                far[b, leaf * 16 + 8 + p * 4 : leaf * 16 + 12 + p * 4] for b in range(in_blocks)
            ]
            left += [jnp.concatenate(pair, axis=0) for pair in zip(real, imag)]
            left += [jnp.concatenate([i, -r], axis=0) for r, i in zip(real, imag)]
        wide = jnp.concatenate(left, axis=1).astype(BF16)
        right = rad_ref[leaf].reshape(depth, unknowns)
        out_ref[leaf] = near_ref[leaf] + jnp.dot(wide, right, preferred_element_type=F32)


def per_device(
    currents,
    radiation,
    near_blocks,
    near_src,
    leaf_parent,
    leaf_shift,
    shift_table,
    interp_idx,
    interp_val,
    top_src,
    top_disp,
    trans_table,
):
    n_samp = lax.axis_size("samp")
    n_box = lax.axis_size("box")
    leaf_count, comps, unknowns = currents.shape
    group = leaf_parent.shape[0]
    top_count, entries = top_src.shape
    local_blocks, _, block, _ = interp_val.shape
    in_blocks = radiation.shape[3] // block
    leaves = 3 * group
    rows = 16 * leaf_count
    extra = 16 * -(-leaf_count // in_blocks)
    tile = min(16, local_blocks)
    slabs = local_blocks // tile

    message = pl.pallas_call(
        functools.partial(radiate_kernel, top_count=top_count),
        out_shape=jax.ShapeDtypeStruct((in_blocks, rows + extra, block), BF16),
        in_specs=[HBM] * 4,
        out_specs=VMEM,
        scratch_shapes=[
            pltpu.SMEM(leaf_parent.shape, jnp.int32),
            pltpu.SMEM(leaf_shift.shape, jnp.int32),
            pltpu.VMEM(currents.shape, BF16),
            pltpu.VMEM(radiation.shape, BF16),
            pltpu.SemaphoreType.DMA((leaf_count + 3,)),
        ],
        compiler_params=params(),
        name="radiate",
    )(*pinned(leaf_parent, leaf_shift, currents, radiation))

    here = lax.all_gather(message, "samp", axis=0)
    last = n_samp - 1
    swap = []
    for box in range(n_box - 1):
        low, high = box * n_samp + last, (box + 1) * n_samp
        swap += [(low, high), (high, low)]
    beyond = lax.ppermute(here, ("box", "samp"), swap)
    ends = lax.all_gather(beyond, "samp", axis=0)

    shift_rows = shift_table.astype(F32).reshape(-1, slabs, tile, block)
    trans_rows = trans_table.astype(F32).reshape(-1, slabs, tile, block)

    fars = pl.pallas_call(
        functools.partial(field_kernel, n_samp=n_samp, leaf_count=leaf_count),
        out_shape=[jax.ShapeDtypeStruct((in_blocks, rows, block), BF16)] * n_samp,
        in_specs=[SMEM] * 5 + [VMEM] * 2 + [HBM] + [VMEM] * 2,
        out_specs=[VMEM] * n_samp,
        scratch_shapes=[
            pltpu.VMEM((leaves, 2, tile, 8, block), F32),
            pltpu.VMEM((group, 2, tile, 8, block), F32),
            pltpu.VMEM((tile, group * 16, block), BF16),
            pltpu.VMEM((in_blocks, group * 16, block), F32),
            pltpu.VMEM((8, block), jnp.int32),
            pltpu.SMEM((8, block), jnp.int32),
            pltpu.SMEM((3 * top_count,), jnp.int32),
            pltpu.SMEM((leaves,), jnp.int32),
            pltpu.SMEM((group,), jnp.int32),
            pltpu.SMEM((group, entries), jnp.int32),
            pltpu.SMEM((group, entries), jnp.int32),
            pltpu.VMEM(interp_val.shape, BF16),
            pltpu.SemaphoreType.DMA,
            pltpu.SemaphoreType.DMA((slabs,)),
        ],
        compiler_params=params(),
        name="field",
    )(
        interp_idx,
        leaf_parent,
        leaf_shift,
        top_src,
        top_disp,
        here,
        ends,
        *pinned(interp_val),
        shift_rows,
        trans_rows,
    )
    received = [fars[0]] + [
        lax.ppermute(fars[d], "samp", [(i, (i + d) % n_samp) for i in range(n_samp)])
        for d in range(1, n_samp)
    ]
    near_out = pl.pallas_call(
        functools.partial(near_kernel, rows=rows, n_samp=n_samp),
        out_shape=jax.ShapeDtypeStruct((leaf_count, comps, unknowns), F32),
        in_specs=[SMEM, VMEM, VMEM, HBM],
        out_specs=VMEM,
        scratch_shapes=[
            pltpu.VMEM((leaves, 16, block), BF16),
            pltpu.VMEM(near_blocks.shape, BF16),
            pltpu.SemaphoreType.DMA((leaf_count,)),
        ],
        compiler_params=params(),
        name="near",
    )(near_src, here, ends, *pinned(near_blocks))
    return pl.pallas_call(
        receive_kernel,
        out_shape=jax.ShapeDtypeStruct((leaf_count, comps, unknowns), F32),
        in_specs=[VMEM] * (2 + n_samp),
        out_specs=VMEM,
        compiler_params=params(),
        name="receive",
    )(near_out, radiation, *received)


def solution(mesh):
    placed = (
        P(("box", "samp"), None, None),
        P(("box", "samp"), None, None, None, None),
        P(("box", "samp"), None, None, None, None),
        P(("box", "samp"), None),
        P("box"),
        P("box"),
        P(None, None, "samp"),
        P("samp", None),
        P("samp", None, None, None),
        P("box", None),
        P("box", None),
        P(None, None, "samp"),
    )
    return jax.shard_map(
        per_device,
        mesh=mesh,
        in_specs=placed,
        out_specs=P(("box", "samp"), None, None),
        check_vma=False,
    )
```

```python
import functools

import jax
import jax.numpy as jnp
from jax import lax
from jax.experimental import pallas as pl
from jax.experimental.pallas import tpu as pltpu
from jax.sharding import PartitionSpec as P

F32 = jnp.float32
BF16 = jnp.bfloat16
HBM = pl.BlockSpec(memory_space=pltpu.HBM)
VMEM = pl.BlockSpec(memory_space=pltpu.VMEM)
SMEM = pl.BlockSpec(memory_space=pltpu.SMEM)
NT = (((1,), (1,)), ((), ()))
LIMIT = 24 * 1024 * 1024


def params():
    return pltpu.CompilerParams(vmem_limit_bytes=LIMIT)


def pinned(*arrays):
    return [pltpu.with_memory_space_constraint(array, pltpu.HBM) for array in arrays]


def radiate_kernel(
    parent_hbm, shift_hbm, cur_hbm, rad_hbm, msg_ref, parent_ref, shift_ref, cur_ref, rad_ref, sem, *, top_count
):
    leaf_count, in_blocks = cur_ref.shape[0], msg_ref.shape[0]
    block = msg_ref.shape[2]
    half = cur_ref.shape[1] // 2
    group = parent_ref.shape[0]
    firsts = [
        pltpu.make_async_copy(src, dst, sem.at[leaf_count + n])
        for n, (src, dst) in enumerate(
            ((parent_hbm, parent_ref), (shift_hbm, shift_ref), (cur_hbm, cur_ref))
        )
    ]
    for copy in firsts:
        copy.start()
    copies = [
        pltpu.make_async_copy(rad_hbm.at[leaf], rad_ref.at[leaf], sem.at[leaf])
        for leaf in range(leaf_count)
    ]
    for copy in copies:
        copy.start()
    base = leaf_count * 4 * half
    lane = lax.broadcasted_iota(jnp.int32, (8, block), 1)
    line = lax.broadcasted_iota(jnp.int32, (8, block), 0)
    meta = jnp.zeros((8, block), jnp.int32)
    for copy in firsts:
        copy.wait()
    for member in range(group):
        pair = jnp.where(
            line == 0, lax.rem(parent_ref[member], top_count), shift_ref[member]
        )
        meta = jnp.where(lane == member, pair, meta)
    meta = meta.astype(F32)
    zero = jnp.zeros((half, cur_ref.shape[2]), F32)
    left = []
    for leaf in range(leaf_count):
        cur = cur_ref[leaf].astype(F32)
        real, imag = cur[:half], cur[half:]
        pieces = [
            jnp.concatenate(rows, axis=0).astype(BF16)
            for rows in (
                (real, zero, imag, zero),
                (-imag, zero, real, zero),
                (zero, real, zero, imag),
                (zero, -imag, zero, real),
            )
        ]
        left.append(jnp.concatenate(pieces, axis=1))
        row = base + leaf // in_blocks * 4 * half
        msg_ref[leaf % in_blocks, row : row + 4 * half, :] = jnp.concatenate(
            [cur, meta], axis=0
        ).astype(BF16)
    for leaf in range(leaf_count):
        copies[leaf].wait()
        right = jnp.concatenate(
            [rad_ref[leaf, p, r] for p in range(2) for r in range(2)], axis=1
        )
        out = lax.dot_general(left[leaf], right, NT, preferred_element_type=F32).astype(BF16)
        for b in range(in_blocks):
            msg_ref[b, leaf * 4 * half : (leaf + 1) * 4 * half, :] = out[
                :, b * block : (b + 1) * block
            ]


def raise_group(msg_ref, sids, idx_ref, val_ref, shift_ref, up_ref, base, rows):
    block = val_ref.shape[2]
    local_blocks = val_ref.shape[0]
    count = len(sids)
    width = min(4, local_blocks)

    def some(step, carry):
        for inner in range(width):
            b = step * width + inner
            left = jnp.concatenate(
                [
                    msg_ref[:, idx_ref[b, r], :rows, :].reshape(count * 16, block)
                    for r in range(2)
                ],
                axis=1,
            )
            right = jnp.concatenate([val_ref[b, 0], val_ref[b, 1]], axis=1)
            moved = lax.dot_general(left, right, NT, preferred_element_type=F32)
            for s, sid in enumerate(sids):
                real, imag = moved[s * 16 : s * 16 + 8], moved[s * 16 + 8 : s * 16 + 16]
                shift_real, shift_imag = shift_ref[2 * sid, b], shift_ref[2 * sid + 1, b]
                up_ref[base + s, 0, b] = real * shift_real - imag * shift_imag
                up_ref[base + s, 1, b] = real * shift_imag + imag * shift_real
        return carry

    lax.fori_loop(0, local_blocks // width, some, 0)


def spread_rows(src_ref, out_ref):
    count, local_blocks, block = src_ref.shape

    def one(index, carry):
        for b in range(local_blocks):
            out_ref[index, b] = jnp.broadcast_to(src_ref[index, b : b + 1, :], (8, block))
        return carry

    lax.fori_loop(0, count, one, 0)


def tables_kernel(
    idx_ref,
    sid_ref,
    here_ref,
    val_hbm,
    shift_ref,
    trans_ref,
    val_ref,
    dense_ref,
    wide_shift_ref,
    wide_trans_ref,
    up_ref,
    sem,
    *,
    rows,
):
    load = pltpu.make_async_copy(val_hbm, val_ref, sem)
    load.start()
    spread_rows(shift_ref, wide_shift_ref)
    load.wait()
    local_blocks, _, block, _ = val_ref.shape
    sids = [sid_ref[s] for s in range(sid_ref.shape[0])]
    raise_group(here_ref, sids, idx_ref, val_ref, wide_shift_ref, up_ref, 0, rows)

    def one(b, carry):
        first, second = idx_ref[b, 0], idx_ref[b, 1]
        zero = jnp.zeros((block, block), BF16)
        for c in range(dense_ref.shape[1] // block):
            dense_ref[pl.ds(pl.multiple_of(b * block, block), block), c * block : (c + 1) * block] = (
                jnp.where(first == c, val_ref[b, 0], jnp.where(second == c, val_ref[b, 1], zero))
            )
        return carry

    lax.fori_loop(0, local_blocks, one, 0)
    spread_rows(trans_ref, wide_trans_ref)


def meta_of(msg_ref, rows):
    return msg_ref[0, 0, rows : rows + 16, :].astype(F32)[8:10]


def raise_kernel(idx_ref, msg_ref, val_ref, shift_ref, up_ref, meta_ref, num_ref, sem, *, rows):
    group = up_ref.shape[0]
    meta = meta_of(msg_ref, rows)
    meta_ref[...] = jnp.concatenate([meta] * 4, axis=0).astype(jnp.int32)
    fetch = pltpu.make_async_copy(meta_ref, num_ref, sem)
    fetch.start()
    fetch.wait()
    sids = [num_ref[1, s] for s in range(group)]
    raise_group(msg_ref, sids, idx_ref, val_ref, shift_ref, up_ref, 0, rows)


def field_kernel(
    idx_ref,
    parent_ref,
    sid_ref,
    src_ref,
    disp_ref,
    here_ref,
    near_ref,
    far_ref,
    near_up_hbm,
    here_up_hbm,
    val_ref,
    dense_ref,
    shift_ref,
    trans_ref,
    *rest,
    n_samp,
    leaf_count,
    tile,
):
    outs = rest[:n_samp]
    (
        top_ref,
        inc_ref,
        down_ref,
        acc_ref,
        meta_ref,
        num_ref,
        box_ref,
        rep_ref,
        count_ref,
        slot_ref,
        coef_ref,
        sem,
    ) = rest[n_samp:]
    block = val_ref.shape[2]
    local_blocks = val_ref.shape[0]
    leaves = top_ref.shape[0]
    group = leaves // 3
    rows = 16 * leaf_count
    top_count, entries = src_ref.shape
    where = lax.axis_index("box")
    me = lax.axis_index("samp")
    turned = jnp.where(me == 1, 1, 0) if n_samp == 2 else jnp.int32(0)
    bases = (1, 2 * turned, 2 - 2 * turned)

    moves = [
        pltpu.make_async_copy(src, top_ref.at[pl.ds(g * group, group)], sem.at[1 + g])
        for g, src in enumerate((here_up_hbm, near_up_hbm))
    ]
    lines = [meta_of(ref, rows) for ref in (here_ref, near_ref, far_ref)]
    meta_ref[...] = jnp.concatenate(lines + lines[:1], axis=0).astype(jnp.int32)
    fetch = pltpu.make_async_copy(meta_ref, num_ref, sem.at[0])
    fetch.start()
    for move in moves:
        move.start()
    for box in range(3 * top_count):
        box_ref[box] = -1
    fetch.wait()
    sids = [num_ref[5, s] for s in range(group)]
    raise_group(far_ref, sids, idx_ref, val_ref, shift_ref, top_ref, 2 * group, rows)
    boxes = [
        num_ref[2 * (s // group), s % group] + bases[s // group] * top_count for s in range(leaves)
    ]
    for s in reversed(range(leaves)):
        box_ref[boxes[s]] = s
    for s in range(leaves):
        rep_ref[s] = box_ref[boxes[s]]

    def listing(leaf, carry):
        parent = parent_ref[leaf] - where * top_count
        count = jnp.int32(0)
        slots = [box_ref[src_ref[parent, j] - (where - 1) * top_count] for j in range(entries)]
        coefs = [2 * disp_ref[parent, j] for j in range(entries)]
        for slot, coef in zip(slots, coefs):
            slot_ref[leaf, count] = slot
            coef_ref[leaf, count] = coef
            count += (slot >= 0).astype(jnp.int32)
        count_ref[leaf] = count
        return carry

    lax.fori_loop(0, group, listing, 0)
    for move in moves:
        move.wait()

    def merge(s, carry):
        rep = rep_ref[s]

        @pl.when(rep != s)
        def _():
            top_ref[rep] = top_ref[rep] + top_ref[s]

        return carry

    lax.fori_loop(0, leaves, merge, 0)

    def target(leaf, carry):
        @pl.when(rep_ref[leaf] == leaf)
        def _():
            for t in range(local_blocks // tile):

                def entry(n, total):
                    slot, coef = slot_ref[leaf, n], coef_ref[leaf, n]
                    real, imag = list(total[:tile]), list(total[tile:])
                    for b in range(tile):
                        place = t * tile + b
                        coef_real, coef_imag = trans_ref[coef, place], trans_ref[coef + 1, place]
                        src_real, src_imag = top_ref[slot, 0, place], top_ref[slot, 1, place]
                        real[b] += coef_real * src_real - coef_imag * src_imag
                        imag[b] += coef_real * src_imag + coef_imag * src_real
                    return tuple(real + imag)

                zero = jnp.zeros((8, block), F32)
                total = lax.fori_loop(0, count_ref[leaf], entry, (zero,) * (2 * tile))
                for b in range(tile):
                    inc_ref[leaf, 0, t * tile + b] = total[b]
                    inc_ref[leaf, 1, t * tile + b] = total[tile + b]

        return carry

    lax.fori_loop(0, group, target, 0)

    def lower(leaf, carry):
        sid = 2 * sid_ref[leaf]
        rep = rep_ref[leaf]
        start = pl.multiple_of(leaf * 16, 16)
        for b in range(local_blocks):
            shift_real, shift_imag = shift_ref[sid, b], shift_ref[sid + 1, b]
            real, imag = inc_ref[rep, 0, b], inc_ref[rep, 1, b]
            down = jnp.concatenate(
                [
                    shift_real * real + shift_imag * imag,
                    shift_real * imag - shift_imag * real,
                ],
                axis=0,
            )
            down_ref[pl.ds(start, 16), b * block : (b + 1) * block] = down.astype(BF16)
        return carry

    lax.fori_loop(0, group, lower, 0)
    acc_ref[...] = jnp.dot(down_ref[...], dense_ref[...], preferred_element_type=F32)
    for d, out in enumerate(outs):
        owner = lax.rem(me + d, n_samp)
        start = pl.multiple_of(owner * rows, rows)
        for c in range(out.shape[0]):
            out[c] = acc_ref[pl.ds(start, rows), c * block : (c + 1) * block].astype(BF16)


def near_kernel(src_ref, here_ref, first_ref, second_ref, near_hbm, out_ref, cur_ref, near_ref, sem, *, rows, n_samp):
    leaf_count, near = near_ref.shape[:2]
    in_blocks = here_ref.shape[1]
    group = n_samp * leaf_count
    copies = [
        pltpu.make_async_copy(near_hbm.at[leaf], near_ref.at[leaf], sem.at[leaf])
        for leaf in range(leaf_count)
    ]
    for copy in copies:
        copy.start()
    where = lax.axis_index("box")
    turned = jnp.where(lax.axis_index("samp") == 1, 1, 0) if n_samp == 2 else jnp.int32(0)
    for place, ref in ((1, here_ref), (2 * turned, first_ref), (2 - 2 * turned, second_ref)):
        for leaf in range(group):
            samp, inner = leaf // leaf_count, leaf % leaf_count
            line = rows + inner // in_blocks * 16
            cur = ref[samp, inner % in_blocks, line : line + 16, :].astype(F32)
            cur_ref[place * group + leaf] = jnp.concatenate(
                [cur[:8], -cur[4:8], cur[:4]], axis=0
            ).astype(BF16)
    for leaf in range(leaf_count):
        left = jnp.concatenate(
            [cur_ref[src_ref[leaf, n] - (where - 1) * group] for n in range(near)], axis=1
        )
        copies[leaf].wait()
        out = [
            lax.dot_general(
                left,
                jnp.concatenate([near_ref[leaf, n, r] for n in range(near)], axis=1),
                NT,
                preferred_element_type=F32,
            )
            for r in range(2)
        ]
        out_ref[leaf] = out[0][:8] + out[1][8:]


def receive_kernel(near_ref, rad_ref, *rest):
    far_refs, out_ref = rest[:-1], rest[-1]
    leaf_count = out_ref.shape[0]
    far = far_refs[0][...].astype(F32)
    for ref in far_refs[1:]:
        far = far + ref[...].astype(F32)
    in_blocks = far.shape[0]
    unknowns = rad_ref.shape[4]
    depth = rad_ref.shape[1] * rad_ref.shape[2] * rad_ref.shape[3]
    for leaf in range(leaf_count):
        left = []
        for p in range(2):
            real = [far[b, leaf * 16 + p * 4 : leaf * 16 + p * 4 + 4] for b in range(in_blocks)]
            imag = [
                far[b, leaf * 16 + 8 + p * 4 : leaf * 16 + 12 + p * 4] for b in range(in_blocks)
            ]
            left += [jnp.concatenate(pair, axis=0) for pair in zip(real, imag)]
            left += [jnp.concatenate([i, -r], axis=0) for r, i in zip(real, imag)]
        wide = jnp.concatenate(left, axis=1).astype(BF16)
        right = rad_ref[leaf].reshape(depth, unknowns)
        out_ref[leaf] = near_ref[leaf] + jnp.dot(wide, right, preferred_element_type=F32)


def per_device(
    currents,
    radiation,
    near_blocks,
    near_src,
    leaf_parent,
    leaf_shift,
    shift_table,
    interp_idx,
    interp_val,
    top_src,
    top_disp,
    trans_table,
):
    n_samp = lax.axis_size("samp")
    n_box = lax.axis_size("box")
    leaf_count, comps, unknowns = currents.shape
    group = leaf_parent.shape[0]
    top_count, entries = top_src.shape
    local_blocks, _, block, _ = interp_val.shape
    in_blocks = radiation.shape[3] // block
    leaves = 3 * group
    rows = 16 * leaf_count
    extra = 16 * -(-leaf_count // in_blocks)
    tile = min(16, local_blocks)

    message = pl.pallas_call(
        functools.partial(radiate_kernel, top_count=top_count),
        out_shape=jax.ShapeDtypeStruct((in_blocks, rows + extra, block), BF16),
        in_specs=[HBM] * 4,
        out_specs=VMEM,
        scratch_shapes=[
            pltpu.SMEM(leaf_parent.shape, jnp.int32),
            pltpu.SMEM(leaf_shift.shape, jnp.int32),
            pltpu.VMEM(currents.shape, BF16),
            pltpu.VMEM(radiation.shape, BF16),
            pltpu.SemaphoreType.DMA((leaf_count + 3,)),
        ],
        compiler_params=params(),
        name="radiate",
    )(*pinned(leaf_parent, leaf_shift, currents, radiation))

    here = lax.all_gather(message, "samp", axis=0)
    last = n_samp - 1
    swap = []
    for box in range(n_box - 1):
        low, high = box * n_samp + last, (box + 1) * n_samp
        swap += [(low, high), (high, low)]
    beyond = lax.ppermute(here, ("box", "samp"), swap)
    shift_rows = shift_table.astype(F32).reshape(-1, local_blocks, block)
    trans_rows = trans_table.astype(F32).reshape(-1, local_blocks, block)
    up_shape = pltpu.VMEM((group, 2, local_blocks, 8, block), F32)
    work = 2 * group * 16 * 2 * block * local_blocks * block
    values, dense, wide_shift, wide_trans, here_up = pl.pallas_call(
        functools.partial(tables_kernel, rows=rows),
        out_shape=[
            pltpu.VMEM(interp_val.shape, BF16),
            pltpu.VMEM((local_blocks * block, in_blocks * block), BF16),
            pltpu.VMEM((shift_rows.shape[0], local_blocks, 8, block), F32),
            pltpu.VMEM((trans_rows.shape[0], local_blocks, 8, block), F32),
            up_shape,
        ],
        in_specs=[SMEM, SMEM, VMEM, HBM, VMEM, VMEM],
        out_specs=[VMEM] * 5,
        scratch_shapes=[pltpu.SemaphoreType.DMA],
        compiler_params=params(),
        cost_estimate=pl.CostEstimate(flops=work, bytes_accessed=1 << 24, transcendentals=0),
        name="tables",
    )(interp_idx, leaf_shift, here, *pinned(interp_val), shift_rows, trans_rows)
    beyond, values = lax.optimization_barrier((beyond, values))
    if n_samp == 2:
        first = beyond
        second = lax.ppermute(beyond, "samp", [(0, 1), (1, 0)])
    else:
        ends = lax.all_gather(beyond, "samp", axis=0)
        first, second = ends[0], ends[n_samp - 1]
    numbers = [pltpu.VMEM((8, block), jnp.int32), pltpu.SMEM((8, block), jnp.int32)]
    first_up = pl.pallas_call(
        functools.partial(raise_kernel, rows=rows),
        out_shape=up_shape,
        in_specs=[SMEM] + [VMEM] * 3,
        out_specs=VMEM,
        scratch_shapes=numbers + [pltpu.SemaphoreType.DMA],
        compiler_params=params(),
        cost_estimate=pl.CostEstimate(flops=work, bytes_accessed=1 << 23, transcendentals=0),
        name="raise",
    )(interp_idx, first, values, wide_shift)

    fars = pl.pallas_call(
        functools.partial(field_kernel, n_samp=n_samp, leaf_count=leaf_count, tile=tile),
        out_shape=[jax.ShapeDtypeStruct((in_blocks, rows, block), BF16)] * n_samp,
        in_specs=[SMEM] * 5 + [VMEM] * 9,
        out_specs=[VMEM] * n_samp,
        scratch_shapes=[
            pltpu.VMEM((leaves, 2, local_blocks, 8, block), F32),
            pltpu.VMEM((group, 2, local_blocks, 8, block), F32),
            pltpu.VMEM((group * 16, local_blocks * block), BF16),
            pltpu.VMEM((group * 16, in_blocks * block), F32),
            *numbers,
            pltpu.SMEM((3 * top_count,), jnp.int32),
            pltpu.SMEM((leaves,), jnp.int32),
            pltpu.SMEM((group,), jnp.int32),
            pltpu.SMEM((group, entries), jnp.int32),
            pltpu.SMEM((group, entries), jnp.int32),
            pltpu.SemaphoreType.DMA((3,)),
        ],
        compiler_params=params(),
        name="field",
    )(
        interp_idx,
        leaf_parent,
        leaf_shift,
        top_src,
        top_disp,
        here,
        first,
        second,
        first_up,
        here_up,
        values,
        dense,
        wide_shift,
        wide_trans,
    )
    received = [fars[0]] + [
        lax.ppermute(fars[d], "samp", [(i, (i + d) % n_samp) for i in range(n_samp)])
        for d in range(1, n_samp)
    ]
    near_out = pl.pallas_call(
        functools.partial(near_kernel, rows=rows, n_samp=n_samp),
        out_shape=jax.ShapeDtypeStruct((leaf_count, comps, unknowns), F32),
        in_specs=[SMEM, VMEM, VMEM, VMEM, HBM],
        out_specs=VMEM,
        scratch_shapes=[
            pltpu.VMEM((leaves, 16, block), BF16),
            pltpu.VMEM(near_blocks.shape, BF16),
            pltpu.SemaphoreType.DMA((leaf_count,)),
        ],
        compiler_params=params(),
        name="near",
    )(near_src, here, first, second, near_blocks)
    return pl.pallas_call(
        receive_kernel,
        out_shape=jax.ShapeDtypeStruct((leaf_count, comps, unknowns), F32),
        in_specs=[VMEM] * (2 + n_samp),
        out_specs=VMEM,
        compiler_params=params(),
        name="receive",
    )(near_out, radiation, *received)


def solution(mesh):
    placed = (
        P(("box", "samp"), None, None),
        P(("box", "samp"), None, None, None, None),
        P(("box", "samp"), None, None, None, None),
        P(("box", "samp"), None),
        P("box"),
        P("box"),
        P(None, None, "samp"),
        P("samp", None),
        P("samp", None, None, None),
        P("box", None),
        P("box", None),
        P(None, None, "samp"),
    )
    return jax.shard_map(
        per_device,
        mesh=mesh,
        in_specs=placed,
        out_specs=P(("box", "samp"), None, None),
        check_vma=False,
    )
```

```python
import functools

import jax
import jax.numpy as jnp
from jax import lax
from jax.experimental import pallas as pl
from jax.experimental.pallas import tpu as pltpu
from jax.sharding import PartitionSpec as P

F32 = jnp.float32
BF16 = jnp.bfloat16
HBM = pl.BlockSpec(memory_space=pltpu.HBM)
VMEM = pl.BlockSpec(memory_space=pltpu.VMEM)
SMEM = pl.BlockSpec(memory_space=pltpu.SMEM)
NT = (((1,), (1,)), ((), ()))
LIMIT = 24 * 1024 * 1024


def params():
    return pltpu.CompilerParams(vmem_limit_bytes=LIMIT)


def pinned(*arrays):
    return [pltpu.with_memory_space_constraint(array, pltpu.HBM) for array in arrays]


def radiate_kernel(
    parent_hbm, shift_hbm, cur_hbm, rad_hbm, msg_ref, parent_ref, shift_ref, cur_ref, rad_ref, sem, *, top_count
):
    leaf_count, in_blocks = cur_ref.shape[0], msg_ref.shape[0]
    block = msg_ref.shape[2]
    half = cur_ref.shape[1] // 2
    group = parent_ref.shape[0]
    firsts = [
        pltpu.make_async_copy(src, dst, sem.at[leaf_count + n])
        for n, (src, dst) in enumerate(
            ((parent_hbm, parent_ref), (shift_hbm, shift_ref), (cur_hbm, cur_ref))
        )
    ]
    for copy in firsts:
        copy.start()
    copies = [
        pltpu.make_async_copy(rad_hbm.at[leaf], rad_ref.at[leaf], sem.at[leaf])
        for leaf in range(leaf_count)
    ]
    for copy in copies:
        copy.start()
    base = leaf_count * 4 * half
    lane = lax.broadcasted_iota(jnp.int32, (8, block), 1)
    line = lax.broadcasted_iota(jnp.int32, (8, block), 0)
    meta = jnp.zeros((8, block), jnp.int32)
    for copy in firsts:
        copy.wait()
    for member in range(group):
        pair = jnp.where(
            line == 0, lax.rem(parent_ref[member], top_count), shift_ref[member]
        )
        meta = jnp.where(lane == member, pair, meta)
    meta = meta.astype(F32)
    zero = jnp.zeros((half, cur_ref.shape[2]), F32)
    left = []
    for leaf in range(leaf_count):
        cur = cur_ref[leaf].astype(F32)
        real, imag = cur[:half], cur[half:]
        pieces = [
            jnp.concatenate(rows, axis=0).astype(BF16)
            for rows in (
                (real, zero, imag, zero),
                (-imag, zero, real, zero),
                (zero, real, zero, imag),
                (zero, -imag, zero, real),
            )
        ]
        left.append(jnp.concatenate(pieces, axis=1))
        row = base + leaf // in_blocks * 4 * half
        msg_ref[leaf % in_blocks, row : row + 4 * half, :] = jnp.concatenate(
            [cur, meta], axis=0
        ).astype(BF16)
    for leaf in range(leaf_count):
        copies[leaf].wait()
        right = jnp.concatenate(
            [rad_ref[leaf, p, r] for p in range(2) for r in range(2)], axis=1
        )
        out = lax.dot_general(left[leaf], right, NT, preferred_element_type=F32).astype(BF16)
        for b in range(in_blocks):
            msg_ref[b, leaf * 4 * half : (leaf + 1) * 4 * half, :] = out[
                :, b * block : (b + 1) * block
            ]


def lift_groups(refs, dense_ref, out_ref, rows):
    left = jnp.concatenate(
        [
            jnp.concatenate([ref[samp, c, :rows, :] for c in range(ref.shape[1])], axis=1)
            for ref in refs
            for samp in range(ref.shape[0])
        ],
        axis=0,
    )
    samples = dense_ref.shape[0]
    width = min(1024, samples)
    for start in range(0, samples, width):
        out_ref[:, start : start + width] = lax.dot_general(
            left, dense_ref[start : start + width, :], NT, preferred_element_type=F32
        )


def spread_rows(src_ref, out_ref):
    count, local_blocks, block = src_ref.shape

    def one(index, carry):
        for b in range(local_blocks):
            out_ref[index, b] = jnp.broadcast_to(src_ref[index, b : b + 1, :], (8, block))
        return carry

    lax.fori_loop(0, count, one, 0)


def tables_kernel(
    idx_ref, val_hbm, shift_ref, trans_ref, dense_ref, wide_shift_ref, wide_trans_ref, val_ref, sem
):
    load = pltpu.make_async_copy(val_hbm, val_ref, sem)
    load.start()
    spread_rows(shift_ref, wide_shift_ref)
    load.wait()
    local_blocks, _, block, _ = val_ref.shape

    def one(b, carry):
        first, second = idx_ref[b, 0], idx_ref[b, 1]
        zero = jnp.zeros((block, block), BF16)
        for c in range(dense_ref.shape[1] // block):
            dense_ref[pl.ds(pl.multiple_of(b * block, block), block), c * block : (c + 1) * block] = (
                jnp.where(first == c, val_ref[b, 0], jnp.where(second == c, val_ref[b, 1], zero))
            )
        return carry

    lax.fori_loop(0, local_blocks, one, 0)
    spread_rows(trans_ref, wide_trans_ref)


def lift_kernel(here_ref, near_ref, dense_ref, out_ref, *, rows):
    lift_groups((here_ref, near_ref), dense_ref, out_ref, rows)


def meta_of(msg_ref, rows):
    return msg_ref[0, 0, rows : rows + 16, :].astype(F32)[8:10]


def field_kernel(
    parent_ref,
    sid_ref,
    src_ref,
    disp_ref,
    here_ref,
    near_ref,
    far_ref,
    lifted_ref,
    dense_ref,
    shift_ref,
    trans_ref,
    *rest,
    n_samp,
    leaf_count,
    tile,
):
    outs = rest[:n_samp]
    (
        top_ref,
        last_ref,
        inc_ref,
        down_ref,
        acc_ref,
        meta_ref,
        num_ref,
        box_ref,
        rep_ref,
        count_ref,
        slot_ref,
        coef_ref,
        sem,
    ) = rest[n_samp:]
    block = here_ref.shape[3]
    local_blocks = top_ref.shape[2]
    leaves = top_ref.shape[0]
    group = leaves // 3
    rows = 16 * leaf_count
    top_count, entries = src_ref.shape
    where = lax.axis_index("box")
    me = lax.axis_index("samp")
    turned = jnp.where(me == 1, 1, 0) if n_samp == 2 else jnp.int32(0)
    bases = (1, 2 * turned, 2 - 2 * turned)

    lines = [meta_of(ref, rows) for ref in (here_ref, near_ref, far_ref)]
    meta_ref[...] = jnp.concatenate(lines + lines[:1], axis=0).astype(jnp.int32)
    fetch = pltpu.make_async_copy(meta_ref, num_ref, sem)
    fetch.start()
    for box in range(3 * top_count):
        box_ref[box] = -1
    lift_groups((far_ref,), dense_ref, last_ref, rows)
    fetch.wait()
    boxes = [
        num_ref[2 * (s // group), s % group] + bases[s // group] * top_count for s in range(leaves)
    ]
    for s in reversed(range(leaves)):
        box_ref[boxes[s]] = s
    for s in range(leaves):
        rep_ref[s] = box_ref[boxes[s]]

    def listing(leaf, carry):
        parent = parent_ref[leaf] - where * top_count
        count = jnp.int32(0)
        slots = [box_ref[src_ref[parent, j] - (where - 1) * top_count] for j in range(entries)]
        coefs = [2 * disp_ref[parent, j] for j in range(entries)]
        for slot, coef in zip(slots, coefs):
            slot_ref[leaf, count] = slot
            coef_ref[leaf, count] = coef
            count += (slot >= 0).astype(jnp.int32)
        count_ref[leaf] = count
        return carry

    lax.fori_loop(0, group, listing, 0)

    def shifted(b, carry):
        start = pl.multiple_of(b * block, block)
        for s in range(leaves):
            ref, line = (lifted_ref, s * 16) if s < 2 * group else (last_ref, (s - 2 * group) * 16)
            real = ref[line : line + 8, pl.ds(start, block)]
            imag = ref[line + 8 : line + 16, pl.ds(start, block)]
            sid = 2 * num_ref[2 * (s // group) + 1, s % group]
            shift_real, shift_imag = shift_ref[sid, b], shift_ref[sid + 1, b]
            top_ref[s, 0, b] = real * shift_real - imag * shift_imag
            top_ref[s, 1, b] = real * shift_imag + imag * shift_real
        return carry

    lax.fori_loop(0, local_blocks, shifted, 0)

    def merge(s, carry):
        rep = rep_ref[s]

        @pl.when(rep != s)
        def _():
            top_ref[rep] = top_ref[rep] + top_ref[s]

        return carry

    lax.fori_loop(0, leaves, merge, 0)

    def target(leaf, carry):
        @pl.when(rep_ref[leaf] == leaf)
        def _():
            for t in range(local_blocks // tile):

                def entry(n, total):
                    slot, coef = slot_ref[leaf, n], coef_ref[leaf, n]
                    real, imag = list(total[:tile]), list(total[tile:])
                    for b in range(tile):
                        place = t * tile + b
                        coef_real, coef_imag = trans_ref[coef, place], trans_ref[coef + 1, place]
                        src_real, src_imag = top_ref[slot, 0, place], top_ref[slot, 1, place]
                        real[b] += coef_real * src_real - coef_imag * src_imag
                        imag[b] += coef_real * src_imag + coef_imag * src_real
                    return tuple(real + imag)

                zero = jnp.zeros((8, block), F32)
                total = lax.fori_loop(0, count_ref[leaf], entry, (zero,) * (2 * tile))
                for b in range(tile):
                    inc_ref[leaf, 0, t * tile + b] = total[b]
                    inc_ref[leaf, 1, t * tile + b] = total[tile + b]

        return carry

    lax.fori_loop(0, group, target, 0)

    def lower(leaf, carry):
        sid = 2 * sid_ref[leaf]
        rep = rep_ref[leaf]
        start = pl.multiple_of(leaf * 16, 16)
        for b in range(local_blocks):
            shift_real, shift_imag = shift_ref[sid, b], shift_ref[sid + 1, b]
            real, imag = inc_ref[rep, 0, b], inc_ref[rep, 1, b]
            down = jnp.concatenate(
                [
                    shift_real * real + shift_imag * imag,
                    shift_real * imag - shift_imag * real,
                ],
                axis=0,
            )
            down_ref[pl.ds(start, 16), b * block : (b + 1) * block] = down.astype(BF16)
        return carry

    lax.fori_loop(0, group, lower, 0)
    acc_ref[...] = jnp.dot(down_ref[...], dense_ref[...], preferred_element_type=F32)
    for d, out in enumerate(outs):
        owner = lax.rem(me + d, n_samp)
        start = pl.multiple_of(owner * rows, rows)
        for c in range(out.shape[0]):
            out[c] = acc_ref[pl.ds(start, rows), c * block : (c + 1) * block].astype(BF16)


def near_kernel(src_ref, here_ref, first_ref, second_ref, near_hbm, out_ref, cur_ref, near_ref, sem, *, rows, n_samp):
    leaf_count, near = near_ref.shape[:2]
    in_blocks = here_ref.shape[1]
    group = n_samp * leaf_count
    copies = [
        pltpu.make_async_copy(near_hbm.at[leaf], near_ref.at[leaf], sem.at[leaf])
        for leaf in range(leaf_count)
    ]
    for copy in copies:
        copy.start()
    where = lax.axis_index("box")
    turned = jnp.where(lax.axis_index("samp") == 1, 1, 0) if n_samp == 2 else jnp.int32(0)
    for place, ref in ((1, here_ref), (2 * turned, first_ref), (2 - 2 * turned, second_ref)):
        for leaf in range(group):
            samp, inner = leaf // leaf_count, leaf % leaf_count
            line = rows + inner // in_blocks * 16
            cur = ref[samp, inner % in_blocks, line : line + 16, :].astype(F32)
            cur_ref[place * group + leaf] = jnp.concatenate(
                [cur[:8], -cur[4:8], cur[:4]], axis=0
            ).astype(BF16)
    for leaf in range(leaf_count):
        left = jnp.concatenate(
            [cur_ref[src_ref[leaf, n] - (where - 1) * group] for n in range(near)], axis=1
        )
        copies[leaf].wait()
        out = [
            lax.dot_general(
                left,
                jnp.concatenate([near_ref[leaf, n, r] for n in range(near)], axis=1),
                NT,
                preferred_element_type=F32,
            )
            for r in range(2)
        ]
        out_ref[leaf] = out[0][:8] + out[1][8:]


def receive_kernel(near_ref, rad_ref, *rest):
    far_refs, out_ref = rest[:-1], rest[-1]
    leaf_count = out_ref.shape[0]
    far = far_refs[0][...].astype(F32)
    for ref in far_refs[1:]:
        far = far + ref[...].astype(F32)
    in_blocks = far.shape[0]
    unknowns = rad_ref.shape[4]
    depth = rad_ref.shape[1] * rad_ref.shape[2] * rad_ref.shape[3]
    for leaf in range(leaf_count):
        left = []
        for p in range(2):
            real = [far[b, leaf * 16 + p * 4 : leaf * 16 + p * 4 + 4] for b in range(in_blocks)]
            imag = [
                far[b, leaf * 16 + 8 + p * 4 : leaf * 16 + 12 + p * 4] for b in range(in_blocks)
            ]
            left += [jnp.concatenate(pair, axis=0) for pair in zip(real, imag)]
            left += [jnp.concatenate([i, -r], axis=0) for r, i in zip(real, imag)]
        wide = jnp.concatenate(left, axis=1).astype(BF16)
        right = rad_ref[leaf].reshape(depth, unknowns)
        out_ref[leaf] = near_ref[leaf] + jnp.dot(wide, right, preferred_element_type=F32)


def per_device(
    currents,
    radiation,
    near_blocks,
    near_src,
    leaf_parent,
    leaf_shift,
    shift_table,
    interp_idx,
    interp_val,
    top_src,
    top_disp,
    trans_table,
):
    n_samp = lax.axis_size("samp")
    n_box = lax.axis_size("box")
    leaf_count, comps, unknowns = currents.shape
    group = leaf_parent.shape[0]
    top_count, entries = top_src.shape
    local_blocks, _, block, _ = interp_val.shape
    in_blocks = radiation.shape[3] // block
    leaves = 3 * group
    rows = 16 * leaf_count
    extra = 16 * -(-leaf_count // in_blocks)
    tile = min(16, local_blocks)

    message = pl.pallas_call(
        functools.partial(radiate_kernel, top_count=top_count),
        out_shape=jax.ShapeDtypeStruct((in_blocks, rows + extra, block), BF16),
        in_specs=[HBM] * 4,
        out_specs=VMEM,
        scratch_shapes=[
            pltpu.SMEM(leaf_parent.shape, jnp.int32),
            pltpu.SMEM(leaf_shift.shape, jnp.int32),
            pltpu.VMEM(currents.shape, BF16),
            pltpu.VMEM(radiation.shape, BF16),
            pltpu.SemaphoreType.DMA((leaf_count + 3,)),
        ],
        compiler_params=params(),
        name="radiate",
    )(*pinned(leaf_parent, leaf_shift, currents, radiation))

    here = lax.all_gather(message, "samp", axis=0)
    last = n_samp - 1
    swap = []
    for box in range(n_box - 1):
        low, high = box * n_samp + last, (box + 1) * n_samp
        swap += [(low, high), (high, low)]
    beyond = lax.ppermute(here, ("box", "samp"), swap)
    shift_rows = shift_table.astype(F32).reshape(-1, local_blocks, block)
    trans_rows = trans_table.astype(F32).reshape(-1, local_blocks, block)
    work = 2 * leaves * 16 * in_blocks * block * local_blocks * block
    dense, wide_shift, wide_trans = pl.pallas_call(
        tables_kernel,
        out_shape=[
            pltpu.VMEM((local_blocks * block, in_blocks * block), BF16),
            pltpu.VMEM((shift_rows.shape[0], local_blocks, 8, block), F32),
            pltpu.VMEM((trans_rows.shape[0], local_blocks, 8, block), F32),
        ],
        in_specs=[SMEM, HBM, VMEM, VMEM],
        out_specs=[VMEM] * 3,
        scratch_shapes=[pltpu.VMEM(interp_val.shape, BF16), pltpu.SemaphoreType.DMA],
        compiler_params=params(),
        cost_estimate=pl.CostEstimate(flops=work, bytes_accessed=1 << 24, transcendentals=0),
        name="tables",
    )(interp_idx, *pinned(interp_val), shift_rows, trans_rows)
    beyond, dense = lax.optimization_barrier((beyond, dense))
    if n_samp == 2:
        first = beyond
        second = lax.ppermute(beyond, "samp", [(0, 1), (1, 0)])
    else:
        ends = lax.all_gather(beyond, "samp", axis=0)
        first, second = ends[0], ends[n_samp - 1]
    numbers = [pltpu.VMEM((8, block), jnp.int32), pltpu.SMEM((8, block), jnp.int32)]
    lifted = pl.pallas_call(
        functools.partial(lift_kernel, rows=rows),
        out_shape=pltpu.VMEM((2 * group * 16, local_blocks * block), F32),
        in_specs=[VMEM] * 3,
        out_specs=VMEM,
        compiler_params=params(),
        cost_estimate=pl.CostEstimate(flops=work, bytes_accessed=1 << 23, transcendentals=0),
        name="lift",
    )(here, first, dense)

    fars = pl.pallas_call(
        functools.partial(field_kernel, n_samp=n_samp, leaf_count=leaf_count, tile=tile),
        out_shape=[jax.ShapeDtypeStruct((in_blocks, rows, block), BF16)] * n_samp,
        in_specs=[SMEM] * 4 + [VMEM] * 7,
        out_specs=[VMEM] * n_samp,
        scratch_shapes=[
            pltpu.VMEM((leaves, 2, local_blocks, 8, block), F32),
            pltpu.VMEM((group * 16, local_blocks * block), F32),
            pltpu.VMEM((group, 2, local_blocks, 8, block), F32),
            pltpu.VMEM((group * 16, local_blocks * block), BF16),
            pltpu.VMEM((group * 16, in_blocks * block), F32),
            *numbers,
            pltpu.SMEM((3 * top_count,), jnp.int32),
            pltpu.SMEM((leaves,), jnp.int32),
            pltpu.SMEM((group,), jnp.int32),
            pltpu.SMEM((group, entries), jnp.int32),
            pltpu.SMEM((group, entries), jnp.int32),
            pltpu.SemaphoreType.DMA,
        ],
        compiler_params=params(),
        name="field",
    )(
        leaf_parent,
        leaf_shift,
        top_src,
        top_disp,
        here,
        first,
        second,
        lifted,
        dense,
        wide_shift,
        wide_trans,
    )
    received = [fars[0]] + [
        lax.ppermute(fars[d], "samp", [(i, (i + d) % n_samp) for i in range(n_samp)])
        for d in range(1, n_samp)
    ]
    near_out = pl.pallas_call(
        functools.partial(near_kernel, rows=rows, n_samp=n_samp),
        out_shape=jax.ShapeDtypeStruct((leaf_count, comps, unknowns), F32),
        in_specs=[SMEM, VMEM, VMEM, VMEM, HBM],
        out_specs=VMEM,
        scratch_shapes=[
            pltpu.VMEM((leaves, 16, block), BF16),
            pltpu.VMEM(near_blocks.shape, BF16),
            pltpu.SemaphoreType.DMA((leaf_count,)),
        ],
        compiler_params=params(),
        name="near",
    )(near_src, here, first, second, near_blocks)
    return pl.pallas_call(
        receive_kernel,
        out_shape=jax.ShapeDtypeStruct((leaf_count, comps, unknowns), F32),
        in_specs=[VMEM] * (2 + n_samp),
        out_specs=VMEM,
        compiler_params=params(),
        name="receive",
    )(near_out, radiation, *received)


def solution(mesh):
    placed = (
        P(("box", "samp"), None, None),
        P(("box", "samp"), None, None, None, None),
        P(("box", "samp"), None, None, None, None),
        P(("box", "samp"), None),
        P("box"),
        P("box"),
        P(None, None, "samp"),
        P("samp", None),
        P("samp", None, None, None),
        P("box", None),
        P("box", None),
        P(None, None, "samp"),
    )
    return jax.shard_map(
        per_device,
        mesh=mesh,
        in_specs=placed,
        out_specs=P(("box", "samp"), None, None),
        check_vma=False,
    )
```

```python
import functools

import jax
import jax.numpy as jnp
from jax import lax
from jax.experimental import pallas as pl
from jax.experimental.pallas import tpu as pltpu
from jax.sharding import PartitionSpec as P

F32 = jnp.float32
BF16 = jnp.bfloat16
HBM = pl.BlockSpec(memory_space=pltpu.HBM)
VMEM = pl.BlockSpec(memory_space=pltpu.VMEM)
SMEM = pl.BlockSpec(memory_space=pltpu.SMEM)
NT = (((1,), (1,)), ((), ()))
LIMIT = 24 * 1024 * 1024


def params():
    return pltpu.CompilerParams(vmem_limit_bytes=LIMIT)


def pinned(*arrays):
    return [pltpu.with_memory_space_constraint(array, pltpu.HBM) for array in arrays]


def radiate_kernel(
    parent_hbm, shift_hbm, cur_hbm, rad_hbm, msg_ref, parent_ref, shift_ref, cur_ref, rad_ref, sem, *, top_count
):
    leaf_count, in_blocks = cur_ref.shape[0], msg_ref.shape[0]
    block = msg_ref.shape[2]
    half = cur_ref.shape[1] // 2
    group = parent_ref.shape[0]
    firsts = [
        pltpu.make_async_copy(src, dst, sem.at[leaf_count + n])
        for n, (src, dst) in enumerate(
            ((parent_hbm, parent_ref), (shift_hbm, shift_ref), (cur_hbm, cur_ref))
        )
    ]
    for copy in firsts:
        copy.start()
    copies = [
        pltpu.make_async_copy(rad_hbm.at[leaf], rad_ref.at[leaf], sem.at[leaf])
        for leaf in range(leaf_count)
    ]
    for copy in copies:
        copy.start()
    base = leaf_count * 4 * half
    lane = lax.broadcasted_iota(jnp.int32, (8, block), 1)
    line = lax.broadcasted_iota(jnp.int32, (8, block), 0)
    meta = jnp.zeros((8, block), jnp.int32)
    for copy in firsts:
        copy.wait()
    for member in range(group):
        pair = jnp.where(
            line == 0, lax.rem(parent_ref[member], top_count), shift_ref[member]
        )
        meta = jnp.where(lane == member, pair, meta)
    meta = meta.astype(F32)
    zero = jnp.zeros((half, cur_ref.shape[2]), F32)
    left = []
    for leaf in range(leaf_count):
        cur = cur_ref[leaf].astype(F32)
        real, imag = cur[:half], cur[half:]
        pieces = [
            jnp.concatenate(rows, axis=0).astype(BF16)
            for rows in (
                (real, zero, imag, zero),
                (-imag, zero, real, zero),
                (zero, real, zero, imag),
                (zero, -imag, zero, real),
            )
        ]
        left.append(jnp.concatenate(pieces, axis=1))
        row = base + leaf // in_blocks * 4 * half
        msg_ref[leaf % in_blocks, row : row + 4 * half, :] = jnp.concatenate(
            [cur, meta], axis=0
        ).astype(BF16)
    for leaf in range(leaf_count):
        copies[leaf].wait()
        right = jnp.concatenate(
            [rad_ref[leaf, p, r] for p in range(2) for r in range(2)], axis=1
        )
        out = lax.dot_general(left[leaf], right, NT, preferred_element_type=F32).astype(BF16)
        for b in range(in_blocks):
            msg_ref[b, leaf * 4 * half : (leaf + 1) * 4 * half, :] = out[
                :, b * block : (b + 1) * block
            ]


def lift_groups(refs, dense_ref, out_ref, rows, base, low, high):
    left = jnp.concatenate(
        [
            jnp.concatenate([ref[samp, c, :rows, :] for c in range(ref.shape[1])], axis=1)
            for ref in refs
            for samp in range(ref.shape[0])
        ],
        axis=0,
    )
    width = min(1024, high - low)
    for start in range(low, high, width):
        out_ref[base : base + left.shape[0], start : start + width] = lax.dot_general(
            left, dense_ref[start : start + width, :], NT, preferred_element_type=F32
        )


def tables_kernel(
    idx_ref, val_hbm, dense_ref, val_ref, sem
):
    load = pltpu.make_async_copy(val_hbm, val_ref, sem)
    load.start()
    load.wait()
    local_blocks, _, block, _ = val_ref.shape

    def one(b, carry):
        first, second = idx_ref[b, 0], idx_ref[b, 1]
        zero = jnp.zeros((block, block), BF16)
        for c in range(dense_ref.shape[1] // block):
            dense_ref[pl.ds(pl.multiple_of(b * block, block), block), c * block : (c + 1) * block] = (
                jnp.where(first == c, val_ref[b, 0], jnp.where(second == c, val_ref[b, 1], zero))
            )
        return carry

    lax.fori_loop(0, local_blocks, one, 0)


def lift_kernel(here_ref, near_ref, dense_ref, out_ref, *, rows):
    lift_groups((here_ref, near_ref), dense_ref, out_ref, rows, 0, 0, dense_ref.shape[0])


def meta_of(msg_ref, rows):
    return msg_ref[0, 0, rows : rows + 16, :].astype(F32)[8:10]


def field_kernel(
    parent_ref,
    sid_ref,
    src_ref,
    disp_ref,
    here_ref,
    near_ref,
    far_ref,
    dense_ref,
    shift_ref,
    trans_ref,
    _,
    *rest,
    n_samp,
    leaf_count,
    tile,
):
    outs = rest[:n_samp]
    (
        lifted_ref,
        inc_ref,
        down_ref,
        acc_ref,
        meta_ref,
        num_ref,
        head_ref,
        next_ref,
        turn_ref,
        count_ref,
        slot_ref,
        coef_ref,
        sem,
    ) = rest[n_samp:]
    block = here_ref.shape[3]
    samples = lifted_ref.shape[1]
    local_blocks = samples // block
    leaves = lifted_ref.shape[0] // 16
    group = leaves // 3
    rows = 16 * leaf_count
    top_count, entries = src_ref.shape
    where = lax.axis_index("box")
    me = lax.axis_index("samp")
    turned = jnp.where(me == 1, 1, 0) if n_samp == 2 else jnp.int32(0)
    bases = (1, 2 * turned, 2 - 2 * turned)

    lines = [meta_of(ref, rows) for ref in (here_ref, near_ref, far_ref)]
    meta_ref[...] = jnp.concatenate(lines + lines[:1], axis=0).astype(jnp.int32)
    fetch = pltpu.make_async_copy(meta_ref, num_ref, sem)
    fetch.start()
    for box in range(3 * top_count):
        head_ref[box] = -1
    base = 2 * group * 16
    lift_groups((far_ref,), dense_ref, lifted_ref, rows, base, 0, samples // 2)
    fetch.wait()
    lift_groups((far_ref,), dense_ref, lifted_ref, rows, base, samples // 2, samples)
    boxes = [
        num_ref[2 * (s // group), s % group] + bases[s // group] * top_count for s in range(leaves)
    ]
    for s in reversed(range(leaves)):
        turn_ref[s] = 2 * num_ref[2 * (s // group) + 1, s % group]
        next_ref[s] = head_ref[boxes[s]]
        head_ref[boxes[s]] = s
    for leaf in range(group):
        parent = parent_ref[leaf] - where * top_count
        count = jnp.int32(0)
        slots = [head_ref[src_ref[parent, j] - (where - 1) * top_count] for j in range(entries)]
        coefs = [2 * disp_ref[parent, j] for j in range(entries)]
        for slot, coef in zip(slots, coefs):
            slot_ref[leaf, count] = slot
            coef_ref[leaf, count] = coef
            count += (slot >= 0).astype(jnp.int32)
        count_ref[leaf] = count

    span = min(8, tile)

    def spread(line, b):
        return jnp.broadcast_to(line[b : b + 1, :], (8, block))

    def target(leaf, carry):
        @pl.when(head_ref[parent_ref[leaf] - (where - 1) * top_count] == leaf)
        def _():
            for t in range(0, local_blocks, tile):

                def member(state):
                    s = state[0]
                    coef = state[1]
                    real, imag = list(state[2 : 2 + tile]), list(state[2 + tile :])
                    sid = turn_ref[s]
                    line = pl.multiple_of(s * 16, 16)
                    for low in range(0, tile, span):
                        part = pl.ds(t + low, span)
                        shift_real, shift_imag = shift_ref[sid, part, :], shift_ref[sid + 1, part, :]
                        move_real, move_imag = trans_ref[coef, part, :], trans_ref[coef + 1, part, :]
                        both_real = move_real * shift_real - move_imag * shift_imag
                        both_imag = move_real * shift_imag + move_imag * shift_real
                        for b in range(span):
                            column = (t + low + b) * block
                            src_real = lifted_ref[pl.ds(line, 8), column : column + block]
                            src_imag = lifted_ref[pl.ds(line + 8, 8), column : column + block]
                            use_real, use_imag = spread(both_real, b), spread(both_imag, b)
                            real[low + b] += use_real * src_real - use_imag * src_imag
                            imag[low + b] += use_real * src_imag + use_imag * src_real
                    return (next_ref[s], coef, *real, *imag)

                def entry(n, total):
                    state = (slot_ref[leaf, n], coef_ref[leaf, n], *total)
                    return lax.while_loop(lambda state: state[0] >= 0, member, state)[2:]

                zero = jnp.zeros((8, block), F32)
                total = lax.fori_loop(0, count_ref[leaf], entry, (zero,) * (2 * tile))
                for b in range(tile):
                    inc_ref[leaf, 0, t + b] = total[b]
                    inc_ref[leaf, 1, t + b] = total[tile + b]

        return carry

    lax.fori_loop(0, group, target, 0)

    def lower(leaf, carry):
        sid = 2 * sid_ref[leaf]
        rep = head_ref[parent_ref[leaf] - (where - 1) * top_count]
        start = pl.multiple_of(leaf * 16, 16)
        for low in range(0, local_blocks, span):
            wide_real = shift_ref[sid, low : low + span, :]
            wide_imag = shift_ref[sid + 1, low : low + span, :]
            for inner in range(span):
                b = low + inner
                shift_real, shift_imag = spread(wide_real, inner), spread(wide_imag, inner)
                real, imag = inc_ref[rep, 0, b], inc_ref[rep, 1, b]
                down = jnp.concatenate(
                    [
                        shift_real * real + shift_imag * imag,
                        shift_real * imag - shift_imag * real,
                    ],
                    axis=0,
                )
                down_ref[pl.ds(start, 16), b * block : (b + 1) * block] = down.astype(BF16)
        return carry

    lax.fori_loop(0, group, lower, 0)
    acc_ref[...] = jnp.dot(down_ref[...], dense_ref[...], preferred_element_type=F32)
    for d, out in enumerate(outs):
        owner = lax.rem(me + d, n_samp)
        start = pl.multiple_of(owner * rows, rows)
        for c in range(out.shape[0]):
            out[c] = acc_ref[pl.ds(start, rows), c * block : (c + 1) * block].astype(BF16)


def near_kernel(src_ref, here_ref, first_ref, second_ref, near_hbm, out_ref, cur_ref, near_ref, sem, *, rows, n_samp):
    leaf_count, near = near_ref.shape[:2]
    in_blocks = here_ref.shape[1]
    group = n_samp * leaf_count
    copies = [
        pltpu.make_async_copy(near_hbm.at[leaf], near_ref.at[leaf], sem.at[leaf])
        for leaf in range(leaf_count)
    ]
    for copy in copies:
        copy.start()
    where = lax.axis_index("box")
    turned = jnp.where(lax.axis_index("samp") == 1, 1, 0) if n_samp == 2 else jnp.int32(0)
    for place, ref in ((1, here_ref), (2 * turned, first_ref), (2 - 2 * turned, second_ref)):
        for leaf in range(group):
            samp, inner = leaf // leaf_count, leaf % leaf_count
            line = rows + inner // in_blocks * 16
            cur = ref[samp, inner % in_blocks, line : line + 16, :].astype(F32)
            cur_ref[place * group + leaf] = jnp.concatenate(
                [cur[:8], -cur[4:8], cur[:4]], axis=0
            ).astype(BF16)
    for leaf in range(leaf_count):
        left = jnp.concatenate(
            [cur_ref[src_ref[leaf, n] - (where - 1) * group] for n in range(near)], axis=1
        )
        copies[leaf].wait()
        out = [
            lax.dot_general(
                left,
                jnp.concatenate([near_ref[leaf, n, r] for n in range(near)], axis=1),
                NT,
                preferred_element_type=F32,
            )
            for r in range(2)
        ]
        out_ref[leaf] = out[0][:8] + out[1][8:]


def receive_kernel(near_ref, rad_ref, *rest):
    far_refs, out_ref = rest[:-1], rest[-1]
    leaf_count = out_ref.shape[0]
    far = far_refs[0][...].astype(F32)
    for ref in far_refs[1:]:
        far = far + ref[...].astype(F32)
    in_blocks = far.shape[0]
    unknowns = rad_ref.shape[4]
    depth = rad_ref.shape[1] * rad_ref.shape[2] * rad_ref.shape[3]
    for leaf in range(leaf_count):
        left = []
        for p in range(2):
            real = [far[b, leaf * 16 + p * 4 : leaf * 16 + p * 4 + 4] for b in range(in_blocks)]
            imag = [
                far[b, leaf * 16 + 8 + p * 4 : leaf * 16 + 12 + p * 4] for b in range(in_blocks)
            ]
            left += [jnp.concatenate(pair, axis=0) for pair in zip(real, imag)]
            left += [jnp.concatenate([i, -r], axis=0) for r, i in zip(real, imag)]
        wide = jnp.concatenate(left, axis=1).astype(BF16)
        right = rad_ref[leaf].reshape(depth, unknowns)
        out_ref[leaf] = near_ref[leaf] + jnp.dot(wide, right, preferred_element_type=F32)


def per_device(
    currents,
    radiation,
    near_blocks,
    near_src,
    leaf_parent,
    leaf_shift,
    shift_table,
    interp_idx,
    interp_val,
    top_src,
    top_disp,
    trans_table,
):
    n_samp = lax.axis_size("samp")
    n_box = lax.axis_size("box")
    leaf_count, comps, unknowns = currents.shape
    group = leaf_parent.shape[0]
    top_count, entries = top_src.shape
    local_blocks, _, block, _ = interp_val.shape
    in_blocks = radiation.shape[3] // block
    leaves = 3 * group
    rows = 16 * leaf_count
    extra = 16 * -(-leaf_count // in_blocks)
    tile = min(16, local_blocks)

    message = pl.pallas_call(
        functools.partial(radiate_kernel, top_count=top_count),
        out_shape=jax.ShapeDtypeStruct((in_blocks, rows + extra, block), BF16),
        in_specs=[HBM] * 4,
        out_specs=VMEM,
        scratch_shapes=[
            pltpu.SMEM(leaf_parent.shape, jnp.int32),
            pltpu.SMEM(leaf_shift.shape, jnp.int32),
            pltpu.VMEM(currents.shape, BF16),
            pltpu.VMEM(radiation.shape, BF16),
            pltpu.SemaphoreType.DMA((leaf_count + 3,)),
        ],
        compiler_params=params(),
        name="radiate",
    )(*pinned(leaf_parent, leaf_shift, currents, radiation))

    here = lax.all_gather(message, "samp", axis=0)
    last = n_samp - 1
    swap = []
    for box in range(n_box - 1):
        low, high = box * n_samp + last, (box + 1) * n_samp
        swap += [(low, high), (high, low)]
    beyond = lax.ppermute(here, ("box", "samp"), swap)
    shift_rows = shift_table.astype(F32).reshape(-1, local_blocks, block)
    trans_rows = trans_table.astype(F32).reshape(-1, local_blocks, block)
    work = 2 * leaves * 16 * in_blocks * block * local_blocks * block
    dense = pl.pallas_call(
        tables_kernel,
        out_shape=pltpu.VMEM((local_blocks * block, in_blocks * block), BF16),
        in_specs=[SMEM, HBM],
        out_specs=VMEM,
        scratch_shapes=[pltpu.VMEM(interp_val.shape, BF16), pltpu.SemaphoreType.DMA],
        compiler_params=params(),
        cost_estimate=pl.CostEstimate(flops=work, bytes_accessed=1 << 24, transcendentals=0),
        name="tables",
    )(interp_idx, *pinned(interp_val))
    beyond, dense, shift_rows, trans_rows = lax.optimization_barrier(
        (beyond, dense, shift_rows, trans_rows)
    )
    if n_samp == 2:
        first = beyond
        second = lax.ppermute(beyond, "samp", [(0, 1), (1, 0)])
    else:
        ends = lax.all_gather(beyond, "samp", axis=0)
        first, second = ends[0], ends[n_samp - 1]
    lifted = pl.pallas_call(
        functools.partial(lift_kernel, rows=rows),
        out_shape=pltpu.VMEM((leaves * 16, local_blocks * block), F32),
        in_specs=[VMEM] * 3,
        out_specs=VMEM,
        compiler_params=params(),
        cost_estimate=pl.CostEstimate(flops=work, bytes_accessed=1 << 23, transcendentals=0),
        name="lift",
    )(here, first, dense)

    *fars, _ = pl.pallas_call(
        functools.partial(field_kernel, n_samp=n_samp, leaf_count=leaf_count, tile=tile),
        out_shape=[jax.ShapeDtypeStruct((in_blocks, rows, block), BF16)] * n_samp
        + [pltpu.VMEM((leaves * 16, local_blocks * block), F32)],
        in_specs=[SMEM] * 4 + [VMEM] * 7,
        out_specs=[VMEM] * (n_samp + 1),
        scratch_shapes=[
            pltpu.VMEM((group, 2, local_blocks, 8, block), F32),
            pltpu.VMEM((group * 16, local_blocks * block), BF16),
            pltpu.VMEM((group * 16, in_blocks * block), F32),
            pltpu.VMEM((8, block), jnp.int32),
            pltpu.SMEM((8, block), jnp.int32),
            pltpu.SMEM((3 * top_count,), jnp.int32),
            pltpu.SMEM((leaves,), jnp.int32),
            pltpu.SMEM((leaves,), jnp.int32),
            pltpu.SMEM((group,), jnp.int32),
            pltpu.SMEM((group, entries), jnp.int32),
            pltpu.SMEM((group, entries), jnp.int32),
            pltpu.SemaphoreType.DMA,
        ],
        input_output_aliases={10: n_samp},
        compiler_params=params(),
        name="field",
    )(
        leaf_parent,
        leaf_shift,
        top_src,
        top_disp,
        here,
        first,
        second,
        dense,
        shift_rows,
        trans_rows,
        lifted,
    )
    received = [fars[0]] + [
        lax.ppermute(fars[d], "samp", [(i, (i + d) % n_samp) for i in range(n_samp)])
        for d in range(1, n_samp)
    ]
    near_out = pl.pallas_call(
        functools.partial(near_kernel, rows=rows, n_samp=n_samp),
        out_shape=jax.ShapeDtypeStruct((leaf_count, comps, unknowns), F32),
        in_specs=[SMEM, VMEM, VMEM, VMEM, HBM],
        out_specs=VMEM,
        scratch_shapes=[
            pltpu.VMEM((leaves, 16, block), BF16),
            pltpu.VMEM(near_blocks.shape, BF16),
            pltpu.SemaphoreType.DMA((leaf_count,)),
        ],
        compiler_params=params(),
        name="near",
    )(near_src, here, first, second, near_blocks)
    return pl.pallas_call(
        receive_kernel,
        out_shape=jax.ShapeDtypeStruct((leaf_count, comps, unknowns), F32),
        in_specs=[VMEM] * (2 + n_samp),
        out_specs=VMEM,
        compiler_params=params(),
        name="receive",
    )(near_out, radiation, *received)


def solution(mesh):
    placed = (
        P(("box", "samp"), None, None),
        P(("box", "samp"), None, None, None, None),
        P(("box", "samp"), None, None, None, None),
        P(("box", "samp"), None),
        P("box"),
        P("box"),
        P(None, None, "samp"),
        P("samp", None),
        P("samp", None, None, None),
        P("box", None),
        P("box", None),
        P(None, None, "samp"),
    )
    return jax.shard_map(
        per_device,
        mesh=mesh,
        in_specs=placed,
        out_specs=P(("box", "samp"), None, None),
        check_vma=False,
    )
```

```python
import functools

import jax
import jax.numpy as jnp
from jax import lax
from jax.experimental import pallas as pl
from jax.experimental.pallas import tpu as pltpu
from jax.sharding import PartitionSpec as P

F32 = jnp.float32
BF16 = jnp.bfloat16
HBM = pl.BlockSpec(memory_space=pltpu.HBM)
VMEM = pl.BlockSpec(memory_space=pltpu.VMEM)
SMEM = pl.BlockSpec(memory_space=pltpu.SMEM)
NT = (((1,), (1,)), ((), ()))
LIMIT = 14 * 1024 * 1024


def params():
    return pltpu.CompilerParams(vmem_limit_bytes=LIMIT)


def pinned(*arrays):
    return [pltpu.with_memory_space_constraint(array, pltpu.HBM) for array in arrays]


def radiate_kernel(
    parent_hbm,
    shift_hbm,
    cur_hbm,
    rad_hbm,
    val_hbm,
    phase_hbm,
    trans_hbm,
    msg_ref,
    val_ref,
    phase_ref,
    trans_ref,
    parent_ref,
    shift_ref,
    cur_ref,
    rad_ref,
    sem,
    *,
    top_count,
):
    leaf_count, in_blocks = cur_ref.shape[0], msg_ref.shape[0]
    block = msg_ref.shape[2]
    half = cur_ref.shape[1] // 2
    group = parent_ref.shape[0]
    firsts = [
        pltpu.make_async_copy(src, dst, sem.at[leaf_count + n])
        for n, (src, dst) in enumerate(
            ((parent_hbm, parent_ref), (shift_hbm, shift_ref), (cur_hbm, cur_ref))
        )
    ]
    for copy in firsts:
        copy.start()
    copies = [
        pltpu.make_async_copy(rad_hbm.at[leaf], rad_ref.at[leaf], sem.at[leaf])
        for leaf in range(leaf_count)
    ]
    for copy in copies:
        copy.start()
    later = [
        pltpu.make_async_copy(src, dst, sem.at[leaf_count + 3 + n])
        for n, (src, dst) in enumerate(
            ((trans_hbm, trans_ref), (phase_hbm, phase_ref), (val_hbm, val_ref))
        )
    ]
    for copy in later:
        copy.start()
    base = leaf_count * 4 * half
    lane = lax.broadcasted_iota(jnp.int32, (8, block), 1)
    line = lax.broadcasted_iota(jnp.int32, (8, block), 0)
    meta = jnp.zeros((8, block), jnp.int32)
    for copy in firsts:
        copy.wait()
    for member in range(group):
        pair = jnp.where(
            line == 0, lax.rem(parent_ref[member], top_count), shift_ref[member]
        )
        meta = jnp.where(lane == member, pair, meta)
    meta = meta.astype(F32)
    zero = jnp.zeros((half, cur_ref.shape[2]), F32)
    left = []
    for leaf in range(leaf_count):
        cur = cur_ref[leaf].astype(F32)
        real, imag = cur[:half], cur[half:]
        pieces = [
            jnp.concatenate(rows, axis=0).astype(BF16)
            for rows in (
                (real, zero, imag, zero),
                (-imag, zero, real, zero),
                (zero, real, zero, imag),
                (zero, -imag, zero, real),
            )
        ]
        left.append(jnp.concatenate(pieces, axis=1))
        row = base + leaf // in_blocks * 4 * half
        msg_ref[leaf % in_blocks, row : row + 4 * half, :] = jnp.concatenate(
            [cur, meta], axis=0
        ).astype(BF16)
    for leaf in range(leaf_count):
        copies[leaf].wait()
        right = jnp.concatenate(
            [rad_ref[leaf, p, r] for p in range(2) for r in range(2)], axis=1
        )
        out = lax.dot_general(left[leaf], right, NT, preferred_element_type=F32).astype(BF16)
        for b in range(in_blocks):
            msg_ref[b, leaf * 4 * half : (leaf + 1) * 4 * half, :] = out[
                :, b * block : (b + 1) * block
            ]
    for copy in later:
        copy.wait()


def lift_groups(refs, dense_ref, shift_ref, top_ref, rows, base, ready):
    left = jnp.concatenate(
        [
            jnp.concatenate([ref[samp, c, :rows, :] for c in range(ref.shape[1])], axis=1)
            for ref in refs
            for samp in range(ref.shape[0])
        ],
        axis=0,
    )
    local_blocks, _, block = top_ref.shape[2:]
    width = min(8, local_blocks)
    for start in range(0, local_blocks, width):
        moved = lax.dot_general(
            left,
            dense_ref[start * block : (start + width) * block, :],
            NT,
            preferred_element_type=F32,
        )
        if start == 0:
            sids = ready()
        for b in range(width):
            for s, sid in enumerate(sids):
                real = moved[s * 16 : s * 16 + 8, b * block : (b + 1) * block]
                imag = moved[s * 16 + 8 : s * 16 + 16, b * block : (b + 1) * block]
                shift_real, shift_imag = shift_ref[sid, start + b], shift_ref[sid + 1, start + b]
                top_ref[base + s, 0, start + b] = real * shift_real - imag * shift_imag
                top_ref[base + s, 1, start + b] = real * shift_imag + imag * shift_real


def spread_rows(src_ref, out_ref):
    count, local_blocks, block = src_ref.shape

    def one(index, carry):
        for b in range(local_blocks):
            out_ref[index, b] = jnp.broadcast_to(src_ref[index, b : b + 1, :], (8, block))
        return carry

    lax.fori_loop(0, count, one, 0)


def tables_kernel(
    idx_ref, val_ref, shift_ref, trans_ref, dense_ref, wide_shift_ref, wide_trans_ref
):
    spread_rows(shift_ref, wide_shift_ref)
    local_blocks, _, block, _ = val_ref.shape

    def one(b, carry):
        first, second = idx_ref[0, b], idx_ref[1, b]
        zero = jnp.zeros((block, block), BF16)
        for c in range(dense_ref.shape[1] // block):
            dense_ref[pl.ds(pl.multiple_of(b * block, block), block), c * block : (c + 1) * block] = (
                jnp.where(first == c, val_ref[b, 0], jnp.where(second == c, val_ref[b, 1], zero))
            )
        return carry

    lax.fori_loop(0, local_blocks, one, 0)
    spread_rows(trans_ref, wide_trans_ref)


def meta_of(msg_ref, rows):
    return msg_ref[0, 0, rows : rows + 16, :].astype(F32)[8:10]


def lift_kernel(
    sid_ref, here_ref, near_ref, dense_ref, shift_ref, top_ref, meta_ref, num_ref, sem, *, rows
):
    group = sid_ref.shape[0]
    meta_ref[...] = jnp.concatenate([meta_of(near_ref, rows)] * 4, axis=0).astype(jnp.int32)
    fetch = pltpu.make_async_copy(meta_ref, num_ref, sem)
    fetch.start()

    def ready():
        fetch.wait()
        return [2 * sid_ref[s] for s in range(group)] + [2 * num_ref[1, s] for s in range(group)]

    lift_groups((here_ref, near_ref), dense_ref, shift_ref, top_ref, rows, 0, ready)


def field_kernel(
    parent_ref,
    sid_ref,
    src_ref,
    disp_ref,
    here_ref,
    near_ref,
    far_ref,
    dense_ref,
    shift_ref,
    trans_ref,
    _,
    *rest,
    n_samp,
    leaf_count,
    tile,
):
    outs = rest[:n_samp]
    (
        top_ref,
        inc_ref,
        down_ref,
        acc_ref,
        meta_ref,
        num_ref,
        head_ref,
        rep_ref,
        count_ref,
        slot_ref,
        coef_ref,
        sem,
    ) = rest[n_samp:]
    block = here_ref.shape[3]
    local_blocks = top_ref.shape[2]
    leaves = top_ref.shape[0]
    group = leaves // 3
    rows = 16 * leaf_count
    top_count, entries = src_ref.shape
    where = lax.axis_index("box")
    me = lax.axis_index("samp")
    turned = jnp.where(me == 1, 1, 0) if n_samp == 2 else jnp.int32(0)
    bases = (1, 2 * turned, 2 - 2 * turned)

    lines = [meta_of(ref, rows) for ref in (here_ref, near_ref, far_ref)]
    meta_ref[...] = jnp.concatenate(lines + lines[:1], axis=0).astype(jnp.int32)
    fetch = pltpu.make_async_copy(meta_ref, num_ref, sem)
    fetch.start()
    for box in range(3 * top_count):
        head_ref[box] = -1

    def ready():
        fetch.wait()
        return [2 * num_ref[5, s] for s in range(group)]

    lift_groups((far_ref,), dense_ref, shift_ref, top_ref, rows, 2 * group, ready)
    boxes = [
        num_ref[2 * (s // group), s % group] + bases[s // group] * top_count for s in range(leaves)
    ]
    for s in reversed(range(leaves)):
        head_ref[boxes[s]] = s
    for s in range(leaves):
        rep_ref[s] = head_ref[boxes[s]]
    for leaf in range(group):
        parent = parent_ref[leaf] - where * top_count
        count = jnp.int32(0)
        slots = [head_ref[src_ref[parent, j] - (where - 1) * top_count] for j in range(entries)]
        coefs = [2 * disp_ref[parent, j] for j in range(entries)]
        for slot, coef in zip(slots, coefs):
            slot_ref[leaf, count] = slot
            coef_ref[leaf, count] = coef
            count += (slot >= 0).astype(jnp.int32)
        count_ref[leaf] = count

    def merge(s, carry):
        rep = rep_ref[s]

        @pl.when(rep != s)
        def _():
            top_ref[rep] = top_ref[rep] + top_ref[s]

        return carry

    lax.fori_loop(0, leaves, merge, 0)

    def target(leaf, carry):
        @pl.when(rep_ref[leaf] == leaf)
        def _():
            for t in range(local_blocks // tile):

                def entry(n, total):
                    slot, coef = slot_ref[leaf, n], coef_ref[leaf, n]
                    real, imag = list(total[:tile]), list(total[tile:])
                    for b in range(tile):
                        place = t * tile + b
                        coef_real, coef_imag = trans_ref[coef, place], trans_ref[coef + 1, place]
                        src_real, src_imag = top_ref[slot, 0, place], top_ref[slot, 1, place]
                        real[b] += coef_real * src_real - coef_imag * src_imag
                        imag[b] += coef_real * src_imag + coef_imag * src_real
                    return tuple(real + imag)

                zero = jnp.zeros((8, block), F32)
                total = lax.fori_loop(0, count_ref[leaf], entry, (zero,) * (2 * tile))
                for b in range(tile):
                    inc_ref[leaf, 0, t * tile + b] = total[b]
                    inc_ref[leaf, 1, t * tile + b] = total[tile + b]

        return carry

    lax.fori_loop(0, group, target, 0)

    def lower(leaf, carry):
        sid = 2 * sid_ref[leaf]
        rep = rep_ref[leaf]
        start = pl.multiple_of(leaf * 16, 16)
        for b in range(local_blocks):
            shift_real, shift_imag = shift_ref[sid, b], shift_ref[sid + 1, b]
            real, imag = inc_ref[rep, 0, b], inc_ref[rep, 1, b]
            down = jnp.concatenate(
                [
                    shift_real * real + shift_imag * imag,
                    shift_real * imag - shift_imag * real,
                ],
                axis=0,
            )
            down_ref[pl.ds(start, 16), b * block : (b + 1) * block] = down.astype(BF16)
        return carry

    lax.fori_loop(0, group, lower, 0)
    acc_ref[...] = jnp.dot(down_ref[...], dense_ref[...], preferred_element_type=F32)
    for d, out in enumerate(outs):
        owner = lax.rem(me + d, n_samp)
        start = pl.multiple_of(owner * rows, rows)
        for c in range(out.shape[0]):
            out[c] = acc_ref[pl.ds(start, rows), c * block : (c + 1) * block].astype(BF16)


def near_kernel(src_ref, here_ref, first_ref, second_ref, near_hbm, out_ref, cur_ref, near_ref, sem, *, rows, n_samp):
    leaf_count, near = near_ref.shape[:2]
    in_blocks = here_ref.shape[1]
    group = n_samp * leaf_count
    copies = [
        pltpu.make_async_copy(near_hbm.at[leaf], near_ref.at[leaf], sem.at[leaf])
        for leaf in range(leaf_count)
    ]
    for copy in copies:
        copy.start()
    where = lax.axis_index("box")
    turned = jnp.where(lax.axis_index("samp") == 1, 1, 0) if n_samp == 2 else jnp.int32(0)
    for place, ref in ((1, here_ref), (2 * turned, first_ref), (2 - 2 * turned, second_ref)):
        for leaf in range(group):
            samp, inner = leaf // leaf_count, leaf % leaf_count
            line = rows + inner // in_blocks * 16
            cur = ref[samp, inner % in_blocks, line : line + 16, :].astype(F32)
            cur_ref[place * group + leaf] = jnp.concatenate(
                [cur[:8], -cur[4:8], cur[:4]], axis=0
            ).astype(BF16)
    for leaf in range(leaf_count):
        left = jnp.concatenate(
            [cur_ref[src_ref[leaf, n] - (where - 1) * group] for n in range(near)], axis=1
        )
        copies[leaf].wait()
        out = [
            lax.dot_general(
                left,
                jnp.concatenate([near_ref[leaf, n, r] for n in range(near)], axis=1),
                NT,
                preferred_element_type=F32,
            )
            for r in range(2)
        ]
        out_ref[leaf] = out[0][:8] + out[1][8:]


def receive_kernel(near_ref, rad_ref, *rest):
    far_refs, out_ref = rest[:-1], rest[-1]
    leaf_count = out_ref.shape[0]
    far = far_refs[0][...].astype(F32)
    for ref in far_refs[1:]:
        far = far + ref[...].astype(F32)
    in_blocks = far.shape[0]
    unknowns = rad_ref.shape[4]
    depth = rad_ref.shape[1] * rad_ref.shape[2] * rad_ref.shape[3]
    for leaf in range(leaf_count):
        left = []
        for p in range(2):
            real = [far[b, leaf * 16 + p * 4 : leaf * 16 + p * 4 + 4] for b in range(in_blocks)]
            imag = [
                far[b, leaf * 16 + 8 + p * 4 : leaf * 16 + 12 + p * 4] for b in range(in_blocks)
            ]
            left += [jnp.concatenate(pair, axis=0) for pair in zip(real, imag)]
            left += [jnp.concatenate([i, -r], axis=0) for r, i in zip(real, imag)]
        wide = jnp.concatenate(left, axis=1).astype(BF16)
        right = rad_ref[leaf].reshape(depth, unknowns)
        out_ref[leaf] = near_ref[leaf] + jnp.dot(wide, right, preferred_element_type=F32)


def per_device(
    currents,
    radiation,
    near_blocks,
    near_src,
    leaf_parent,
    leaf_shift,
    shift_table,
    interp_idx,
    interp_val,
    top_src,
    top_disp,
    trans_table,
):
    n_samp = lax.axis_size("samp")
    n_box = lax.axis_size("box")
    leaf_count, comps, unknowns = currents.shape
    group = leaf_parent.shape[0]
    top_count, entries = top_src.shape
    local_blocks, _, block, _ = interp_val.shape
    in_blocks = radiation.shape[3] // block
    leaves = 3 * group
    rows = 16 * leaf_count
    extra = 16 * -(-leaf_count // in_blocks)
    tile = min(16, local_blocks)

    message, values, phases, moves = pl.pallas_call(
        functools.partial(radiate_kernel, top_count=top_count),
        out_shape=[
            jax.ShapeDtypeStruct((in_blocks, rows + extra, block), BF16),
            pltpu.VMEM(interp_val.shape, BF16),
            pltpu.VMEM(shift_table.shape, BF16),
            pltpu.VMEM(trans_table.shape, BF16),
        ],
        in_specs=[HBM] * 7,
        out_specs=[VMEM] * 4,
        scratch_shapes=[
            pltpu.SMEM(leaf_parent.shape, jnp.int32),
            pltpu.SMEM(leaf_shift.shape, jnp.int32),
            pltpu.VMEM(currents.shape, BF16),
            pltpu.VMEM(radiation.shape, BF16),
            pltpu.SemaphoreType.DMA((leaf_count + 6,)),
        ],
        compiler_params=params(),
        name="radiate",
    )(
        *pinned(
            leaf_parent, leaf_shift, currents, radiation, interp_val, shift_table, trans_table
        )
    )

    here = lax.all_gather(message, "samp", axis=0)
    last = n_samp - 1
    swap = []
    for box in range(n_box - 1):
        low, high = box * n_samp + last, (box + 1) * n_samp
        swap += [(low, high), (high, low)]
    beyond = lax.ppermute(here, ("box", "samp"), swap)
    shift_rows = phases.astype(F32).reshape(-1, local_blocks, block)
    trans_rows = moves.astype(F32).reshape(-1, local_blocks, block)
    work = 2 * leaves * 16 * in_blocks * block * local_blocks * block
    dense, wide_shift, wide_trans = pl.pallas_call(
        tables_kernel,
        out_shape=[
            pltpu.VMEM((local_blocks * block, in_blocks * block), BF16),
            pltpu.VMEM((shift_rows.shape[0], local_blocks, 8, block), F32),
            pltpu.VMEM((trans_rows.shape[0], local_blocks, 8, block), F32),
        ],
        in_specs=[SMEM] + [VMEM] * 3,
        out_specs=[VMEM] * 3,
        compiler_params=params(),
        cost_estimate=pl.CostEstimate(flops=work, bytes_accessed=1 << 24, transcendentals=0),
        name="tables",
    )(interp_idx.T, values, shift_rows, trans_rows)
    beyond, dense = lax.optimization_barrier((beyond, dense))
    if n_samp == 2:
        first = beyond
        second = lax.ppermute(beyond, "samp", [(0, 1), (1, 0)])
    else:
        ends = lax.all_gather(beyond, "samp", axis=0)
        first, second = ends[0], ends[n_samp - 1]
    numbers = [pltpu.VMEM((8, block), jnp.int32), pltpu.SMEM((8, block), jnp.int32)]
    top_shape = pltpu.VMEM((leaves, 2, local_blocks, 8, block), F32)
    lifted = pl.pallas_call(
        functools.partial(lift_kernel, rows=rows),
        out_shape=top_shape,
        in_specs=[SMEM] + [VMEM] * 4,
        out_specs=VMEM,
        scratch_shapes=numbers + [pltpu.SemaphoreType.DMA],
        compiler_params=params(),
        cost_estimate=pl.CostEstimate(flops=work, bytes_accessed=1 << 23, transcendentals=0),
        name="lift",
    )(leaf_shift, here, first, dense, wide_shift)

    *fars, _ = pl.pallas_call(
        functools.partial(field_kernel, n_samp=n_samp, leaf_count=leaf_count, tile=tile),
        out_shape=[jax.ShapeDtypeStruct((in_blocks, rows, block), BF16)] * n_samp
        + [top_shape],
        in_specs=[SMEM] * 4 + [VMEM] * 7,
        out_specs=[VMEM] * (n_samp + 1),
        scratch_shapes=[
            pltpu.VMEM((group, 2, local_blocks, 8, block), F32),
            pltpu.VMEM((group * 16, local_blocks * block), BF16),
            pltpu.VMEM((group * 16, in_blocks * block), F32),
            *numbers,
            pltpu.SMEM((3 * top_count,), jnp.int32),
            pltpu.SMEM((leaves,), jnp.int32),
            pltpu.SMEM((group,), jnp.int32),
            pltpu.SMEM((group, entries), jnp.int32),
            pltpu.SMEM((group, entries), jnp.int32),
            pltpu.SemaphoreType.DMA,
        ],
        input_output_aliases={10: n_samp},
        compiler_params=params(),
        name="field",
    )(
        leaf_parent,
        leaf_shift,
        top_src,
        top_disp,
        here,
        first,
        second,
        dense,
        wide_shift,
        wide_trans,
        lifted,
    )
    received = [fars[0]] + [
        lax.ppermute(fars[d], "samp", [(i, (i + d) % n_samp) for i in range(n_samp)])
        for d in range(1, n_samp)
    ]
    near_out = pl.pallas_call(
        functools.partial(near_kernel, rows=rows, n_samp=n_samp),
        out_shape=jax.ShapeDtypeStruct((leaf_count, comps, unknowns), F32),
        in_specs=[SMEM, VMEM, VMEM, VMEM, HBM],
        out_specs=VMEM,
        scratch_shapes=[
            pltpu.VMEM((leaves, 16, block), BF16),
            pltpu.VMEM(near_blocks.shape, BF16),
            pltpu.SemaphoreType.DMA((leaf_count,)),
        ],
        compiler_params=params(),
        name="near",
    )(near_src, here, first, second, near_blocks)
    return pl.pallas_call(
        receive_kernel,
        out_shape=jax.ShapeDtypeStruct((leaf_count, comps, unknowns), F32),
        in_specs=[VMEM] * (2 + n_samp),
        out_specs=VMEM,
        compiler_params=params(),
        name="receive",
    )(near_out, radiation, *received)


def solution(mesh):
    placed = (
        P(("box", "samp"), None, None),
        P(("box", "samp"), None, None, None, None),
        P(("box", "samp"), None, None, None, None),
        P(("box", "samp"), None),
        P("box"),
        P("box"),
        P(None, None, "samp"),
        P("samp", None),
        P("samp", None, None, None),
        P("box", None),
        P("box", None),
        P(None, None, "samp"),
    )
    return jax.shard_map(
        per_device,
        mesh=mesh,
        in_specs=placed,
        out_specs=P(("box", "samp"), None, None),
        check_vma=False,
    )
```

```python
import functools

import jax
import jax.numpy as jnp
from jax import lax
from jax.experimental import pallas as pl
from jax.experimental.pallas import tpu as pltpu
from jax.sharding import PartitionSpec as P

F32 = jnp.float32
BF16 = jnp.bfloat16
HBM = pl.BlockSpec(memory_space=pltpu.HBM)
VMEM = pl.BlockSpec(memory_space=pltpu.VMEM)
SMEM = pl.BlockSpec(memory_space=pltpu.SMEM)
NT = (((1,), (1,)), ((), ()))
LIMIT = 14 * 1024 * 1024


def params():
    return pltpu.CompilerParams(vmem_limit_bytes=LIMIT)


def pinned(*arrays):
    return [pltpu.with_memory_space_constraint(array, pltpu.HBM) for array in arrays]


def radiate_kernel(
    parent_hbm,
    shift_hbm,
    cur_hbm,
    rad_hbm,
    phase_hbm,
    trans_hbm,
    msg_ref,
    phase_ref,
    trans_ref,
    parent_ref,
    shift_ref,
    cur_ref,
    rad_ref,
    sem,
    *,
    top_count,
):
    leaf_count, in_blocks = cur_ref.shape[0], msg_ref.shape[0]
    block = msg_ref.shape[2]
    half = cur_ref.shape[1] // 2
    group = parent_ref.shape[0]
    firsts = [
        pltpu.make_async_copy(src, dst, sem.at[leaf_count + n])
        for n, (src, dst) in enumerate(
            ((parent_hbm, parent_ref), (shift_hbm, shift_ref), (cur_hbm, cur_ref))
        )
    ]
    for copy in firsts:
        copy.start()
    copies = [
        pltpu.make_async_copy(rad_hbm.at[leaf], rad_ref.at[leaf], sem.at[leaf])
        for leaf in range(leaf_count)
    ]
    for copy in copies:
        copy.start()
    later = [
        pltpu.make_async_copy(src, dst, sem.at[leaf_count + 3 + n])
        for n, (src, dst) in enumerate(
            ((trans_hbm, trans_ref), (phase_hbm, phase_ref))
        )
    ]
    for copy in later:
        copy.start()
    base = leaf_count * 4 * half
    lane = lax.broadcasted_iota(jnp.int32, (8, block), 1)
    line = lax.broadcasted_iota(jnp.int32, (8, block), 0)
    meta = jnp.zeros((8, block), jnp.int32)
    for copy in firsts:
        copy.wait()
    for member in range(group):
        pair = jnp.where(
            line == 0, lax.rem(parent_ref[member], top_count), shift_ref[member]
        )
        meta = jnp.where(lane == member, pair, meta)
    meta = meta.astype(F32)
    zero = jnp.zeros((half, cur_ref.shape[2]), F32)
    left = []
    for leaf in range(leaf_count):
        cur = cur_ref[leaf].astype(F32)
        real, imag = cur[:half], cur[half:]
        pieces = [
            jnp.concatenate(rows, axis=0).astype(BF16)
            for rows in (
                (real, zero, imag, zero),
                (-imag, zero, real, zero),
                (zero, real, zero, imag),
                (zero, -imag, zero, real),
            )
        ]
        left.append(jnp.concatenate(pieces, axis=1))
        row = base + leaf // in_blocks * 4 * half
        msg_ref[leaf % in_blocks, row : row + 4 * half, :] = jnp.concatenate(
            [cur, meta], axis=0
        ).astype(BF16)
    for leaf in range(leaf_count):
        copies[leaf].wait()
        right = jnp.concatenate(
            [rad_ref[leaf, p, r] for p in range(2) for r in range(2)], axis=1
        )
        out = lax.dot_general(left[leaf], right, NT, preferred_element_type=F32).astype(BF16)
        for b in range(in_blocks):
            msg_ref[b, leaf * 4 * half : (leaf + 1) * 4 * half, :] = out[
                :, b * block : (b + 1) * block
            ]
    for copy in later:
        copy.wait()


def lift_groups(refs, dense_ref, shift_ref, top_ref, rows, base, ready):
    left = jnp.concatenate(
        [
            jnp.concatenate([ref[samp, c, :rows, :] for c in range(ref.shape[1])], axis=1)
            for ref in refs
            for samp in range(ref.shape[0])
        ],
        axis=0,
    )
    local_blocks, _, block = top_ref.shape[2:]
    width = min(8, local_blocks)
    for start in range(0, local_blocks, width):
        moved = lax.dot_general(
            left,
            dense_ref[start * block : (start + width) * block, :],
            NT,
            preferred_element_type=F32,
        )
        if start == 0:
            sids = ready()
        for b in range(width):
            for s, sid in enumerate(sids):
                real = moved[s * 16 : s * 16 + 8, b * block : (b + 1) * block]
                imag = moved[s * 16 + 8 : s * 16 + 16, b * block : (b + 1) * block]
                shift_real, shift_imag = shift_ref[sid, start + b], shift_ref[sid + 1, start + b]
                top_ref[base + s, 0, start + b] = real * shift_real - imag * shift_imag
                top_ref[base + s, 1, start + b] = real * shift_imag + imag * shift_real


def spread_rows(src_ref, out_ref):
    count, local_blocks, block = src_ref.shape

    def one(index, carry):
        for b in range(local_blocks):
            out_ref[index, b] = jnp.broadcast_to(src_ref[index, b : b + 1, :], (8, block))
        return carry

    lax.fori_loop(0, count, one, 0)


def tables_kernel(
    idx_ref,
    sid_ref,
    val_hbm,
    here_ref,
    shift_ref,
    trans_ref,
    dense_ref,
    wide_shift_ref,
    wide_trans_ref,
    top_ref,
    val_ref,
    sem,
    *,
    rows,
):
    load = pltpu.make_async_copy(val_hbm, val_ref, sem)
    load.start()
    spread_rows(shift_ref, wide_shift_ref)
    spread_rows(trans_ref, wide_trans_ref)
    load.wait()
    local_blocks, _, block, _ = val_ref.shape

    def one(b, carry):
        first, second = idx_ref[0, b], idx_ref[1, b]
        zero = jnp.zeros((block, block), BF16)
        for c in range(dense_ref.shape[1] // block):
            dense_ref[pl.ds(pl.multiple_of(b * block, block), block), c * block : (c + 1) * block] = (
                jnp.where(first == c, val_ref[b, 0], jnp.where(second == c, val_ref[b, 1], zero))
            )
        return carry

    lax.fori_loop(0, local_blocks, one, 0)
    sids = [2 * sid_ref[s] for s in range(sid_ref.shape[0])]
    lift_groups((here_ref,), dense_ref, wide_shift_ref, top_ref, rows, 0, lambda: sids)


def meta_of(msg_ref, rows):
    return msg_ref[0, 0, rows : rows + 16, :].astype(F32)[8:10]


def lift_kernel(near_ref, dense_ref, shift_ref, _, top_ref, meta_ref, num_ref, sem, *, rows):
    group = top_ref.shape[0] // 3
    meta_ref[...] = jnp.concatenate([meta_of(near_ref, rows)] * 4, axis=0).astype(jnp.int32)
    fetch = pltpu.make_async_copy(meta_ref, num_ref, sem)
    fetch.start()

    def ready():
        fetch.wait()
        return [2 * num_ref[1, s] for s in range(group)]

    lift_groups((near_ref,), dense_ref, shift_ref, top_ref, rows, group, ready)


def field_kernel(
    parent_hbm,
    sid_hbm,
    src_hbm,
    disp_hbm,
    here_ref,
    near_ref,
    far_ref,
    dense_ref,
    shift_ref,
    trans_ref,
    _,
    *rest,
    n_samp,
    leaf_count,
    tile,
):
    outs = rest[:n_samp]
    (
        top_ref,
        parent_ref,
        sid_ref,
        src_ref,
        disp_ref,
        inc_ref,
        down_ref,
        acc_ref,
        meta_ref,
        num_ref,
        head_ref,
        rep_ref,
        count_ref,
        slot_ref,
        coef_ref,
        sem,
    ) = rest[n_samp:]
    block = here_ref.shape[3]
    local_blocks = top_ref.shape[2]
    leaves = top_ref.shape[0]
    group = leaves // 3
    rows = 16 * leaf_count
    top_count, entries = src_ref.shape
    where = lax.axis_index("box")
    me = lax.axis_index("samp")
    turned = jnp.where(me == 1, 1, 0) if n_samp == 2 else jnp.int32(0)
    bases = (1, 2 * turned, 2 - 2 * turned)

    lines = [meta_of(ref, rows) for ref in (here_ref, near_ref, far_ref)]
    meta_ref[...] = jnp.concatenate(lines + lines[:1], axis=0).astype(jnp.int32)
    fetches = [
        pltpu.make_async_copy(src, dst, sem.at[n])
        for n, (src, dst) in enumerate(
            (
                (parent_hbm, parent_ref),
                (sid_hbm, sid_ref),
                (src_hbm, src_ref),
                (disp_hbm, disp_ref),
                (meta_ref, num_ref),
            )
        )
    ]
    for fetch in fetches:
        fetch.start()
    for box in range(3 * top_count):
        head_ref[box] = -1

    def ready():
        for fetch in fetches:
            fetch.wait()
        return [2 * num_ref[5, s] for s in range(group)]

    lift_groups((far_ref,), dense_ref, shift_ref, top_ref, rows, 2 * group, ready)
    boxes = [
        num_ref[2 * (s // group), s % group] + bases[s // group] * top_count for s in range(leaves)
    ]
    for s in reversed(range(leaves)):
        head_ref[boxes[s]] = s
    for s in range(leaves):
        rep_ref[s] = head_ref[boxes[s]]
    for leaf in range(group):
        parent = parent_ref[leaf] - where * top_count
        count = jnp.int32(0)
        slots = [head_ref[src_ref[parent, j] - (where - 1) * top_count] for j in range(entries)]
        coefs = [2 * disp_ref[parent, j] for j in range(entries)]
        for slot, coef in zip(slots, coefs):
            slot_ref[leaf, count] = slot
            coef_ref[leaf, count] = coef
            count += (slot >= 0).astype(jnp.int32)
        count_ref[leaf] = count

    def merge(s, carry):
        rep = rep_ref[s]

        @pl.when(rep != s)
        def _():
            top_ref[rep] = top_ref[rep] + top_ref[s]

        return carry

    lax.fori_loop(0, leaves, merge, 0)

    def target(leaf, carry):
        @pl.when(rep_ref[leaf] == leaf)
        def _():
            for t in range(local_blocks // tile):

                def entry(n, total):
                    slot, coef = slot_ref[leaf, n], coef_ref[leaf, n]
                    real, imag = list(total[:tile]), list(total[tile:])
                    for b in range(tile):
                        place = t * tile + b
                        coef_real, coef_imag = trans_ref[coef, place], trans_ref[coef + 1, place]
                        src_real, src_imag = top_ref[slot, 0, place], top_ref[slot, 1, place]
                        real[b] += coef_real * src_real - coef_imag * src_imag
                        imag[b] += coef_real * src_imag + coef_imag * src_real
                    return tuple(real + imag)

                zero = jnp.zeros((8, block), F32)
                total = lax.fori_loop(0, count_ref[leaf], entry, (zero,) * (2 * tile))
                for b in range(tile):
                    inc_ref[leaf, 0, t * tile + b] = total[b]
                    inc_ref[leaf, 1, t * tile + b] = total[tile + b]

        return carry

    lax.fori_loop(0, group, target, 0)

    def lower(leaf, carry):
        sid = 2 * sid_ref[leaf]
        rep = rep_ref[leaf]
        start = pl.multiple_of(leaf * 16, 16)
        for b in range(local_blocks):
            shift_real, shift_imag = shift_ref[sid, b], shift_ref[sid + 1, b]
            real, imag = inc_ref[rep, 0, b], inc_ref[rep, 1, b]
            down = jnp.concatenate(
                [
                    shift_real * real + shift_imag * imag,
                    shift_real * imag - shift_imag * real,
                ],
                axis=0,
            )
            down_ref[pl.ds(start, 16), b * block : (b + 1) * block] = down.astype(BF16)
        return carry

    lax.fori_loop(0, group, lower, 0)
    acc_ref[...] = jnp.dot(down_ref[...], dense_ref[...], preferred_element_type=F32)
    for d, out in enumerate(outs):
        owner = lax.rem(me + d, n_samp)
        start = pl.multiple_of(owner * rows, rows)
        for c in range(out.shape[0]):
            out[c] = acc_ref[pl.ds(start, rows), c * block : (c + 1) * block].astype(BF16)


def near_kernel(src_ref, here_ref, first_ref, second_ref, near_hbm, out_ref, cur_ref, near_ref, sem, *, rows, n_samp):
    leaf_count, near = near_ref.shape[:2]
    in_blocks = here_ref.shape[1]
    group = n_samp * leaf_count
    copies = [
        pltpu.make_async_copy(near_hbm.at[leaf], near_ref.at[leaf], sem.at[leaf])
        for leaf in range(leaf_count)
    ]
    for copy in copies:
        copy.start()
    where = lax.axis_index("box")
    turned = jnp.where(lax.axis_index("samp") == 1, 1, 0) if n_samp == 2 else jnp.int32(0)
    for place, ref in ((1, here_ref), (2 * turned, first_ref), (2 - 2 * turned, second_ref)):
        for leaf in range(group):
            samp, inner = leaf // leaf_count, leaf % leaf_count
            line = rows + inner // in_blocks * 16
            cur = ref[samp, inner % in_blocks, line : line + 16, :].astype(F32)
            cur_ref[place * group + leaf] = jnp.concatenate(
                [cur[:8], -cur[4:8], cur[:4]], axis=0
            ).astype(BF16)
    for leaf in range(leaf_count):
        left = jnp.concatenate(
            [cur_ref[src_ref[leaf, n] - (where - 1) * group] for n in range(near)], axis=1
        )
        copies[leaf].wait()
        out = [
            lax.dot_general(
                left,
                jnp.concatenate([near_ref[leaf, n, r] for n in range(near)], axis=1),
                NT,
                preferred_element_type=F32,
            )
            for r in range(2)
        ]
        out_ref[leaf] = out[0][:8] + out[1][8:]


def receive_kernel(near_ref, rad_ref, *rest):
    far_refs, out_ref = rest[:-1], rest[-1]
    leaf_count = out_ref.shape[0]
    far = far_refs[0][...].astype(F32)
    for ref in far_refs[1:]:
        far = far + ref[...].astype(F32)
    in_blocks = far.shape[0]
    unknowns = rad_ref.shape[4]
    depth = rad_ref.shape[1] * rad_ref.shape[2] * rad_ref.shape[3]
    for leaf in range(leaf_count):
        left = []
        for p in range(2):
            real = [far[b, leaf * 16 + p * 4 : leaf * 16 + p * 4 + 4] for b in range(in_blocks)]
            imag = [
                far[b, leaf * 16 + 8 + p * 4 : leaf * 16 + 12 + p * 4] for b in range(in_blocks)
            ]
            left += [jnp.concatenate(pair, axis=0) for pair in zip(real, imag)]
            left += [jnp.concatenate([i, -r], axis=0) for r, i in zip(real, imag)]
        wide = jnp.concatenate(left, axis=1).astype(BF16)
        right = rad_ref[leaf].reshape(depth, unknowns)
        out_ref[leaf] = near_ref[leaf] + jnp.dot(wide, right, preferred_element_type=F32)


def per_device(
    currents,
    radiation,
    near_blocks,
    near_src,
    leaf_parent,
    leaf_shift,
    shift_table,
    interp_idx,
    interp_val,
    top_src,
    top_disp,
    trans_table,
):
    n_samp = lax.axis_size("samp")
    n_box = lax.axis_size("box")
    leaf_count, comps, unknowns = currents.shape
    group = leaf_parent.shape[0]
    top_count, entries = top_src.shape
    local_blocks, _, block, _ = interp_val.shape
    in_blocks = radiation.shape[3] // block
    leaves = 3 * group
    rows = 16 * leaf_count
    extra = 16 * -(-leaf_count // in_blocks)
    tile = min(16, local_blocks)

    message, phases, moves = pl.pallas_call(
        functools.partial(radiate_kernel, top_count=top_count),
        out_shape=[
            jax.ShapeDtypeStruct((in_blocks, rows + extra, block), BF16),
            pltpu.VMEM(shift_table.shape, BF16),
            pltpu.VMEM(trans_table.shape, BF16),
        ],
        in_specs=[HBM] * 6,
        out_specs=[VMEM] * 3,
        scratch_shapes=[
            pltpu.SMEM(leaf_parent.shape, jnp.int32),
            pltpu.SMEM(leaf_shift.shape, jnp.int32),
            pltpu.VMEM(currents.shape, BF16),
            pltpu.VMEM(radiation.shape, BF16),
            pltpu.SemaphoreType.DMA((leaf_count + 5,)),
        ],
        compiler_params=params(),
        name="radiate",
    )(
        *pinned(
            leaf_parent, leaf_shift, currents, radiation, shift_table, trans_table
        )
    )

    here = lax.all_gather(message, "samp", axis=0)
    last = n_samp - 1
    swap = []
    for box in range(n_box - 1):
        low, high = box * n_samp + last, (box + 1) * n_samp
        swap += [(low, high), (high, low)]
    beyond = lax.ppermute(here, ("box", "samp"), swap)
    shift_rows = phases.astype(F32).reshape(-1, local_blocks, block)
    trans_rows = moves.astype(F32).reshape(-1, local_blocks, block)
    work = 2 * leaves * 16 * in_blocks * block * local_blocks * block
    top_shape = pltpu.VMEM((leaves, 2, local_blocks, 8, block), F32)
    dense, wide_shift, wide_trans, own_top = pl.pallas_call(
        functools.partial(tables_kernel, rows=rows),
        out_shape=[
            pltpu.VMEM((local_blocks * block, in_blocks * block), BF16),
            pltpu.VMEM((shift_rows.shape[0], local_blocks, 8, block), F32),
            pltpu.VMEM((trans_rows.shape[0], local_blocks, 8, block), F32),
            top_shape,
        ],
        in_specs=[SMEM, SMEM, HBM] + [VMEM] * 3,
        out_specs=[VMEM] * 4,
        scratch_shapes=[pltpu.VMEM(interp_val.shape, BF16), pltpu.SemaphoreType.DMA],
        compiler_params=params(),
        cost_estimate=pl.CostEstimate(flops=work, bytes_accessed=1 << 24, transcendentals=0),
        name="tables",
    )(interp_idx.T, leaf_shift, *pinned(interp_val), here, shift_rows, trans_rows)
    beyond, dense = lax.optimization_barrier((beyond, dense))
    if n_samp == 2:
        first = beyond
        second = lax.ppermute(beyond, "samp", [(0, 1), (1, 0)])
    else:
        ends = lax.all_gather(beyond, "samp", axis=0)
        first, second = ends[0], ends[n_samp - 1]
    numbers = [pltpu.VMEM((8, block), jnp.int32), pltpu.SMEM((8, block), jnp.int32)]
    lifted = pl.pallas_call(
        functools.partial(lift_kernel, rows=rows),
        out_shape=top_shape,
        in_specs=[VMEM] * 4,
        out_specs=VMEM,
        scratch_shapes=numbers + [pltpu.SemaphoreType.DMA],
        input_output_aliases={3: 0},
        compiler_params=params(),
        cost_estimate=pl.CostEstimate(flops=work, bytes_accessed=1 << 23, transcendentals=0),
        name="lift",
    )(first, dense, wide_shift, own_top)

    *fars, _ = pl.pallas_call(
        functools.partial(field_kernel, n_samp=n_samp, leaf_count=leaf_count, tile=tile),
        out_shape=[jax.ShapeDtypeStruct((in_blocks, rows, block), BF16)] * n_samp
        + [top_shape],
        in_specs=[HBM] * 4 + [VMEM] * 7,
        out_specs=[VMEM] * (n_samp + 1),
        scratch_shapes=[
            pltpu.SMEM(leaf_parent.shape, jnp.int32),
            pltpu.SMEM(leaf_shift.shape, jnp.int32),
            pltpu.SMEM(top_src.shape, jnp.int32),
            pltpu.SMEM(top_disp.shape, jnp.int32),
            pltpu.VMEM((group, 2, local_blocks, 8, block), F32),
            pltpu.VMEM((group * 16, local_blocks * block), BF16),
            pltpu.VMEM((group * 16, in_blocks * block), F32),
            *numbers,
            pltpu.SMEM((3 * top_count,), jnp.int32),
            pltpu.SMEM((leaves,), jnp.int32),
            pltpu.SMEM((group,), jnp.int32),
            pltpu.SMEM((group, entries), jnp.int32),
            pltpu.SMEM((group, entries), jnp.int32),
            pltpu.SemaphoreType.DMA((5,)),
        ],
        input_output_aliases={10: n_samp},
        compiler_params=params(),
        name="field",
    )(
        *pinned(leaf_parent, leaf_shift, top_src, top_disp),
        here,
        first,
        second,
        dense,
        wide_shift,
        wide_trans,
        lifted,
    )
    received = [fars[0]] + [
        lax.ppermute(fars[d], "samp", [(i, (i + d) % n_samp) for i in range(n_samp)])
        for d in range(1, n_samp)
    ]
    near_out = pl.pallas_call(
        functools.partial(near_kernel, rows=rows, n_samp=n_samp),
        out_shape=jax.ShapeDtypeStruct((leaf_count, comps, unknowns), F32),
        in_specs=[SMEM, VMEM, VMEM, VMEM, HBM],
        out_specs=VMEM,
        scratch_shapes=[
            pltpu.VMEM((leaves, 16, block), BF16),
            pltpu.VMEM(near_blocks.shape, BF16),
            pltpu.SemaphoreType.DMA((leaf_count,)),
        ],
        compiler_params=params(),
        name="near",
    )(near_src, here, first, second, near_blocks)
    return pl.pallas_call(
        receive_kernel,
        out_shape=jax.ShapeDtypeStruct((leaf_count, comps, unknowns), F32),
        in_specs=[VMEM] * (2 + n_samp),
        out_specs=VMEM,
        compiler_params=params(),
        name="receive",
    )(near_out, radiation, *received)


def solution(mesh):
    placed = (
        P(("box", "samp"), None, None),
        P(("box", "samp"), None, None, None, None),
        P(("box", "samp"), None, None, None, None),
        P(("box", "samp"), None),
        P("box"),
        P("box"),
        P(None, None, "samp"),
        P("samp", None),
        P("samp", None, None, None),
        P("box", None),
        P("box", None),
        P(None, None, "samp"),
    )
    return jax.shard_map(
        per_device,
        mesh=mesh,
        in_specs=placed,
        out_specs=P(("box", "samp"), None, None),
        check_vma=False,
    )
```

```python
import functools

import jax
import jax.numpy as jnp
from jax import lax
from jax.experimental import pallas as pl
from jax.experimental.pallas import tpu as pltpu
from jax.sharding import PartitionSpec as P

F32 = jnp.float32
BF16 = jnp.bfloat16
HBM = pl.BlockSpec(memory_space=pltpu.HBM)
VMEM = pl.BlockSpec(memory_space=pltpu.VMEM)
SMEM = pl.BlockSpec(memory_space=pltpu.SMEM)
NT = (((1,), (1,)), ((), ()))
LIMIT = 14 * 1024 * 1024


def params():
    return pltpu.CompilerParams(vmem_limit_bytes=LIMIT)


def pinned(*arrays):
    return [pltpu.with_memory_space_constraint(array, pltpu.HBM) for array in arrays]


def radiate_kernel(
    parent_hbm,
    shift_hbm,
    cur_hbm,
    rad_hbm,
    phase_hbm,
    trans_hbm,
    msg_ref,
    phase_ref,
    trans_ref,
    parent_ref,
    shift_ref,
    cur_ref,
    rad_ref,
    sem,
    *,
    top_count,
):
    leaf_count, in_blocks = cur_ref.shape[0], msg_ref.shape[0]
    block = msg_ref.shape[2]
    half = cur_ref.shape[1] // 2
    group = parent_ref.shape[0]
    firsts = [
        pltpu.make_async_copy(src, dst, sem.at[leaf_count + n])
        for n, (src, dst) in enumerate(
            ((parent_hbm, parent_ref), (shift_hbm, shift_ref), (cur_hbm, cur_ref))
        )
    ]
    for copy in firsts:
        copy.start()
    copies = [
        pltpu.make_async_copy(rad_hbm.at[leaf], rad_ref.at[leaf], sem.at[leaf])
        for leaf in range(leaf_count)
    ]
    for copy in copies:
        copy.start()
    later = [
        pltpu.make_async_copy(src, dst, sem.at[leaf_count + 3 + n])
        for n, (src, dst) in enumerate(
            ((trans_hbm, trans_ref), (phase_hbm, phase_ref))
        )
    ]
    for copy in later:
        copy.start()
    base = leaf_count * 4 * half
    lane = lax.broadcasted_iota(jnp.int32, (8, block), 1)
    line = lax.broadcasted_iota(jnp.int32, (8, block), 0)
    meta = jnp.zeros((8, block), jnp.int32)
    for copy in firsts:
        copy.wait()
    for member in range(group):
        pair = jnp.where(
            line == 0, lax.rem(parent_ref[member], top_count), shift_ref[member]
        )
        meta = jnp.where(lane == member, pair, meta)
    meta = meta.astype(F32)
    zero = jnp.zeros((half, cur_ref.shape[2]), F32)
    left = []
    for leaf in range(leaf_count):
        cur = cur_ref[leaf].astype(F32)
        real, imag = cur[:half], cur[half:]
        pieces = [
            jnp.concatenate(rows, axis=0).astype(BF16)
            for rows in (
                (real, zero, imag, zero),
                (-imag, zero, real, zero),
                (zero, real, zero, imag),
                (zero, -imag, zero, real),
            )
        ]
        left.append(jnp.concatenate(pieces, axis=1))
        row = base + leaf // in_blocks * 4 * half
        msg_ref[leaf % in_blocks, row : row + 4 * half, :] = jnp.concatenate(
            [cur, meta], axis=0
        ).astype(BF16)
    for leaf in range(leaf_count):
        copies[leaf].wait()
        right = jnp.concatenate(
            [rad_ref[leaf, p, r] for p in range(2) for r in range(2)], axis=1
        )
        out = lax.dot_general(left[leaf], right, NT, preferred_element_type=F32).astype(BF16)
        for b in range(in_blocks):
            msg_ref[b, leaf * 4 * half : (leaf + 1) * 4 * half, :] = out[
                :, b * block : (b + 1) * block
            ]
    for copy in later:
        copy.wait()


def lift_groups(refs, dense_ref, shift_ref, top_ref, rows, base, ready):
    left = jnp.concatenate(
        [
            jnp.concatenate([ref[samp, c, :rows, :] for c in range(ref.shape[1])], axis=1)
            for ref in refs
            for samp in range(ref.shape[0])
        ],
        axis=0,
    )
    local_blocks, _, block = top_ref.shape[2:]
    width = min(8, local_blocks)
    for start in range(0, local_blocks, width):
        moved = lax.dot_general(
            left,
            dense_ref[start * block : (start + width) * block, :],
            NT,
            preferred_element_type=F32,
        )
        if start == 0:
            sids = ready()
        for b in range(width):
            for s, sid in enumerate(sids):
                real = moved[s * 16 : s * 16 + 8, b * block : (b + 1) * block]
                imag = moved[s * 16 + 8 : s * 16 + 16, b * block : (b + 1) * block]
                shift_real, shift_imag = shift_ref[sid, start + b], shift_ref[sid + 1, start + b]
                top_ref[base + s, 0, start + b] = real * shift_real - imag * shift_imag
                top_ref[base + s, 1, start + b] = real * shift_imag + imag * shift_real


def spread_rows(src_ref, out_ref):
    count, local_blocks, block = src_ref.shape

    def one(index, carry):
        for b in range(local_blocks):
            out_ref[index, b] = jnp.broadcast_to(src_ref[index, b : b + 1, :], (8, block))
        return carry

    lax.fori_loop(0, count, one, 0)


def tables_kernel(
    idx_ref,
    sid_ref,
    val_hbm,
    near_hbm,
    here_ref,
    shift_ref,
    trans_ref,
    dense_ref,
    wide_shift_ref,
    wide_trans_ref,
    top_ref,
    near_ref,
    val_ref,
    sem,
    *,
    rows,
):
    load = pltpu.make_async_copy(val_hbm, val_ref, sem.at[0])
    load.start()
    other = pltpu.make_async_copy(near_hbm, near_ref, sem.at[1])
    other.start()
    spread_rows(shift_ref, wide_shift_ref)
    spread_rows(trans_ref, wide_trans_ref)
    load.wait()
    local_blocks, _, block, _ = val_ref.shape

    def one(b, carry):
        first, second = idx_ref[0, b], idx_ref[1, b]
        zero = jnp.zeros((block, block), BF16)
        for c in range(dense_ref.shape[1] // block):
            dense_ref[pl.ds(pl.multiple_of(b * block, block), block), c * block : (c + 1) * block] = (
                jnp.where(first == c, val_ref[b, 0], jnp.where(second == c, val_ref[b, 1], zero))
            )
        return carry

    lax.fori_loop(0, local_blocks, one, 0)
    sids = [2 * sid_ref[s] for s in range(sid_ref.shape[0])]
    lift_groups((here_ref,), dense_ref, wide_shift_ref, top_ref, rows, 0, lambda: sids)
    other.wait()


def meta_of(msg_ref, rows):
    return msg_ref[0, 0, rows : rows + 16, :].astype(F32)[8:10]


def field_kernel(
    parent_hbm,
    sid_hbm,
    src_hbm,
    disp_hbm,
    here_ref,
    near_ref,
    far_ref,
    dense_ref,
    shift_ref,
    trans_ref,
    _,
    *rest,
    n_samp,
    leaf_count,
    tile,
):
    outs = rest[:n_samp]
    (
        top_ref,
        parent_ref,
        sid_ref,
        src_ref,
        disp_ref,
        inc_ref,
        down_ref,
        acc_ref,
        meta_ref,
        num_ref,
        head_ref,
        rep_ref,
        count_ref,
        slot_ref,
        coef_ref,
        sem,
    ) = rest[n_samp:]
    block = here_ref.shape[3]
    local_blocks = top_ref.shape[2]
    leaves = top_ref.shape[0]
    group = leaves // 3
    rows = 16 * leaf_count
    top_count, entries = src_ref.shape
    where = lax.axis_index("box")
    me = lax.axis_index("samp")
    turned = jnp.where(me == 1, 1, 0) if n_samp == 2 else jnp.int32(0)
    bases = (1, 2 * turned, 2 - 2 * turned)

    lines = [meta_of(ref, rows) for ref in (here_ref, near_ref, far_ref)]
    meta_ref[...] = jnp.concatenate(lines + lines[:1], axis=0).astype(jnp.int32)
    fetches = [
        pltpu.make_async_copy(src, dst, sem.at[n])
        for n, (src, dst) in enumerate(
            (
                (parent_hbm, parent_ref),
                (sid_hbm, sid_ref),
                (src_hbm, src_ref),
                (disp_hbm, disp_ref),
                (meta_ref, num_ref),
            )
        )
    ]
    for fetch in fetches:
        fetch.start()
    for box in range(3 * top_count):
        head_ref[box] = -1

    def ready():
        for fetch in fetches:
            fetch.wait()
        return [2 * num_ref[line, s] for line in (3, 5) for s in range(group)]

    lift_groups((near_ref, far_ref), dense_ref, shift_ref, top_ref, rows, group, ready)
    boxes = [
        num_ref[2 * (s // group), s % group] + bases[s // group] * top_count for s in range(leaves)
    ]
    for s in reversed(range(leaves)):
        head_ref[boxes[s]] = s
    for s in range(leaves):
        rep_ref[s] = head_ref[boxes[s]]
    for leaf in range(group):
        parent = parent_ref[leaf] - where * top_count
        count = jnp.int32(0)
        slots = [head_ref[src_ref[parent, j] - (where - 1) * top_count] for j in range(entries)]
        coefs = [2 * disp_ref[parent, j] for j in range(entries)]
        for slot, coef in zip(slots, coefs):
            slot_ref[leaf, count] = slot
            coef_ref[leaf, count] = coef
            count += (slot >= 0).astype(jnp.int32)
        count_ref[leaf] = count

    def merge(s, carry):
        rep = rep_ref[s]

        @pl.when(rep != s)
        def _():
            top_ref[rep] = top_ref[rep] + top_ref[s]

        return carry

    lax.fori_loop(0, leaves, merge, 0)

    def target(leaf, carry):
        @pl.when(rep_ref[leaf] == leaf)
        def _():
            for t in range(local_blocks // tile):

                def entry(n, total):
                    slot, coef = slot_ref[leaf, n], coef_ref[leaf, n]
                    real, imag = list(total[:tile]), list(total[tile:])
                    for b in range(tile):
                        place = t * tile + b
                        coef_real, coef_imag = trans_ref[coef, place], trans_ref[coef + 1, place]
                        src_real, src_imag = top_ref[slot, 0, place], top_ref[slot, 1, place]
                        real[b] += coef_real * src_real - coef_imag * src_imag
                        imag[b] += coef_real * src_imag + coef_imag * src_real
                    return tuple(real + imag)

                zero = jnp.zeros((8, block), F32)
                total = lax.fori_loop(0, count_ref[leaf], entry, (zero,) * (2 * tile))
                for b in range(tile):
                    inc_ref[leaf, 0, t * tile + b] = total[b]
                    inc_ref[leaf, 1, t * tile + b] = total[tile + b]

        return carry

    lax.fori_loop(0, group, target, 0)

    def lower(leaf, carry):
        sid = 2 * sid_ref[leaf]
        rep = rep_ref[leaf]
        start = pl.multiple_of(leaf * 16, 16)
        for b in range(local_blocks):
            shift_real, shift_imag = shift_ref[sid, b], shift_ref[sid + 1, b]
            real, imag = inc_ref[rep, 0, b], inc_ref[rep, 1, b]
            down = jnp.concatenate(
                [
                    shift_real * real + shift_imag * imag,
                    shift_real * imag - shift_imag * real,
                ],
                axis=0,
            )
            down_ref[pl.ds(start, 16), b * block : (b + 1) * block] = down.astype(BF16)
        return carry

    lax.fori_loop(0, group, lower, 0)
    acc_ref[...] = jnp.dot(down_ref[...], dense_ref[...], preferred_element_type=F32)
    for d, out in enumerate(outs):
        owner = lax.rem(me + d, n_samp)
        start = pl.multiple_of(owner * rows, rows)
        for c in range(out.shape[0]):
            out[c] = acc_ref[pl.ds(start, rows), c * block : (c + 1) * block].astype(BF16)


def near_kernel(src_ref, near_ref, here_ref, *rest, rows, n_samp):
    other_refs, out_ref, cur_ref = rest[:-2], rest[-2], rest[-1]
    leaf_count, near = near_ref.shape[:2]
    in_blocks = here_ref.shape[1]
    group = n_samp * leaf_count
    where = lax.axis_index("box")
    turned = jnp.where(lax.axis_index("samp") == 1, 1, 0) if n_samp == 2 else jnp.int32(0)
    places = (1, 2 * turned, 2 - 2 * turned)
    for place, ref in zip(places, (here_ref,) + other_refs):
        for leaf in range(group):
            samp, inner = leaf // leaf_count, leaf % leaf_count
            line = rows + inner // in_blocks * 16
            cur = ref[samp, inner % in_blocks, line : line + 16, :].astype(F32)
            cur_ref[place * group + leaf] = jnp.concatenate(
                [cur[:8], -cur[4:8], cur[:4]], axis=0
            ).astype(BF16)
    for leaf in range(leaf_count):
        left = jnp.concatenate(
            [cur_ref[src_ref[leaf, n] - (where - 1) * group] for n in range(near)], axis=1
        )
        out = [
            lax.dot_general(
                left,
                jnp.concatenate([near_ref[leaf, n, r] for n in range(near)], axis=1),
                NT,
                preferred_element_type=F32,
            )
            for r in range(2)
        ]
        out_ref[leaf] = out[0][:8] + out[1][8:]


def receive_kernel(near_ref, rad_ref, *rest):
    far_refs, out_ref = rest[:-1], rest[-1]
    leaf_count = out_ref.shape[0]
    far = far_refs[0][...].astype(F32)
    for ref in far_refs[1:]:
        far = far + ref[...].astype(F32)
    in_blocks = far.shape[0]
    unknowns = rad_ref.shape[4]
    depth = rad_ref.shape[1] * rad_ref.shape[2] * rad_ref.shape[3]
    for leaf in range(leaf_count):
        left = []
        for p in range(2):
            real = [far[b, leaf * 16 + p * 4 : leaf * 16 + p * 4 + 4] for b in range(in_blocks)]
            imag = [
                far[b, leaf * 16 + 8 + p * 4 : leaf * 16 + 12 + p * 4] for b in range(in_blocks)
            ]
            left += [jnp.concatenate(pair, axis=0) for pair in zip(real, imag)]
            left += [jnp.concatenate([i, -r], axis=0) for r, i in zip(real, imag)]
        wide = jnp.concatenate(left, axis=1).astype(BF16)
        right = rad_ref[leaf].reshape(depth, unknowns)
        out_ref[leaf] = near_ref[leaf] + jnp.dot(wide, right, preferred_element_type=F32)


def per_device(
    currents,
    radiation,
    near_blocks,
    near_src,
    leaf_parent,
    leaf_shift,
    shift_table,
    interp_idx,
    interp_val,
    top_src,
    top_disp,
    trans_table,
):
    n_samp = lax.axis_size("samp")
    n_box = lax.axis_size("box")
    leaf_count, comps, unknowns = currents.shape
    group = leaf_parent.shape[0]
    top_count, entries = top_src.shape
    local_blocks, _, block, _ = interp_val.shape
    in_blocks = radiation.shape[3] // block
    leaves = 3 * group
    rows = 16 * leaf_count
    extra = 16 * -(-leaf_count // in_blocks)
    tile = min(16, local_blocks)

    message, phases, moves = pl.pallas_call(
        functools.partial(radiate_kernel, top_count=top_count),
        out_shape=[
            jax.ShapeDtypeStruct((in_blocks, rows + extra, block), BF16),
            pltpu.VMEM(shift_table.shape, BF16),
            pltpu.VMEM(trans_table.shape, BF16),
        ],
        in_specs=[HBM] * 6,
        out_specs=[VMEM] * 3,
        scratch_shapes=[
            pltpu.SMEM(leaf_parent.shape, jnp.int32),
            pltpu.SMEM(leaf_shift.shape, jnp.int32),
            pltpu.VMEM(currents.shape, BF16),
            pltpu.VMEM(radiation.shape, BF16),
            pltpu.SemaphoreType.DMA((leaf_count + 5,)),
        ],
        compiler_params=params(),
        name="radiate",
    )(
        *pinned(
            leaf_parent, leaf_shift, currents, radiation, shift_table, trans_table
        )
    )

    here = lax.all_gather(message, "samp", axis=0)
    last = n_samp - 1
    swap = []
    for box in range(n_box - 1):
        low, high = box * n_samp + last, (box + 1) * n_samp
        swap += [(low, high), (high, low)]
    beyond = lax.ppermute(here, ("box", "samp"), swap)
    shift_rows = phases.astype(F32).reshape(-1, local_blocks, block)
    trans_rows = moves.astype(F32).reshape(-1, local_blocks, block)
    work = 2 * leaves * 16 * in_blocks * block * local_blocks * block
    top_shape = pltpu.VMEM((leaves, 2, local_blocks, 8, block), F32)
    dense, wide_shift, wide_trans, own_top, near_values = pl.pallas_call(
        functools.partial(tables_kernel, rows=rows),
        out_shape=[
            pltpu.VMEM((local_blocks * block, in_blocks * block), BF16),
            pltpu.VMEM((shift_rows.shape[0], local_blocks, 8, block), F32),
            pltpu.VMEM((trans_rows.shape[0], local_blocks, 8, block), F32),
            top_shape,
            pltpu.VMEM(near_blocks.shape, BF16),
        ],
        in_specs=[SMEM, SMEM, HBM, HBM] + [VMEM] * 3,
        out_specs=[VMEM] * 5,
        scratch_shapes=[pltpu.VMEM(interp_val.shape, BF16), pltpu.SemaphoreType.DMA((2,))],
        compiler_params=params(),
        cost_estimate=pl.CostEstimate(flops=work, bytes_accessed=1 << 24, transcendentals=0),
        name="tables",
    )(interp_idx.T, leaf_shift, *pinned(interp_val, near_blocks), here, shift_rows, trans_rows)
    beyond, dense = lax.optimization_barrier((beyond, dense))
    if n_samp == 2:
        first = beyond
        second = lax.ppermute(beyond, "samp", [(0, 1), (1, 0)])
    else:
        ends = lax.all_gather(beyond, "samp", axis=0)
        first, second = ends[0], ends[n_samp - 1]
    numbers = [pltpu.VMEM((8, block), jnp.int32), pltpu.SMEM((8, block), jnp.int32)]
    sources = (here, first) if n_samp == 2 else (here, first, second)
    near_out = pl.pallas_call(
        functools.partial(near_kernel, rows=rows, n_samp=n_samp),
        out_shape=jax.ShapeDtypeStruct((leaf_count, comps, unknowns), F32),
        in_specs=[SMEM] + [VMEM] * (1 + len(sources)),
        out_specs=VMEM,
        scratch_shapes=[pltpu.VMEM((leaves, 16, block), BF16)],
        compiler_params=params(),
        cost_estimate=pl.CostEstimate(flops=work, bytes_accessed=1 << 22, transcendentals=0),
        name="near",
    )(near_src, near_values, *sources)
    second, near_out = lax.optimization_barrier((second, near_out))

    *fars, _ = pl.pallas_call(
        functools.partial(field_kernel, n_samp=n_samp, leaf_count=leaf_count, tile=tile),
        out_shape=[jax.ShapeDtypeStruct((in_blocks, rows, block), BF16)] * n_samp
        + [top_shape],
        in_specs=[HBM] * 4 + [VMEM] * 7,
        out_specs=[VMEM] * (n_samp + 1),
        scratch_shapes=[
            pltpu.SMEM(leaf_parent.shape, jnp.int32),
            pltpu.SMEM(leaf_shift.shape, jnp.int32),
            pltpu.SMEM(top_src.shape, jnp.int32),
            pltpu.SMEM(top_disp.shape, jnp.int32),
            pltpu.VMEM((group, 2, local_blocks, 8, block), F32),
            pltpu.VMEM((group * 16, local_blocks * block), BF16),
            pltpu.VMEM((group * 16, in_blocks * block), F32),
            *numbers,
            pltpu.SMEM((3 * top_count,), jnp.int32),
            pltpu.SMEM((leaves,), jnp.int32),
            pltpu.SMEM((group,), jnp.int32),
            pltpu.SMEM((group, entries), jnp.int32),
            pltpu.SMEM((group, entries), jnp.int32),
            pltpu.SemaphoreType.DMA((5,)),
        ],
        input_output_aliases={10: n_samp},
        compiler_params=params(),
        name="field",
    )(
        *pinned(leaf_parent, leaf_shift, top_src, top_disp),
        here,
        first,
        second,
        dense,
        wide_shift,
        wide_trans,
        own_top,
    )
    received = [fars[0]] + [
        lax.ppermute(fars[d], "samp", [(i, (i + d) % n_samp) for i in range(n_samp)])
        for d in range(1, n_samp)
    ]
    return pl.pallas_call(
        receive_kernel,
        out_shape=jax.ShapeDtypeStruct((leaf_count, comps, unknowns), F32),
        in_specs=[VMEM] * (2 + n_samp),
        out_specs=VMEM,
        compiler_params=params(),
        name="receive",
    )(near_out, radiation, *received)


def solution(mesh):
    placed = (
        P(("box", "samp"), None, None),
        P(("box", "samp"), None, None, None, None),
        P(("box", "samp"), None, None, None, None),
        P(("box", "samp"), None),
        P("box"),
        P("box"),
        P(None, None, "samp"),
        P("samp", None),
        P("samp", None, None, None),
        P("box", None),
        P("box", None),
        P(None, None, "samp"),
    )
    return jax.shard_map(
        per_device,
        mesh=mesh,
        in_specs=placed,
        out_specs=P(("box", "samp"), None, None),
        check_vma=False,
    )
```

```python
import functools

import jax
import jax.numpy as jnp
from jax import lax
from jax.experimental import pallas as pl
from jax.experimental.pallas import tpu as pltpu
from jax.sharding import PartitionSpec as P

F32 = jnp.float32
BF16 = jnp.bfloat16
HBM = pl.BlockSpec(memory_space=pltpu.HBM)
VMEM = pl.BlockSpec(memory_space=pltpu.VMEM)
SMEM = pl.BlockSpec(memory_space=pltpu.SMEM)
NT = (((1,), (1,)), ((), ()))
LIMIT = 14 * 1024 * 1024


def params():
    return pltpu.CompilerParams(vmem_limit_bytes=LIMIT)


def pinned(*arrays):
    return [pltpu.with_memory_space_constraint(array, pltpu.HBM) for array in arrays]


def radiate_kernel(
    parent_hbm,
    shift_hbm,
    cur_hbm,
    rad_hbm,
    phase_hbm,
    trans_hbm,
    msg_ref,
    phase_ref,
    trans_ref,
    parent_ref,
    shift_ref,
    cur_ref,
    rad_ref,
    sem,
    *,
    top_count,
):
    leaf_count, in_blocks = cur_ref.shape[0], msg_ref.shape[0]
    block = msg_ref.shape[2]
    half = cur_ref.shape[1] // 2
    group = parent_ref.shape[0]
    firsts = [
        pltpu.make_async_copy(src, dst, sem.at[leaf_count + n])
        for n, (src, dst) in enumerate(
            ((parent_hbm, parent_ref), (shift_hbm, shift_ref), (cur_hbm, cur_ref))
        )
    ]
    for copy in firsts:
        copy.start()
    copies = [
        pltpu.make_async_copy(rad_hbm.at[leaf], rad_ref.at[leaf], sem.at[leaf])
        for leaf in range(leaf_count)
    ]
    for copy in copies:
        copy.start()
    later = [
        pltpu.make_async_copy(src, dst, sem.at[leaf_count + 3 + n])
        for n, (src, dst) in enumerate(
            ((trans_hbm, trans_ref), (phase_hbm, phase_ref))
        )
    ]
    for copy in later:
        copy.start()
    base = leaf_count * 4 * half
    lane = lax.broadcasted_iota(jnp.int32, (8, block), 1)
    line = lax.broadcasted_iota(jnp.int32, (8, block), 0)
    meta = jnp.zeros((8, block), jnp.int32)
    for copy in firsts:
        copy.wait()
    for member in range(group):
        pair = jnp.where(
            line == 0, lax.rem(parent_ref[member], top_count), shift_ref[member]
        )
        meta = jnp.where(lane == member, pair, meta)
    meta = meta.astype(F32)
    zero = jnp.zeros((half, cur_ref.shape[2]), F32)
    left = []
    for leaf in range(leaf_count):
        cur = cur_ref[leaf].astype(F32)
        real, imag = cur[:half], cur[half:]
        pieces = [
            jnp.concatenate(rows, axis=0).astype(BF16)
            for rows in (
                (real, zero, imag, zero),
                (-imag, zero, real, zero),
                (zero, real, zero, imag),
                (zero, -imag, zero, real),
            )
        ]
        left.append(jnp.concatenate(pieces, axis=1))
        row = base + leaf // in_blocks * 4 * half
        msg_ref[leaf % in_blocks, row : row + 4 * half, :] = jnp.concatenate(
            [cur, meta], axis=0
        ).astype(BF16)
    for leaf in range(leaf_count):
        copies[leaf].wait()
        right = jnp.concatenate(
            [rad_ref[leaf, p, r] for p in range(2) for r in range(2)], axis=1
        )
        out = lax.dot_general(left[leaf], right, NT, preferred_element_type=F32).astype(BF16)
        for b in range(in_blocks):
            msg_ref[b, leaf * 4 * half : (leaf + 1) * 4 * half, :] = out[
                :, b * block : (b + 1) * block
            ]
    for copy in later:
        copy.wait()


def lift_groups(refs, dense_ref, shift_ref, top_ref, rows, base, ready):
    left = jnp.concatenate(
        [
            jnp.concatenate([ref[samp, c, :rows, :] for c in range(ref.shape[1])], axis=1)
            for ref in refs
            for samp in range(ref.shape[0])
        ],
        axis=0,
    )
    local_blocks, _, block = top_ref.shape[2:]
    width = min(8, local_blocks)
    for start in range(0, local_blocks, width):
        moved = lax.dot_general(
            left,
            dense_ref[start * block : (start + width) * block, :],
            NT,
            preferred_element_type=F32,
        )
        if start == 0:
            sids = ready()
        for b in range(width):
            for s, sid in enumerate(sids):
                real = moved[s * 16 : s * 16 + 8, b * block : (b + 1) * block]
                imag = moved[s * 16 + 8 : s * 16 + 16, b * block : (b + 1) * block]
                shift_real, shift_imag = shift_ref[sid, start + b], shift_ref[sid + 1, start + b]
                top_ref[base + s, 0, start + b] = real * shift_real - imag * shift_imag
                top_ref[base + s, 1, start + b] = real * shift_imag + imag * shift_real


def spread_rows(src_ref, out_ref):
    count, local_blocks, block = src_ref.shape

    def one(index, carry):
        for b in range(local_blocks):
            out_ref[index, b] = jnp.broadcast_to(src_ref[index, b : b + 1, :], (8, block))
        return carry

    lax.fori_loop(0, count, one, 0)


def tables_kernel(
    idx_ref,
    sid_ref,
    val_hbm,
    near_hbm,
    here_ref,
    shift_ref,
    trans_ref,
    dense_ref,
    wide_shift_ref,
    wide_trans_ref,
    top_ref,
    near_ref,
    val_ref,
    sem,
    *,
    rows,
):
    load = pltpu.make_async_copy(val_hbm, val_ref, sem.at[0])
    load.start()
    other = pltpu.make_async_copy(near_hbm, near_ref, sem.at[1])
    other.start()
    spread_rows(shift_ref, wide_shift_ref)
    spread_rows(trans_ref, wide_trans_ref)
    last = trans_ref.shape[0]
    wide_trans_ref[last:] = jnp.zeros((2, *wide_trans_ref.shape[1:]), F32)
    load.wait()
    local_blocks, _, block, _ = val_ref.shape

    def one(b, carry):
        first, second = idx_ref[0, b], idx_ref[1, b]
        zero = jnp.zeros((block, block), BF16)
        for c in range(dense_ref.shape[1] // block):
            dense_ref[pl.ds(pl.multiple_of(b * block, block), block), c * block : (c + 1) * block] = (
                jnp.where(first == c, val_ref[b, 0], jnp.where(second == c, val_ref[b, 1], zero))
            )
        return carry

    lax.fori_loop(0, local_blocks, one, 0)
    sids = [2 * sid_ref[s] for s in range(sid_ref.shape[0])]
    lift_groups((here_ref,), dense_ref, wide_shift_ref, top_ref, rows, 0, lambda: sids)
    other.wait()


def meta_of(msg_ref, rows):
    return msg_ref[0, 0, rows : rows + 16, :].astype(F32)[8:10]


def field_kernel(
    parent_hbm,
    sid_hbm,
    src_hbm,
    disp_hbm,
    here_ref,
    near_ref,
    far_ref,
    dense_ref,
    shift_ref,
    trans_ref,
    _,
    *rest,
    n_samp,
    leaf_count,
    tile,
):
    outs = rest[:n_samp]
    (
        top_ref,
        parent_ref,
        sid_ref,
        src_ref,
        disp_ref,
        inc_ref,
        down_ref,
        acc_ref,
        meta_ref,
        num_ref,
        head_ref,
        rep_ref,
        count_ref,
        slot_ref,
        coef_ref,
        sem,
    ) = rest[n_samp:]
    block = here_ref.shape[3]
    local_blocks = top_ref.shape[2]
    leaves = top_ref.shape[0]
    group = leaves // 3
    rows = 16 * leaf_count
    top_count, entries = src_ref.shape
    where = lax.axis_index("box")
    me = lax.axis_index("samp")
    turned = jnp.where(me == 1, 1, 0) if n_samp == 2 else jnp.int32(0)
    bases = (1, 2 * turned, 2 - 2 * turned)

    lines = [meta_of(ref, rows) for ref in (here_ref, near_ref, far_ref)]
    meta_ref[...] = jnp.concatenate(lines + lines[:1], axis=0).astype(jnp.int32)
    fetches = [
        pltpu.make_async_copy(src, dst, sem.at[n])
        for n, (src, dst) in enumerate(
            (
                (parent_hbm, parent_ref),
                (sid_hbm, sid_ref),
                (src_hbm, src_ref),
                (disp_hbm, disp_ref),
                (meta_ref, num_ref),
            )
        )
    ]
    for fetch in fetches:
        fetch.start()
    for box in range(3 * top_count):
        head_ref[box] = -1

    def ready():
        for fetch in fetches:
            fetch.wait()
        return [2 * num_ref[line, s] for line in (3, 5) for s in range(group)]

    lift_groups((near_ref, far_ref), dense_ref, shift_ref, top_ref, rows, group, ready)
    boxes = [
        num_ref[2 * (s // group), s % group] + bases[s // group] * top_count for s in range(leaves)
    ]
    for s in reversed(range(leaves)):
        head_ref[boxes[s]] = s
    for s in range(leaves):
        rep_ref[s] = head_ref[boxes[s]]
    for leaf in range(group):
        parent = parent_ref[leaf] - where * top_count
        count = jnp.int32(0)
        slots = [head_ref[src_ref[parent, j] - (where - 1) * top_count] for j in range(entries)]
        coefs = [2 * disp_ref[parent, j] for j in range(entries)]
        for slot, coef in zip(slots, coefs):
            slot_ref[leaf, count] = slot
            coef_ref[leaf, count] = coef
            count += (slot >= 0).astype(jnp.int32)
        slot_ref[leaf, count] = 0
        coef_ref[leaf, count] = trans_ref.shape[0] - 2
        count_ref[leaf] = lax.div(count + 1, 2)

    def merge(s, carry):
        rep = rep_ref[s]

        @pl.when(rep != s)
        def _():
            top_ref[rep] = top_ref[rep] + top_ref[s]

        return carry

    lax.fori_loop(0, leaves, merge, 0)

    def store_down(leaf, b, real, imag):
        sid = 2 * sid_ref[leaf]
        shift_real, shift_imag = shift_ref[sid, b], shift_ref[sid + 1, b]
        down = jnp.concatenate(
            [
                shift_real * real + shift_imag * imag,
                shift_real * imag - shift_imag * real,
            ],
            axis=0,
        )
        start = pl.multiple_of(leaf * 16, 16)
        down_ref[pl.ds(start, 16), b * block : (b + 1) * block] = down.astype(BF16)

    def target(leaf, carry):
        @pl.when(rep_ref[leaf] == leaf)
        def _():
            for t in range(0, local_blocks, tile):

                def entries_of(n, total):
                    real, imag = list(total[:tile]), list(total[tile:])
                    pair = [
                        (slot_ref[leaf, 2 * n + m], coef_ref[leaf, 2 * n + m]) for m in range(2)
                    ]
                    for b in range(tile):
                        place = t + b
                        for slot, coef in pair:
                            move_real, move_imag = trans_ref[coef, place], trans_ref[coef + 1, place]
                            src_real, src_imag = top_ref[slot, 0, place], top_ref[slot, 1, place]
                            real[b] += move_real * src_real - move_imag * src_imag
                            imag[b] += move_real * src_imag + move_imag * src_real
                    return tuple(real + imag)

                zero = jnp.zeros((8, block), F32)
                total = lax.fori_loop(0, count_ref[leaf], entries_of, (zero,) * (2 * tile))
                for b in range(tile):
                    inc_ref[leaf, 0, t + b] = total[b]
                    inc_ref[leaf, 1, t + b] = total[tile + b]
                    store_down(leaf, t + b, total[b], total[tile + b])

        return carry

    lax.fori_loop(0, group, target, 0)

    def lower(leaf, carry):
        rep = rep_ref[leaf]

        @pl.when(rep != leaf)
        def _():
            for b in range(local_blocks):
                store_down(leaf, b, inc_ref[rep, 0, b], inc_ref[rep, 1, b])

        return carry

    lax.fori_loop(0, group, lower, 0)
    acc_ref[...] = jnp.dot(down_ref[...], dense_ref[...], preferred_element_type=F32)
    for d, out in enumerate(outs):
        owner = lax.rem(me + d, n_samp)
        start = pl.multiple_of(owner * rows, rows)
        for c in range(out.shape[0]):
            out[c] = acc_ref[pl.ds(start, rows), c * block : (c + 1) * block].astype(BF16)


def near_kernel(src_ref, near_ref, here_ref, *rest, rows, n_samp):
    other_refs, out_ref, cur_ref = rest[:-2], rest[-2], rest[-1]
    leaf_count, near = near_ref.shape[:2]
    in_blocks = here_ref.shape[1]
    group = n_samp * leaf_count
    where = lax.axis_index("box")
    turned = jnp.where(lax.axis_index("samp") == 1, 1, 0) if n_samp == 2 else jnp.int32(0)
    places = (1, 2 * turned, 2 - 2 * turned)
    for place, ref in zip(places, (here_ref,) + other_refs):
        for leaf in range(group):
            samp, inner = leaf // leaf_count, leaf % leaf_count
            line = rows + inner // in_blocks * 16
            cur = ref[samp, inner % in_blocks, line : line + 16, :].astype(F32)
            cur_ref[place * group + leaf] = jnp.concatenate(
                [cur[:8], -cur[4:8], cur[:4]], axis=0
            ).astype(BF16)
    for leaf in range(leaf_count):
        left = jnp.concatenate(
            [cur_ref[src_ref[leaf, n] - (where - 1) * group] for n in range(near)], axis=1
        )
        out = [
            lax.dot_general(
                left,
                jnp.concatenate([near_ref[leaf, n, r] for n in range(near)], axis=1),
                NT,
                preferred_element_type=F32,
            )
            for r in range(2)
        ]
        out_ref[leaf] = out[0][:8] + out[1][8:]


def receive_kernel(near_ref, rad_ref, *rest):
    far_refs, out_ref = rest[:-1], rest[-1]
    leaf_count = out_ref.shape[0]
    far = far_refs[0][...].astype(F32)
    for ref in far_refs[1:]:
        far = far + ref[...].astype(F32)
    in_blocks = far.shape[0]
    unknowns = rad_ref.shape[4]
    depth = rad_ref.shape[1] * rad_ref.shape[2] * rad_ref.shape[3]
    for leaf in range(leaf_count):
        left = []
        for p in range(2):
            real = [far[b, leaf * 16 + p * 4 : leaf * 16 + p * 4 + 4] for b in range(in_blocks)]
            imag = [
                far[b, leaf * 16 + 8 + p * 4 : leaf * 16 + 12 + p * 4] for b in range(in_blocks)
            ]
            left += [jnp.concatenate(pair, axis=0) for pair in zip(real, imag)]
            left += [jnp.concatenate([i, -r], axis=0) for r, i in zip(real, imag)]
        wide = jnp.concatenate(left, axis=1).astype(BF16)
        right = rad_ref[leaf].reshape(depth, unknowns)
        out_ref[leaf] = near_ref[leaf] + jnp.dot(wide, right, preferred_element_type=F32)


def per_device(
    currents,
    radiation,
    near_blocks,
    near_src,
    leaf_parent,
    leaf_shift,
    shift_table,
    interp_idx,
    interp_val,
    top_src,
    top_disp,
    trans_table,
):
    n_samp = lax.axis_size("samp")
    n_box = lax.axis_size("box")
    leaf_count, comps, unknowns = currents.shape
    group = leaf_parent.shape[0]
    top_count, entries = top_src.shape
    local_blocks, _, block, _ = interp_val.shape
    in_blocks = radiation.shape[3] // block
    leaves = 3 * group
    rows = 16 * leaf_count
    extra = 16 * -(-leaf_count // in_blocks)
    tile = min(16, local_blocks)

    message, phases, moves = pl.pallas_call(
        functools.partial(radiate_kernel, top_count=top_count),
        out_shape=[
            jax.ShapeDtypeStruct((in_blocks, rows + extra, block), BF16),
            pltpu.VMEM(shift_table.shape, BF16),
            pltpu.VMEM(trans_table.shape, BF16),
        ],
        in_specs=[HBM] * 6,
        out_specs=[VMEM] * 3,
        scratch_shapes=[
            pltpu.SMEM(leaf_parent.shape, jnp.int32),
            pltpu.SMEM(leaf_shift.shape, jnp.int32),
            pltpu.VMEM(currents.shape, BF16),
            pltpu.VMEM(radiation.shape, BF16),
            pltpu.SemaphoreType.DMA((leaf_count + 5,)),
        ],
        compiler_params=params(),
        name="radiate",
    )(
        *pinned(
            leaf_parent, leaf_shift, currents, radiation, shift_table, trans_table
        )
    )

    here = lax.all_gather(message, "samp", axis=0)
    last = n_samp - 1
    swap = []
    for box in range(n_box - 1):
        low, high = box * n_samp + last, (box + 1) * n_samp
        swap += [(low, high), (high, low)]
    beyond = lax.ppermute(here, ("box", "samp"), swap)
    shift_rows = phases.astype(F32).reshape(-1, local_blocks, block)
    trans_rows = moves.astype(F32).reshape(-1, local_blocks, block)
    work = 2 * leaves * 16 * in_blocks * block * local_blocks * block
    top_shape = pltpu.VMEM((leaves, 2, local_blocks, 8, block), F32)
    dense, wide_shift, wide_trans, own_top, near_values = pl.pallas_call(
        functools.partial(tables_kernel, rows=rows),
        out_shape=[
            pltpu.VMEM((local_blocks * block, in_blocks * block), BF16),
            pltpu.VMEM((shift_rows.shape[0], local_blocks, 8, block), F32),
            pltpu.VMEM((trans_rows.shape[0] + 2, local_blocks, 8, block), F32),
            top_shape,
            pltpu.VMEM(near_blocks.shape, BF16),
        ],
        in_specs=[SMEM, SMEM, HBM, HBM] + [VMEM] * 3,
        out_specs=[VMEM] * 5,
        scratch_shapes=[pltpu.VMEM(interp_val.shape, BF16), pltpu.SemaphoreType.DMA((2,))],
        compiler_params=params(),
        cost_estimate=pl.CostEstimate(flops=work, bytes_accessed=1 << 24, transcendentals=0),
        name="tables",
    )(interp_idx.T, leaf_shift, *pinned(interp_val, near_blocks), here, shift_rows, trans_rows)
    beyond, dense = lax.optimization_barrier((beyond, dense))
    if n_samp == 2:
        first = beyond
        second = lax.ppermute(beyond, "samp", [(0, 1), (1, 0)])
    else:
        ends = lax.all_gather(beyond, "samp", axis=0)
        first, second = ends[0], ends[n_samp - 1]
    numbers = [pltpu.VMEM((8, block), jnp.int32), pltpu.SMEM((8, block), jnp.int32)]
    sources = (here, first) if n_samp == 2 else (here, first, second)
    near_out = pl.pallas_call(
        functools.partial(near_kernel, rows=rows, n_samp=n_samp),
        out_shape=jax.ShapeDtypeStruct((leaf_count, comps, unknowns), F32),
        in_specs=[SMEM] + [VMEM] * (1 + len(sources)),
        out_specs=VMEM,
        scratch_shapes=[pltpu.VMEM((leaves, 16, block), BF16)],
        compiler_params=params(),
        cost_estimate=pl.CostEstimate(flops=work, bytes_accessed=1 << 22, transcendentals=0),
        name="near",
    )(near_src, near_values, *sources)
    second, near_out = lax.optimization_barrier((second, near_out))

    *fars, _ = pl.pallas_call(
        functools.partial(field_kernel, n_samp=n_samp, leaf_count=leaf_count, tile=tile),
        out_shape=[jax.ShapeDtypeStruct((in_blocks, rows, block), BF16)] * n_samp
        + [top_shape],
        in_specs=[HBM] * 4 + [VMEM] * 7,
        out_specs=[VMEM] * (n_samp + 1),
        scratch_shapes=[
            pltpu.SMEM(leaf_parent.shape, jnp.int32),
            pltpu.SMEM(leaf_shift.shape, jnp.int32),
            pltpu.SMEM(top_src.shape, jnp.int32),
            pltpu.SMEM(top_disp.shape, jnp.int32),
            pltpu.VMEM((group, 2, local_blocks, 8, block), F32),
            pltpu.VMEM((group * 16, local_blocks * block), BF16),
            pltpu.VMEM((group * 16, in_blocks * block), F32),
            *numbers,
            pltpu.SMEM((3 * top_count,), jnp.int32),
            pltpu.SMEM((leaves,), jnp.int32),
            pltpu.SMEM((group,), jnp.int32),
            pltpu.SMEM((group, entries + 1), jnp.int32),
            pltpu.SMEM((group, entries + 1), jnp.int32),
            pltpu.SemaphoreType.DMA((5,)),
        ],
        input_output_aliases={10: n_samp},
        compiler_params=params(),
        name="field",
    )(
        *pinned(leaf_parent, leaf_shift, top_src, top_disp),
        here,
        first,
        second,
        dense,
        wide_shift,
        wide_trans,
        own_top,
    )
    received = [fars[0]] + [
        lax.ppermute(fars[d], "samp", [(i, (i + d) % n_samp) for i in range(n_samp)])
        for d in range(1, n_samp)
    ]
    return pl.pallas_call(
        receive_kernel,
        out_shape=jax.ShapeDtypeStruct((leaf_count, comps, unknowns), F32),
        in_specs=[VMEM] * (2 + n_samp),
        out_specs=VMEM,
        compiler_params=params(),
        name="receive",
    )(near_out, radiation, *received)


def solution(mesh):
    placed = (
        P(("box", "samp"), None, None),
        P(("box", "samp"), None, None, None, None),
        P(("box", "samp"), None, None, None, None),
        P(("box", "samp"), None),
        P("box"),
        P("box"),
        P(None, None, "samp"),
        P("samp", None),
        P("samp", None, None, None),
        P("box", None),
        P("box", None),
        P(None, None, "samp"),
    )
    return jax.shard_map(
        per_device,
        mesh=mesh,
        in_specs=placed,
        out_specs=P(("box", "samp"), None, None),
        check_vma=False,
    )
```

```python
import functools

import jax
import jax.numpy as jnp
from jax import lax
from jax.experimental import pallas as pl
from jax.experimental.pallas import tpu as pltpu
from jax.sharding import PartitionSpec as P

F32 = jnp.float32
BF16 = jnp.bfloat16
HBM = pl.BlockSpec(memory_space=pltpu.HBM)
VMEM = pl.BlockSpec(memory_space=pltpu.VMEM)
SMEM = pl.BlockSpec(memory_space=pltpu.SMEM)
NT = (((1,), (1,)), ((), ()))
LIMIT = 14 * 1024 * 1024


def params():
    return pltpu.CompilerParams(vmem_limit_bytes=LIMIT)


def pinned(*arrays):
    return [pltpu.with_memory_space_constraint(array, pltpu.HBM) for array in arrays]


def radiate_kernel(
    parent_hbm,
    shift_hbm,
    cur_hbm,
    rad_hbm,
    phase_hbm,
    trans_hbm,
    msg_ref,
    phase_ref,
    trans_ref,
    parent_ref,
    shift_ref,
    cur_ref,
    rad_ref,
    sem,
    *,
    top_count,
):
    leaf_count, in_blocks = cur_ref.shape[0], msg_ref.shape[0]
    block = msg_ref.shape[2]
    half = cur_ref.shape[1] // 2
    group = parent_ref.shape[0]
    firsts = [
        pltpu.make_async_copy(src, dst, sem.at[leaf_count + n])
        for n, (src, dst) in enumerate(
            ((parent_hbm, parent_ref), (shift_hbm, shift_ref), (cur_hbm, cur_ref))
        )
    ]
    for copy in firsts:
        copy.start()
    copies = [
        pltpu.make_async_copy(rad_hbm.at[leaf], rad_ref.at[leaf], sem.at[leaf])
        for leaf in range(leaf_count)
    ]
    for copy in copies:
        copy.start()
    later = [
        pltpu.make_async_copy(src, dst, sem.at[leaf_count + 3 + n])
        for n, (src, dst) in enumerate(
            ((trans_hbm, trans_ref), (phase_hbm, phase_ref))
        )
    ]
    for copy in later:
        copy.start()
    base = leaf_count * 4 * half
    lane = lax.broadcasted_iota(jnp.int32, (8, block), 1)
    line = lax.broadcasted_iota(jnp.int32, (8, block), 0)
    meta = jnp.zeros((8, block), jnp.int32)
    for copy in firsts:
        copy.wait()
    for member in range(group):
        pair = jnp.where(
            line == 0, lax.rem(parent_ref[member], top_count), shift_ref[member]
        )
        meta = jnp.where(lane == member, pair, meta)
    meta = meta.astype(F32)
    zero = jnp.zeros((half, cur_ref.shape[2]), F32)
    left = []
    for leaf in range(leaf_count):
        cur = cur_ref[leaf].astype(F32)
        real, imag = cur[:half], cur[half:]
        pieces = [
            jnp.concatenate(rows, axis=0).astype(BF16)
            for rows in (
                (real, zero, imag, zero),
                (-imag, zero, real, zero),
                (zero, real, zero, imag),
                (zero, -imag, zero, real),
            )
        ]
        left.append(jnp.concatenate(pieces, axis=1))
        row = base + leaf // in_blocks * 4 * half
        msg_ref[leaf % in_blocks, row : row + 4 * half, :] = jnp.concatenate(
            [cur, meta], axis=0
        ).astype(BF16)
    for leaf in range(leaf_count):
        copies[leaf].wait()
        right = jnp.concatenate(
            [rad_ref[leaf, p, r] for p in range(2) for r in range(2)], axis=1
        )
        out = lax.dot_general(left[leaf], right, NT, preferred_element_type=F32).astype(BF16)
        for b in range(in_blocks):
            msg_ref[b, leaf * 4 * half : (leaf + 1) * 4 * half, :] = out[
                :, b * block : (b + 1) * block
            ]
    for copy in later:
        copy.wait()


def lift_groups(refs, dense_ref, shift_ref, top_ref, rows, base, ready):
    left = jnp.concatenate(
        [
            jnp.concatenate([ref[samp, c, :rows, :] for c in range(ref.shape[1])], axis=1)
            for ref in refs
            for samp in range(ref.shape[0])
        ],
        axis=0,
    )
    local_blocks, _, block = top_ref.shape[2:]
    width = min(4, local_blocks)
    for start in range(0, local_blocks, width):
        moved = lax.dot_general(
            left,
            dense_ref[start * block : (start + width) * block, :],
            NT,
            preferred_element_type=F32,
        )
        if start == 0:
            sids = ready()
        for b in range(width):
            for s, sid in enumerate(sids):
                real = moved[s * 16 : s * 16 + 8, b * block : (b + 1) * block]
                imag = moved[s * 16 + 8 : s * 16 + 16, b * block : (b + 1) * block]
                shift_real, shift_imag = shift_ref[sid, start + b], shift_ref[sid + 1, start + b]
                top_ref[base + s, 0, start + b] = real * shift_real - imag * shift_imag
                top_ref[base + s, 1, start + b] = real * shift_imag + imag * shift_real


def spread_rows(src_ref, out_ref):
    count, local_blocks, block = src_ref.shape

    def one(index, carry):
        for b in range(local_blocks):
            out_ref[index, b] = jnp.broadcast_to(src_ref[index, b : b + 1, :], (8, block))
        return carry

    lax.fori_loop(0, count, one, 0)


def tables_kernel(
    idx_ref,
    sid_ref,
    val_hbm,
    near_hbm,
    here_ref,
    shift_ref,
    trans_ref,
    dense_ref,
    wide_shift_ref,
    wide_trans_ref,
    top_ref,
    near_ref,
    val_ref,
    sem,
    *,
    rows,
):
    load = pltpu.make_async_copy(val_hbm, val_ref, sem.at[0])
    load.start()
    other = pltpu.make_async_copy(near_hbm, near_ref, sem.at[1])
    other.start()
    spread_rows(shift_ref, wide_shift_ref)
    spread_rows(trans_ref, wide_trans_ref)
    last = trans_ref.shape[0]
    wide_trans_ref[last:] = jnp.zeros((2, *wide_trans_ref.shape[1:]), F32)
    load.wait()
    local_blocks, _, block, _ = val_ref.shape

    def one(b, carry):
        first, second = idx_ref[0, b], idx_ref[1, b]
        zero = jnp.zeros((block, block), BF16)
        for c in range(dense_ref.shape[1] // block):
            dense_ref[pl.ds(pl.multiple_of(b * block, block), block), c * block : (c + 1) * block] = (
                jnp.where(first == c, val_ref[b, 0], jnp.where(second == c, val_ref[b, 1], zero))
            )
        return carry

    lax.fori_loop(0, local_blocks, one, 0)
    sids = [2 * sid_ref[s] for s in range(sid_ref.shape[0])]
    lift_groups((here_ref,), dense_ref, wide_shift_ref, top_ref, rows, 0, lambda: sids)
    other.wait()


def meta_of(msg_ref, rows):
    return msg_ref[0, 0, rows : rows + 16, :].astype(F32)[8:10]


def field_kernel(
    parent_hbm,
    sid_hbm,
    src_hbm,
    disp_hbm,
    here_ref,
    near_ref,
    far_ref,
    dense_ref,
    shift_ref,
    trans_ref,
    _,
    *rest,
    n_samp,
    leaf_count,
    tile,
):
    outs = rest[:n_samp]
    (
        top_ref,
        parent_ref,
        sid_ref,
        src_ref,
        disp_ref,
        inc_ref,
        down_ref,
        acc_ref,
        meta_ref,
        num_ref,
        head_ref,
        rep_ref,
        count_ref,
        slot_ref,
        coef_ref,
        sem,
    ) = rest[n_samp:]
    block = here_ref.shape[3]
    local_blocks = top_ref.shape[2]
    leaves = top_ref.shape[0]
    group = leaves // 3
    rows = 16 * leaf_count
    top_count, entries = src_ref.shape
    where = lax.axis_index("box")
    me = lax.axis_index("samp")
    turned = jnp.where(me == 1, 1, 0) if n_samp == 2 else jnp.int32(0)
    bases = (1, 2 * turned, 2 - 2 * turned)

    lines = [meta_of(ref, rows) for ref in (here_ref, near_ref, far_ref)]
    meta_ref[...] = jnp.concatenate(lines + lines[:1], axis=0).astype(jnp.int32)
    fetches = [
        pltpu.make_async_copy(src, dst, sem.at[n])
        for n, (src, dst) in enumerate(
            (
                (parent_hbm, parent_ref),
                (sid_hbm, sid_ref),
                (src_hbm, src_ref),
                (disp_hbm, disp_ref),
                (meta_ref, num_ref),
            )
        )
    ]
    for fetch in fetches:
        fetch.start()
    for box in range(3 * top_count):
        head_ref[box] = -1

    def ready():
        for fetch in fetches:
            fetch.wait()
        return [2 * num_ref[line, s] for line in (3, 5) for s in range(group)]

    lift_groups((near_ref, far_ref), dense_ref, shift_ref, top_ref, rows, group, ready)
    boxes = [
        num_ref[2 * (s // group), s % group] + bases[s // group] * top_count for s in range(leaves)
    ]
    for s in reversed(range(leaves)):
        head_ref[boxes[s]] = s
    for s in range(leaves):
        rep_ref[s] = head_ref[boxes[s]]
    for leaf in range(group):
        parent = parent_ref[leaf] - where * top_count
        count = jnp.int32(0)
        slots = [head_ref[src_ref[parent, j] - (where - 1) * top_count] for j in range(entries)]
        coefs = [2 * disp_ref[parent, j] for j in range(entries)]
        for slot, coef in zip(slots, coefs):
            slot_ref[leaf, count] = slot
            coef_ref[leaf, count] = coef
            count += (slot >= 0).astype(jnp.int32)
        slot_ref[leaf, count] = 0
        coef_ref[leaf, count] = trans_ref.shape[0] - 2
        count_ref[leaf] = lax.div(count + 1, 2)

    def merge(s, carry):
        rep = rep_ref[s]

        @pl.when(rep != s)
        def _():
            top_ref[rep] = top_ref[rep] + top_ref[s]

        return carry

    lax.fori_loop(0, leaves, merge, 0)

    def store_down(leaf, b, real, imag):
        sid = 2 * sid_ref[leaf]
        shift_real, shift_imag = shift_ref[sid, b], shift_ref[sid + 1, b]
        down = jnp.concatenate(
            [
                shift_real * real + shift_imag * imag,
                shift_real * imag - shift_imag * real,
            ],
            axis=0,
        )
        start = pl.multiple_of(leaf * 16, 16)
        down_ref[pl.ds(start, 16), b * block : (b + 1) * block] = down.astype(BF16)

    def target(leaf, carry):
        @pl.when(rep_ref[leaf] == leaf)
        def _():
            for t in range(0, local_blocks, tile):

                def entries_of(n, total):
                    real, imag = list(total[:tile]), list(total[tile:])
                    pair = [
                        (slot_ref[leaf, 2 * n + m], coef_ref[leaf, 2 * n + m]) for m in range(2)
                    ]
                    for b in range(tile):
                        place = t + b
                        for slot, coef in pair:
                            move_real, move_imag = trans_ref[coef, place], trans_ref[coef + 1, place]
                            src_real, src_imag = top_ref[slot, 0, place], top_ref[slot, 1, place]
                            real[b] += move_real * src_real - move_imag * src_imag
                            imag[b] += move_real * src_imag + move_imag * src_real
                    return tuple(real + imag)

                zero = jnp.zeros((8, block), F32)
                total = lax.fori_loop(0, count_ref[leaf], entries_of, (zero,) * (2 * tile))
                for b in range(tile):
                    inc_ref[leaf, 0, t + b] = total[b]
                    inc_ref[leaf, 1, t + b] = total[tile + b]
                    store_down(leaf, t + b, total[b], total[tile + b])

        return carry

    lax.fori_loop(0, group, target, 0)

    def lower(leaf, carry):
        rep = rep_ref[leaf]

        @pl.when(rep != leaf)
        def _():
            for b in range(local_blocks):
                store_down(leaf, b, inc_ref[rep, 0, b], inc_ref[rep, 1, b])

        return carry

    lax.fori_loop(0, group, lower, 0)
    acc_ref[...] = jnp.dot(down_ref[...], dense_ref[...], preferred_element_type=F32)
    for d, out in enumerate(outs):
        owner = lax.rem(me + d, n_samp)
        start = pl.multiple_of(owner * rows, rows)
        for c in range(out.shape[0]):
            out[c] = acc_ref[pl.ds(start, rows), c * block : (c + 1) * block].astype(BF16)


def near_kernel(src_ref, near_ref, here_ref, *rest, rows, n_samp):
    other_refs, out_ref, cur_ref = rest[:-2], rest[-2], rest[-1]
    leaf_count, near = near_ref.shape[:2]
    in_blocks = here_ref.shape[1]
    group = n_samp * leaf_count
    where = lax.axis_index("box")
    turned = jnp.where(lax.axis_index("samp") == 1, 1, 0) if n_samp == 2 else jnp.int32(0)
    places = (1, 2 * turned, 2 - 2 * turned)
    for place, ref in zip(places, (here_ref,) + other_refs):
        for leaf in range(group):
            samp, inner = leaf // leaf_count, leaf % leaf_count
            line = rows + inner // in_blocks * 16
            cur = ref[samp, inner % in_blocks, line : line + 16, :].astype(F32)
            cur_ref[place * group + leaf] = jnp.concatenate(
                [cur[:8], -cur[4:8], cur[:4]], axis=0
            ).astype(BF16)
    for leaf in range(leaf_count):
        left = jnp.concatenate(
            [cur_ref[src_ref[leaf, n] - (where - 1) * group] for n in range(near)], axis=1
        )
        out = [
            lax.dot_general(
                left,
                jnp.concatenate([near_ref[leaf, n, r] for n in range(near)], axis=1),
                NT,
                preferred_element_type=F32,
            )
            for r in range(2)
        ]
        out_ref[leaf] = out[0][:8] + out[1][8:]


def receive_kernel(near_ref, rad_ref, *rest):
    far_refs, out_ref = rest[:-1], rest[-1]
    leaf_count = out_ref.shape[0]
    far = far_refs[0][...].astype(F32)
    for ref in far_refs[1:]:
        far = far + ref[...].astype(F32)
    in_blocks = far.shape[0]
    unknowns = rad_ref.shape[4]
    depth = rad_ref.shape[1] * rad_ref.shape[2] * rad_ref.shape[3]
    for leaf in range(leaf_count):
        left = []
        for p in range(2):
            real = [far[b, leaf * 16 + p * 4 : leaf * 16 + p * 4 + 4] for b in range(in_blocks)]
            imag = [
                far[b, leaf * 16 + 8 + p * 4 : leaf * 16 + 12 + p * 4] for b in range(in_blocks)
            ]
            left += [jnp.concatenate(pair, axis=0) for pair in zip(real, imag)]
            left += [jnp.concatenate([i, -r], axis=0) for r, i in zip(real, imag)]
        wide = jnp.concatenate(left, axis=1).astype(BF16)
        right = rad_ref[leaf].reshape(depth, unknowns)
        out_ref[leaf] = near_ref[leaf] + jnp.dot(wide, right, preferred_element_type=F32)


def per_device(
    currents,
    radiation,
    near_blocks,
    near_src,
    leaf_parent,
    leaf_shift,
    shift_table,
    interp_idx,
    interp_val,
    top_src,
    top_disp,
    trans_table,
):
    n_samp = lax.axis_size("samp")
    n_box = lax.axis_size("box")
    leaf_count, comps, unknowns = currents.shape
    group = leaf_parent.shape[0]
    top_count, entries = top_src.shape
    local_blocks, _, block, _ = interp_val.shape
    in_blocks = radiation.shape[3] // block
    leaves = 3 * group
    rows = 16 * leaf_count
    extra = 16 * -(-leaf_count // in_blocks)
    tile = min(16, local_blocks)

    message, phases, moves = pl.pallas_call(
        functools.partial(radiate_kernel, top_count=top_count),
        out_shape=[
            jax.ShapeDtypeStruct((in_blocks, rows + extra, block), BF16),
            pltpu.VMEM(shift_table.shape, BF16),
            pltpu.VMEM(trans_table.shape, BF16),
        ],
        in_specs=[HBM] * 6,
        out_specs=[VMEM] * 3,
        scratch_shapes=[
            pltpu.SMEM(leaf_parent.shape, jnp.int32),
            pltpu.SMEM(leaf_shift.shape, jnp.int32),
            pltpu.VMEM(currents.shape, BF16),
            pltpu.VMEM(radiation.shape, BF16),
            pltpu.SemaphoreType.DMA((leaf_count + 5,)),
        ],
        compiler_params=params(),
        name="radiate",
    )(
        *pinned(
            leaf_parent, leaf_shift, currents, radiation, shift_table, trans_table
        )
    )

    here = lax.all_gather(message, "samp", axis=0)
    last = n_samp - 1
    swap = []
    for box in range(n_box - 1):
        low, high = box * n_samp + last, (box + 1) * n_samp
        swap += [(low, high), (high, low)]
    beyond = lax.ppermute(here, ("box", "samp"), swap)
    shift_rows = phases.astype(F32).reshape(-1, local_blocks, block)
    trans_rows = moves.astype(F32).reshape(-1, local_blocks, block)
    work = 2 * leaves * 16 * in_blocks * block * local_blocks * block
    top_shape = pltpu.VMEM((leaves, 2, local_blocks, 8, block), F32)
    dense, wide_shift, wide_trans, own_top, near_values = pl.pallas_call(
        functools.partial(tables_kernel, rows=rows),
        out_shape=[
            pltpu.VMEM((local_blocks * block, in_blocks * block), BF16),
            pltpu.VMEM((shift_rows.shape[0], local_blocks, 8, block), F32),
            pltpu.VMEM((trans_rows.shape[0] + 2, local_blocks, 8, block), F32),
            top_shape,
            pltpu.VMEM(near_blocks.shape, BF16),
        ],
        in_specs=[SMEM, SMEM, HBM, HBM] + [VMEM] * 3,
        out_specs=[VMEM] * 5,
        scratch_shapes=[pltpu.VMEM(interp_val.shape, BF16), pltpu.SemaphoreType.DMA((2,))],
        compiler_params=params(),
        cost_estimate=pl.CostEstimate(flops=work, bytes_accessed=1 << 24, transcendentals=0),
        name="tables",
    )(interp_idx.T, leaf_shift, *pinned(interp_val, near_blocks), here, shift_rows, trans_rows)
    beyond, dense = lax.optimization_barrier((beyond, dense))
    if n_samp == 2:
        first = beyond
        second = lax.ppermute(beyond, "samp", [(0, 1), (1, 0)])
    else:
        ends = lax.all_gather(beyond, "samp", axis=0)
        first, second = ends[0], ends[n_samp - 1]
    numbers = [pltpu.VMEM((8, block), jnp.int32), pltpu.SMEM((8, block), jnp.int32)]
    sources = (here, first) if n_samp == 2 else (here, first, second)
    near_out = pl.pallas_call(
        functools.partial(near_kernel, rows=rows, n_samp=n_samp),
        out_shape=jax.ShapeDtypeStruct((leaf_count, comps, unknowns), F32),
        in_specs=[SMEM] + [VMEM] * (1 + len(sources)),
        out_specs=VMEM,
        scratch_shapes=[pltpu.VMEM((leaves, 16, block), BF16)],
        compiler_params=params(),
        cost_estimate=pl.CostEstimate(flops=work, bytes_accessed=1 << 22, transcendentals=0),
        name="near",
    )(near_src, near_values, *sources)
    second, near_out = lax.optimization_barrier((second, near_out))

    *fars, _ = pl.pallas_call(
        functools.partial(field_kernel, n_samp=n_samp, leaf_count=leaf_count, tile=tile),
        out_shape=[jax.ShapeDtypeStruct((in_blocks, rows, block), BF16)] * n_samp
        + [top_shape],
        in_specs=[HBM] * 4 + [VMEM] * 7,
        out_specs=[VMEM] * (n_samp + 1),
        scratch_shapes=[
            pltpu.SMEM(leaf_parent.shape, jnp.int32),
            pltpu.SMEM(leaf_shift.shape, jnp.int32),
            pltpu.SMEM(top_src.shape, jnp.int32),
            pltpu.SMEM(top_disp.shape, jnp.int32),
            pltpu.VMEM((group, 2, local_blocks, 8, block), F32),
            pltpu.VMEM((group * 16, local_blocks * block), BF16),
            pltpu.VMEM((group * 16, in_blocks * block), F32),
            *numbers,
            pltpu.SMEM((3 * top_count,), jnp.int32),
            pltpu.SMEM((leaves,), jnp.int32),
            pltpu.SMEM((group,), jnp.int32),
            pltpu.SMEM((group, entries + 1), jnp.int32),
            pltpu.SMEM((group, entries + 1), jnp.int32),
            pltpu.SemaphoreType.DMA((5,)),
        ],
        input_output_aliases={10: n_samp},
        compiler_params=params(),
        name="field",
    )(
        *pinned(leaf_parent, leaf_shift, top_src, top_disp),
        here,
        first,
        second,
        dense,
        wide_shift,
        wide_trans,
        own_top,
    )
    received = [fars[0]] + [
        lax.ppermute(fars[d], "samp", [(i, (i + d) % n_samp) for i in range(n_samp)])
        for d in range(1, n_samp)
    ]
    return pl.pallas_call(
        receive_kernel,
        out_shape=jax.ShapeDtypeStruct((leaf_count, comps, unknowns), F32),
        in_specs=[VMEM] * (2 + n_samp),
        out_specs=VMEM,
        compiler_params=params(),
        name="receive",
    )(near_out, radiation, *received)


def solution(mesh):
    placed = (
        P(("box", "samp"), None, None),
        P(("box", "samp"), None, None, None, None),
        P(("box", "samp"), None, None, None, None),
        P(("box", "samp"), None),
        P("box"),
        P("box"),
        P(None, None, "samp"),
        P("samp", None),
        P("samp", None, None, None),
        P("box", None),
        P("box", None),
        P(None, None, "samp"),
    )
    return jax.shard_map(
        per_device,
        mesh=mesh,
        in_specs=placed,
        out_specs=P(("box", "samp"), None, None),
        check_vma=False,
    )
```

```python
import functools

import jax
import jax.numpy as jnp
from jax import lax
from jax.experimental import pallas as pl
from jax.experimental.pallas import tpu as pltpu
from jax.sharding import PartitionSpec as P

F32 = jnp.float32
BF16 = jnp.bfloat16
HBM = pl.BlockSpec(memory_space=pltpu.HBM)
VMEM = pl.BlockSpec(memory_space=pltpu.VMEM)
SMEM = pl.BlockSpec(memory_space=pltpu.SMEM)
NT = (((1,), (1,)), ((), ()))
LIMIT = 14 * 1024 * 1024


def params():
    return pltpu.CompilerParams(vmem_limit_bytes=LIMIT)


def pinned(*arrays):
    return [pltpu.with_memory_space_constraint(array, pltpu.HBM) for array in arrays]


def radiate_kernel(
    parent_hbm,
    shift_hbm,
    cur_hbm,
    rad_hbm,
    phase_hbm,
    trans_hbm,
    msg_ref,
    phase_ref,
    trans_ref,
    parent_ref,
    shift_ref,
    cur_ref,
    rad_ref,
    sem,
    *,
    top_count,
):
    leaf_count, in_blocks = cur_ref.shape[0], msg_ref.shape[0]
    block = msg_ref.shape[2]
    half = cur_ref.shape[1] // 2
    group = parent_ref.shape[0]
    firsts = [
        pltpu.make_async_copy(src, dst, sem.at[leaf_count + n])
        for n, (src, dst) in enumerate(
            ((parent_hbm, parent_ref), (shift_hbm, shift_ref), (cur_hbm, cur_ref))
        )
    ]
    for copy in firsts:
        copy.start()
    copies = [
        pltpu.make_async_copy(rad_hbm.at[leaf], rad_ref.at[leaf], sem.at[leaf])
        for leaf in range(leaf_count)
    ]
    for copy in copies:
        copy.start()
    later = [
        pltpu.make_async_copy(src, dst, sem.at[leaf_count + 3 + n])
        for n, (src, dst) in enumerate(
            ((trans_hbm, trans_ref), (phase_hbm, phase_ref))
        )
    ]
    for copy in later:
        copy.start()
    base = leaf_count * 4 * half
    lane = lax.broadcasted_iota(jnp.int32, (8, block), 1)
    line = lax.broadcasted_iota(jnp.int32, (8, block), 0)
    meta = jnp.zeros((8, block), jnp.int32)
    for copy in firsts:
        copy.wait()
    for member in range(group):
        pair = jnp.where(
            line == 0, lax.rem(parent_ref[member], top_count), shift_ref[member]
        )
        meta = jnp.where(lane == member, pair, meta)
    meta = meta.astype(F32)
    zero = jnp.zeros((half, cur_ref.shape[2]), F32)
    left = []
    for leaf in range(leaf_count):
        cur = cur_ref[leaf].astype(F32)
        real, imag = cur[:half], cur[half:]
        pieces = [
            jnp.concatenate(rows, axis=0).astype(BF16)
            for rows in (
                (real, zero, imag, zero),
                (-imag, zero, real, zero),
                (zero, real, zero, imag),
                (zero, -imag, zero, real),
            )
        ]
        left.append(jnp.concatenate(pieces, axis=1))
        row = base + leaf // in_blocks * 4 * half
        msg_ref[leaf % in_blocks, row : row + 4 * half, :] = jnp.concatenate(
            [cur, meta], axis=0
        ).astype(BF16)
    for leaf in range(leaf_count):
        copies[leaf].wait()
        right = jnp.concatenate(
            [rad_ref[leaf, p, r] for p in range(2) for r in range(2)], axis=1
        )
        out = lax.dot_general(left[leaf], right, NT, preferred_element_type=F32).astype(BF16)
        for b in range(in_blocks):
            msg_ref[b, leaf * 4 * half : (leaf + 1) * 4 * half, :] = out[
                :, b * block : (b + 1) * block
            ]
    for copy in later:
        copy.wait()


def lift_groups(refs, dense_ref, shift_ref, top_ref, rows, base, ready):
    left = jnp.concatenate(
        [
            jnp.concatenate([ref[samp, c, :rows, :] for c in range(ref.shape[1])], axis=1)
            for ref in refs
            for samp in range(ref.shape[0])
        ],
        axis=0,
    )
    local_blocks, _, block = top_ref.shape[2:]
    width = min(2, local_blocks)
    for start in range(0, local_blocks, width):
        moved = lax.dot_general(
            left,
            dense_ref[start * block : (start + width) * block, :],
            NT,
            preferred_element_type=F32,
        )
        if start == 0:
            sids = ready()
        for b in range(width):
            for s, sid in enumerate(sids):
                real = moved[s * 16 : s * 16 + 8, b * block : (b + 1) * block]
                imag = moved[s * 16 + 8 : s * 16 + 16, b * block : (b + 1) * block]
                shift_real, shift_imag = shift_ref[sid, start + b], shift_ref[sid + 1, start + b]
                top_ref[base + s, 0, start + b] = real * shift_real - imag * shift_imag
                top_ref[base + s, 1, start + b] = real * shift_imag + imag * shift_real


def spread_rows(src_ref, out_ref):
    count, local_blocks, block = src_ref.shape

    def one(index, carry):
        for b in range(local_blocks):
            out_ref[index, b] = jnp.broadcast_to(src_ref[index, b : b + 1, :], (8, block))
        return carry

    lax.fori_loop(0, count, one, 0)


def tables_kernel(
    idx_ref,
    sid_ref,
    val_hbm,
    near_hbm,
    here_ref,
    shift_ref,
    trans_ref,
    dense_ref,
    wide_shift_ref,
    wide_trans_ref,
    top_ref,
    near_ref,
    val_ref,
    sem,
    *,
    rows,
):
    load = pltpu.make_async_copy(val_hbm, val_ref, sem.at[0])
    load.start()
    other = pltpu.make_async_copy(near_hbm, near_ref, sem.at[1])
    other.start()
    spread_rows(shift_ref, wide_shift_ref)
    spread_rows(trans_ref, wide_trans_ref)
    last = trans_ref.shape[0]
    wide_trans_ref[last:] = jnp.zeros((2, *wide_trans_ref.shape[1:]), F32)
    load.wait()
    local_blocks, _, block, _ = val_ref.shape

    def one(b, carry):
        first, second = idx_ref[0, b], idx_ref[1, b]
        zero = jnp.zeros((block, block), BF16)
        for c in range(dense_ref.shape[1] // block):
            dense_ref[pl.ds(pl.multiple_of(b * block, block), block), c * block : (c + 1) * block] = (
                jnp.where(first == c, val_ref[b, 0], jnp.where(second == c, val_ref[b, 1], zero))
            )
        return carry

    lax.fori_loop(0, local_blocks, one, 0)
    sids = [2 * sid_ref[s] for s in range(sid_ref.shape[0])]
    lift_groups((here_ref,), dense_ref, wide_shift_ref, top_ref, rows, 0, lambda: sids)
    other.wait()


def meta_of(msg_ref, rows):
    return msg_ref[0, 0, rows : rows + 16, :].astype(F32)[8:10]


def field_kernel(
    parent_hbm,
    sid_hbm,
    src_hbm,
    disp_hbm,
    here_ref,
    near_ref,
    far_ref,
    dense_ref,
    shift_ref,
    trans_ref,
    _,
    *rest,
    n_samp,
    leaf_count,
    tile,
):
    outs = rest[:n_samp]
    (
        top_ref,
        parent_ref,
        sid_ref,
        src_ref,
        disp_ref,
        inc_ref,
        down_ref,
        acc_ref,
        meta_ref,
        num_ref,
        head_ref,
        rep_ref,
        count_ref,
        slot_ref,
        coef_ref,
        sem,
    ) = rest[n_samp:]
    block = here_ref.shape[3]
    local_blocks = top_ref.shape[2]
    leaves = top_ref.shape[0]
    group = leaves // 3
    rows = 16 * leaf_count
    top_count, entries = src_ref.shape
    where = lax.axis_index("box")
    me = lax.axis_index("samp")
    turned = jnp.where(me == 1, 1, 0) if n_samp == 2 else jnp.int32(0)
    bases = (1, 2 * turned, 2 - 2 * turned)

    lines = [meta_of(ref, rows) for ref in (here_ref, near_ref, far_ref)]
    meta_ref[...] = jnp.concatenate(lines + lines[:1], axis=0).astype(jnp.int32)
    fetches = [
        pltpu.make_async_copy(src, dst, sem.at[n])
        for n, (src, dst) in enumerate(
            (
                (parent_hbm, parent_ref),
                (sid_hbm, sid_ref),
                (src_hbm, src_ref),
                (disp_hbm, disp_ref),
                (meta_ref, num_ref),
            )
        )
    ]
    for fetch in fetches:
        fetch.start()
    for box in range(3 * top_count):
        head_ref[box] = -1

    def ready():
        for fetch in fetches:
            fetch.wait()
        return [2 * num_ref[line, s] for line in (3, 5) for s in range(group)]

    lift_groups((near_ref, far_ref), dense_ref, shift_ref, top_ref, rows, group, ready)
    boxes = [
        num_ref[2 * (s // group), s % group] + bases[s // group] * top_count for s in range(leaves)
    ]
    for s in reversed(range(leaves)):
        head_ref[boxes[s]] = s
    for s in range(leaves):
        rep_ref[s] = head_ref[boxes[s]]
    for leaf in range(group):
        parent = parent_ref[leaf] - where * top_count
        count = jnp.int32(0)
        slots = [head_ref[src_ref[parent, j] - (where - 1) * top_count] for j in range(entries)]
        coefs = [2 * disp_ref[parent, j] for j in range(entries)]
        for slot, coef in zip(slots, coefs):
            slot_ref[leaf, count] = slot
            coef_ref[leaf, count] = coef
            count += (slot >= 0).astype(jnp.int32)
        slot_ref[leaf, count] = 0
        coef_ref[leaf, count] = trans_ref.shape[0] - 2
        count_ref[leaf] = lax.div(count + 1, 2)

    def merge(s, carry):
        rep = rep_ref[s]

        @pl.when(rep != s)
        def _():
            top_ref[rep] = top_ref[rep] + top_ref[s]

        return carry

    lax.fori_loop(0, leaves, merge, 0)

    def store_down(leaf, b, real, imag):
        sid = 2 * sid_ref[leaf]
        shift_real, shift_imag = shift_ref[sid, b], shift_ref[sid + 1, b]
        down = jnp.concatenate(
            [
                shift_real * real + shift_imag * imag,
                shift_real * imag - shift_imag * real,
            ],
            axis=0,
        )
        start = pl.multiple_of(leaf * 16, 16)
        down_ref[pl.ds(start, 16), b * block : (b + 1) * block] = down.astype(BF16)

    def target(leaf, carry):
        @pl.when(rep_ref[leaf] == leaf)
        def _():
            for t in range(0, local_blocks, tile):

                def entries_of(n, total):
                    real, imag = list(total[:tile]), list(total[tile:])
                    pair = [
                        (slot_ref[leaf, 2 * n + m], coef_ref[leaf, 2 * n + m]) for m in range(2)
                    ]
                    for b in range(tile):
                        place = t + b
                        for slot, coef in pair:
                            move_real, move_imag = trans_ref[coef, place], trans_ref[coef + 1, place]
                            src_real, src_imag = top_ref[slot, 0, place], top_ref[slot, 1, place]
                            real[b] += move_real * src_real - move_imag * src_imag
                            imag[b] += move_real * src_imag + move_imag * src_real
                    return tuple(real + imag)

                zero = jnp.zeros((8, block), F32)
                total = lax.fori_loop(0, count_ref[leaf], entries_of, (zero,) * (2 * tile))
                for b in range(tile):
                    inc_ref[leaf, 0, t + b] = total[b]
                    inc_ref[leaf, 1, t + b] = total[tile + b]
                    store_down(leaf, t + b, total[b], total[tile + b])

        return carry

    lax.fori_loop(0, group, target, 0)

    def lower(leaf, carry):
        rep = rep_ref[leaf]

        @pl.when(rep != leaf)
        def _():
            for b in range(local_blocks):
                store_down(leaf, b, inc_ref[rep, 0, b], inc_ref[rep, 1, b])

        return carry

    lax.fori_loop(0, group, lower, 0)
    acc_ref[...] = jnp.dot(down_ref[...], dense_ref[...], preferred_element_type=F32)
    for d, out in enumerate(outs):
        owner = lax.rem(me + d, n_samp)
        start = pl.multiple_of(owner * rows, rows)
        for c in range(out.shape[0]):
            out[c] = acc_ref[pl.ds(start, rows), c * block : (c + 1) * block].astype(BF16)


def near_kernel(src_ref, near_ref, here_ref, *rest, rows, n_samp):
    other_refs, out_ref, cur_ref = rest[:-2], rest[-2], rest[-1]
    leaf_count, near = near_ref.shape[:2]
    in_blocks = here_ref.shape[1]
    group = n_samp * leaf_count
    where = lax.axis_index("box")
    turned = jnp.where(lax.axis_index("samp") == 1, 1, 0) if n_samp == 2 else jnp.int32(0)
    places = (1, 2 * turned, 2 - 2 * turned)
    for place, ref in zip(places, (here_ref,) + other_refs):
        for leaf in range(group):
            samp, inner = leaf // leaf_count, leaf % leaf_count
            line = rows + inner // in_blocks * 16
            cur = ref[samp, inner % in_blocks, line : line + 16, :].astype(F32)
            cur_ref[place * group + leaf] = jnp.concatenate(
                [cur[:8], -cur[4:8], cur[:4]], axis=0
            ).astype(BF16)
    for leaf in range(leaf_count):
        left = jnp.concatenate(
            [cur_ref[src_ref[leaf, n] - (where - 1) * group] for n in range(near)], axis=1
        )
        out = [
            lax.dot_general(
                left,
                jnp.concatenate([near_ref[leaf, n, r] for n in range(near)], axis=1),
                NT,
                preferred_element_type=F32,
            )
            for r in range(2)
        ]
        out_ref[leaf] = out[0][:8] + out[1][8:]


def receive_kernel(near_ref, rad_ref, *rest):
    far_refs, out_ref = rest[:-1], rest[-1]
    leaf_count = out_ref.shape[0]
    far = far_refs[0][...].astype(F32)
    for ref in far_refs[1:]:
        far = far + ref[...].astype(F32)
    in_blocks = far.shape[0]
    unknowns = rad_ref.shape[4]
    depth = rad_ref.shape[1] * rad_ref.shape[2] * rad_ref.shape[3]
    for leaf in range(leaf_count):
        left = []
        for p in range(2):
            real = [far[b, leaf * 16 + p * 4 : leaf * 16 + p * 4 + 4] for b in range(in_blocks)]
            imag = [
                far[b, leaf * 16 + 8 + p * 4 : leaf * 16 + 12 + p * 4] for b in range(in_blocks)
            ]
            left += [jnp.concatenate(pair, axis=0) for pair in zip(real, imag)]
            left += [jnp.concatenate([i, -r], axis=0) for r, i in zip(real, imag)]
        wide = jnp.concatenate(left, axis=1).astype(BF16)
        right = rad_ref[leaf].reshape(depth, unknowns)
        out_ref[leaf] = near_ref[leaf] + jnp.dot(wide, right, preferred_element_type=F32)


def per_device(
    currents,
    radiation,
    near_blocks,
    near_src,
    leaf_parent,
    leaf_shift,
    shift_table,
    interp_idx,
    interp_val,
    top_src,
    top_disp,
    trans_table,
):
    n_samp = lax.axis_size("samp")
    n_box = lax.axis_size("box")
    leaf_count, comps, unknowns = currents.shape
    group = leaf_parent.shape[0]
    top_count, entries = top_src.shape
    local_blocks, _, block, _ = interp_val.shape
    in_blocks = radiation.shape[3] // block
    leaves = 3 * group
    rows = 16 * leaf_count
    extra = 16 * -(-leaf_count // in_blocks)
    tile = min(16, local_blocks)

    message, phases, moves = pl.pallas_call(
        functools.partial(radiate_kernel, top_count=top_count),
        out_shape=[
            jax.ShapeDtypeStruct((in_blocks, rows + extra, block), BF16),
            pltpu.VMEM(shift_table.shape, BF16),
            pltpu.VMEM(trans_table.shape, BF16),
        ],
        in_specs=[HBM] * 6,
        out_specs=[VMEM] * 3,
        scratch_shapes=[
            pltpu.SMEM(leaf_parent.shape, jnp.int32),
            pltpu.SMEM(leaf_shift.shape, jnp.int32),
            pltpu.VMEM(currents.shape, BF16),
            pltpu.VMEM(radiation.shape, BF16),
            pltpu.SemaphoreType.DMA((leaf_count + 5,)),
        ],
        compiler_params=params(),
        name="radiate",
    )(
        *pinned(
            leaf_parent, leaf_shift, currents, radiation, shift_table, trans_table
        )
    )

    here = lax.all_gather(message, "samp", axis=0)
    last = n_samp - 1
    swap = []
    for box in range(n_box - 1):
        low, high = box * n_samp + last, (box + 1) * n_samp
        swap += [(low, high), (high, low)]
    beyond = lax.ppermute(here, ("box", "samp"), swap)
    shift_rows = phases.astype(F32).reshape(-1, local_blocks, block)
    trans_rows = moves.astype(F32).reshape(-1, local_blocks, block)
    work = 2 * leaves * 16 * in_blocks * block * local_blocks * block
    top_shape = pltpu.VMEM((leaves, 2, local_blocks, 8, block), F32)
    dense, wide_shift, wide_trans, own_top, near_values = pl.pallas_call(
        functools.partial(tables_kernel, rows=rows),
        out_shape=[
            pltpu.VMEM((local_blocks * block, in_blocks * block), BF16),
            pltpu.VMEM((shift_rows.shape[0], local_blocks, 8, block), F32),
            pltpu.VMEM((trans_rows.shape[0] + 2, local_blocks, 8, block), F32),
            top_shape,
            pltpu.VMEM(near_blocks.shape, BF16),
        ],
        in_specs=[SMEM, SMEM, HBM, HBM] + [VMEM] * 3,
        out_specs=[VMEM] * 5,
        scratch_shapes=[pltpu.VMEM(interp_val.shape, BF16), pltpu.SemaphoreType.DMA((2,))],
        compiler_params=params(),
        cost_estimate=pl.CostEstimate(flops=work, bytes_accessed=1 << 24, transcendentals=0),
        name="tables",
    )(interp_idx.T, leaf_shift, *pinned(interp_val, near_blocks), here, shift_rows, trans_rows)
    beyond, dense = lax.optimization_barrier((beyond, dense))
    if n_samp == 2:
        first = beyond
        second = lax.ppermute(beyond, "samp", [(0, 1), (1, 0)])
    else:
        ends = lax.all_gather(beyond, "samp", axis=0)
        first, second = ends[0], ends[n_samp - 1]
    numbers = [pltpu.VMEM((8, block), jnp.int32), pltpu.SMEM((8, block), jnp.int32)]
    sources = (here, first) if n_samp == 2 else (here, first, second)
    near_out = pl.pallas_call(
        functools.partial(near_kernel, rows=rows, n_samp=n_samp),
        out_shape=jax.ShapeDtypeStruct((leaf_count, comps, unknowns), F32),
        in_specs=[SMEM] + [VMEM] * (1 + len(sources)),
        out_specs=VMEM,
        scratch_shapes=[pltpu.VMEM((leaves, 16, block), BF16)],
        compiler_params=params(),
        cost_estimate=pl.CostEstimate(flops=work, bytes_accessed=1 << 22, transcendentals=0),
        name="near",
    )(near_src, near_values, *sources)
    second, near_out = lax.optimization_barrier((second, near_out))

    *fars, _ = pl.pallas_call(
        functools.partial(field_kernel, n_samp=n_samp, leaf_count=leaf_count, tile=tile),
        out_shape=[jax.ShapeDtypeStruct((in_blocks, rows, block), BF16)] * n_samp
        + [top_shape],
        in_specs=[HBM] * 4 + [VMEM] * 7,
        out_specs=[VMEM] * (n_samp + 1),
        scratch_shapes=[
            pltpu.SMEM(leaf_parent.shape, jnp.int32),
            pltpu.SMEM(leaf_shift.shape, jnp.int32),
            pltpu.SMEM(top_src.shape, jnp.int32),
            pltpu.SMEM(top_disp.shape, jnp.int32),
            pltpu.VMEM((group, 2, local_blocks, 8, block), F32),
            pltpu.VMEM((group * 16, local_blocks * block), BF16),
            pltpu.VMEM((group * 16, in_blocks * block), F32),
            *numbers,
            pltpu.SMEM((3 * top_count,), jnp.int32),
            pltpu.SMEM((leaves,), jnp.int32),
            pltpu.SMEM((group,), jnp.int32),
            pltpu.SMEM((group, entries + 1), jnp.int32),
            pltpu.SMEM((group, entries + 1), jnp.int32),
            pltpu.SemaphoreType.DMA((5,)),
        ],
        input_output_aliases={10: n_samp},
        compiler_params=params(),
        name="field",
    )(
        *pinned(leaf_parent, leaf_shift, top_src, top_disp),
        here,
        first,
        second,
        dense,
        wide_shift,
        wide_trans,
        own_top,
    )
    received = [fars[0]] + [
        lax.ppermute(fars[d], "samp", [(i, (i + d) % n_samp) for i in range(n_samp)])
        for d in range(1, n_samp)
    ]
    return pl.pallas_call(
        receive_kernel,
        out_shape=jax.ShapeDtypeStruct((leaf_count, comps, unknowns), F32),
        in_specs=[VMEM] * (2 + n_samp),
        out_specs=VMEM,
        compiler_params=params(),
        name="receive",
    )(near_out, radiation, *received)


def solution(mesh):
    placed = (
        P(("box", "samp"), None, None),
        P(("box", "samp"), None, None, None, None),
        P(("box", "samp"), None, None, None, None),
        P(("box", "samp"), None),
        P("box"),
        P("box"),
        P(None, None, "samp"),
        P("samp", None),
        P("samp", None, None, None),
        P("box", None),
        P("box", None),
        P(None, None, "samp"),
    )
    return jax.shard_map(
        per_device,
        mesh=mesh,
        in_specs=placed,
        out_specs=P(("box", "samp"), None, None),
        check_vma=False,
    )
```

```python
import functools

import jax
import jax.numpy as jnp
from jax import lax
from jax.experimental import pallas as pl
from jax.experimental.pallas import tpu as pltpu
from jax.sharding import PartitionSpec as P

F32 = jnp.float32
BF16 = jnp.bfloat16
HBM = pl.BlockSpec(memory_space=pltpu.HBM)
VMEM = pl.BlockSpec(memory_space=pltpu.VMEM)
SMEM = pl.BlockSpec(memory_space=pltpu.SMEM)
NT = (((1,), (1,)), ((), ()))
LIMIT = 14 * 1024 * 1024


def params():
    return pltpu.CompilerParams(vmem_limit_bytes=LIMIT)


def pinned(*arrays):
    return [pltpu.with_memory_space_constraint(array, pltpu.HBM) for array in arrays]


def radiate_kernel(
    parent_hbm,
    shift_hbm,
    cur_hbm,
    rad_hbm,
    phase_hbm,
    trans_hbm,
    msg_ref,
    phase_ref,
    trans_ref,
    parent_ref,
    shift_ref,
    cur_ref,
    rad_ref,
    sem,
    *,
    top_count,
):
    leaf_count, in_blocks = cur_ref.shape[0], msg_ref.shape[0]
    block = msg_ref.shape[2]
    half = cur_ref.shape[1] // 2
    group = parent_ref.shape[0]
    firsts = [
        pltpu.make_async_copy(src, dst, sem.at[leaf_count + n])
        for n, (src, dst) in enumerate(
            ((parent_hbm, parent_ref), (shift_hbm, shift_ref), (cur_hbm, cur_ref))
        )
    ]
    for copy in firsts:
        copy.start()
    copies = [
        pltpu.make_async_copy(rad_hbm.at[leaf], rad_ref.at[leaf], sem.at[leaf])
        for leaf in range(leaf_count)
    ]
    for copy in copies:
        copy.start()
    later = [
        pltpu.make_async_copy(src, dst, sem.at[leaf_count + 3 + n])
        for n, (src, dst) in enumerate(
            ((trans_hbm, trans_ref), (phase_hbm, phase_ref))
        )
    ]
    for copy in later:
        copy.start()
    base = leaf_count * 4 * half
    lane = lax.broadcasted_iota(jnp.int32, (8, block), 1)
    line = lax.broadcasted_iota(jnp.int32, (8, block), 0)
    meta = jnp.zeros((8, block), jnp.int32)
    for copy in firsts:
        copy.wait()
    for member in range(group):
        pair = jnp.where(
            line == 0, lax.rem(parent_ref[member], top_count), shift_ref[member]
        )
        meta = jnp.where(lane == member, pair, meta)
    meta = meta.astype(F32)
    zero = jnp.zeros((half, cur_ref.shape[2]), F32)
    left = []
    for leaf in range(leaf_count):
        cur = cur_ref[leaf].astype(F32)
        real, imag = cur[:half], cur[half:]
        pieces = [
            jnp.concatenate(rows, axis=0).astype(BF16)
            for rows in (
                (real, zero, imag, zero),
                (-imag, zero, real, zero),
                (zero, real, zero, imag),
                (zero, -imag, zero, real),
            )
        ]
        left.append(jnp.concatenate(pieces, axis=1))
        row = base + leaf // in_blocks * 4 * half
        msg_ref[leaf % in_blocks, row : row + 4 * half, :] = jnp.concatenate(
            [cur, meta], axis=0
        ).astype(BF16)
    for leaf in range(leaf_count):
        copies[leaf].wait()
        right = jnp.concatenate(
            [rad_ref[leaf, p, r] for p in range(2) for r in range(2)], axis=1
        )
        out = lax.dot_general(left[leaf], right, NT, preferred_element_type=F32).astype(BF16)
        for b in range(in_blocks):
            msg_ref[b, leaf * 4 * half : (leaf + 1) * 4 * half, :] = out[
                :, b * block : (b + 1) * block
            ]
    for copy in later:
        copy.wait()


def lift_groups(refs, dense_ref, shift_ref, top_ref, rows, base, ready):
    left = jnp.concatenate(
        [
            jnp.concatenate([ref[samp, c, :rows, :] for c in range(ref.shape[1])], axis=1)
            for ref in refs
            for samp in range(ref.shape[0])
        ],
        axis=0,
    )
    local_blocks, _, block = top_ref.shape[2:]
    width = min(4, local_blocks)
    for start in range(0, local_blocks, width):
        moved = lax.dot_general(
            left,
            dense_ref[start * block : (start + width) * block, :],
            NT,
            preferred_element_type=F32,
        )
        if start == 0:
            sids = ready()
        for b in range(width):
            for s, sid in enumerate(sids):
                real = moved[s * 16 : s * 16 + 8, b * block : (b + 1) * block]
                imag = moved[s * 16 + 8 : s * 16 + 16, b * block : (b + 1) * block]
                shift_real, shift_imag = shift_ref[sid, start + b], shift_ref[sid + 1, start + b]
                top_ref[base + s, 0, start + b] = real * shift_real - imag * shift_imag
                top_ref[base + s, 1, start + b] = real * shift_imag + imag * shift_real


def spread_rows(src_ref, out_ref):
    count, local_blocks, block = src_ref.shape

    def one(index, carry):
        for b in range(local_blocks):
            out_ref[index, b] = jnp.broadcast_to(src_ref[index, b : b + 1, :], (8, block))
        return carry

    lax.fori_loop(0, count, one, 0)


def tables_kernel(
    idx_ref,
    sid_ref,
    val_hbm,
    near_hbm,
    here_ref,
    shift_ref,
    trans_ref,
    dense_ref,
    wide_shift_ref,
    wide_trans_ref,
    top_ref,
    near_ref,
    val_ref,
    sem,
    *,
    rows,
):
    load = pltpu.make_async_copy(val_hbm, val_ref, sem.at[0])
    load.start()
    other = pltpu.make_async_copy(near_hbm, near_ref, sem.at[1])
    other.start()
    spread_rows(shift_ref, wide_shift_ref)
    spread_rows(trans_ref, wide_trans_ref)
    last = trans_ref.shape[0]
    wide_trans_ref[last:] = jnp.zeros((2, *wide_trans_ref.shape[1:]), F32)
    load.wait()
    local_blocks, _, block, _ = val_ref.shape

    def one(b, carry):
        first, second = idx_ref[0, b], idx_ref[1, b]
        zero = jnp.zeros((block, block), BF16)
        for c in range(dense_ref.shape[1] // block):
            dense_ref[pl.ds(pl.multiple_of(b * block, block), block), c * block : (c + 1) * block] = (
                jnp.where(first == c, val_ref[b, 0], jnp.where(second == c, val_ref[b, 1], zero))
            )
        return carry

    lax.fori_loop(0, local_blocks, one, 0)
    sids = [2 * sid_ref[s] for s in range(sid_ref.shape[0])]
    lift_groups((here_ref,), dense_ref, wide_shift_ref, top_ref, rows, 0, lambda: sids)
    other.wait()


def meta_of(msg_ref, rows):
    return msg_ref[0, 0, rows : rows + 16, :].astype(F32)[8:10]


def field_kernel(
    parent_hbm,
    sid_hbm,
    src_hbm,
    disp_hbm,
    here_ref,
    near_ref,
    far_ref,
    dense_ref,
    shift_ref,
    trans_ref,
    _,
    *rest,
    n_samp,
    leaf_count,
    tile,
):
    outs = rest[:n_samp]
    (
        top_ref,
        parent_ref,
        sid_ref,
        src_ref,
        disp_ref,
        inc_ref,
        down_ref,
        acc_ref,
        meta_ref,
        num_ref,
        head_ref,
        rep_ref,
        count_ref,
        slot_ref,
        coef_ref,
        sem,
    ) = rest[n_samp:]
    block = here_ref.shape[3]
    local_blocks = top_ref.shape[2]
    leaves = top_ref.shape[0]
    group = leaves // 3
    rows = 16 * leaf_count
    top_count, entries = src_ref.shape
    where = lax.axis_index("box")
    me = lax.axis_index("samp")
    turned = jnp.where(me == 1, 1, 0) if n_samp == 2 else jnp.int32(0)
    bases = (1, 2 * turned, 2 - 2 * turned)

    lines = [meta_of(ref, rows) for ref in (here_ref, near_ref, far_ref)]
    meta_ref[...] = jnp.concatenate(lines + lines[:1], axis=0).astype(jnp.int32)
    fetches = [
        pltpu.make_async_copy(src, dst, sem.at[n])
        for n, (src, dst) in enumerate(
            (
                (parent_hbm, parent_ref),
                (sid_hbm, sid_ref),
                (src_hbm, src_ref),
                (disp_hbm, disp_ref),
                (meta_ref, num_ref),
            )
        )
    ]
    for fetch in fetches:
        fetch.start()
    for box in range(3 * top_count):
        head_ref[box] = -1

    def ready():
        for fetch in fetches:
            fetch.wait()
        return [2 * num_ref[line, s] for line in (3, 5) for s in range(group)]

    lift_groups((near_ref, far_ref), dense_ref, shift_ref, top_ref, rows, group, ready)
    boxes = [
        num_ref[2 * (s // group), s % group] + bases[s // group] * top_count for s in range(leaves)
    ]
    for s in reversed(range(leaves)):
        head_ref[boxes[s]] = s
    for s in range(leaves):
        rep_ref[s] = head_ref[boxes[s]]
    for leaf in range(group):
        parent = parent_ref[leaf] - where * top_count
        count = jnp.int32(0)
        slots = [head_ref[src_ref[parent, j] - (where - 1) * top_count] for j in range(entries)]
        coefs = [2 * disp_ref[parent, j] for j in range(entries)]
        for slot, coef in zip(slots, coefs):
            slot_ref[leaf, count] = slot
            coef_ref[leaf, count] = coef
            count += (slot >= 0).astype(jnp.int32)
        slot_ref[leaf, count] = 0
        coef_ref[leaf, count] = trans_ref.shape[0] - 2
        count_ref[leaf] = lax.div(count + 1, 2)

    def merge(s):
        rep = rep_ref[s]

        @pl.when(rep != s)
        def _():
            top_ref[rep] = top_ref[rep] + top_ref[s]

    for s in range(1, leaves):
        merge(s)

    def store_down(leaf, b, real, imag):
        sid = 2 * sid_ref[leaf]
        shift_real, shift_imag = shift_ref[sid, b], shift_ref[sid + 1, b]
        down = jnp.concatenate(
            [
                shift_real * real + shift_imag * imag,
                shift_real * imag - shift_imag * real,
            ],
            axis=0,
        )
        start = pl.multiple_of(leaf * 16, 16)
        down_ref[pl.ds(start, 16), b * block : (b + 1) * block] = down.astype(BF16)

    def target(leaf, carry):
        @pl.when(rep_ref[leaf] == leaf)
        def _():
            for t in range(0, local_blocks, tile):

                def entries_of(n, total):
                    real, imag = list(total[:tile]), list(total[tile:])
                    pair = [
                        (slot_ref[leaf, 2 * n + m], coef_ref[leaf, 2 * n + m]) for m in range(2)
                    ]
                    for b in range(tile):
                        place = t + b
                        for slot, coef in pair:
                            move_real, move_imag = trans_ref[coef, place], trans_ref[coef + 1, place]
                            src_real, src_imag = top_ref[slot, 0, place], top_ref[slot, 1, place]
                            real[b] += move_real * src_real - move_imag * src_imag
                            imag[b] += move_real * src_imag + move_imag * src_real
                    return tuple(real + imag)

                zero = jnp.zeros((8, block), F32)
                total = lax.fori_loop(0, count_ref[leaf], entries_of, (zero,) * (2 * tile))
                for b in range(tile):
                    inc_ref[leaf, 0, t + b] = total[b]
                    inc_ref[leaf, 1, t + b] = total[tile + b]
                    store_down(leaf, t + b, total[b], total[tile + b])

        return carry

    lax.fori_loop(0, group, target, 0)

    def lower(leaf, carry):
        rep = rep_ref[leaf]

        @pl.when(rep != leaf)
        def _():
            for b in range(local_blocks):
                store_down(leaf, b, inc_ref[rep, 0, b], inc_ref[rep, 1, b])

        return carry

    lax.fori_loop(0, group, lower, 0)
    acc_ref[...] = jnp.dot(down_ref[...], dense_ref[...], preferred_element_type=F32)
    for d, out in enumerate(outs):
        owner = lax.rem(me + d, n_samp)
        start = pl.multiple_of(owner * rows, rows)
        for c in range(out.shape[0]):
            out[c] = acc_ref[pl.ds(start, rows), c * block : (c + 1) * block].astype(BF16)


def near_kernel(src_ref, near_ref, here_ref, *rest, rows, n_samp):
    other_refs, out_ref, cur_ref = rest[:-2], rest[-2], rest[-1]
    leaf_count, near = near_ref.shape[:2]
    in_blocks = here_ref.shape[1]
    group = n_samp * leaf_count
    where = lax.axis_index("box")
    turned = jnp.where(lax.axis_index("samp") == 1, 1, 0) if n_samp == 2 else jnp.int32(0)
    places = (1, 2 * turned, 2 - 2 * turned)
    for place, ref in zip(places, (here_ref,) + other_refs):
        for leaf in range(group):
            samp, inner = leaf // leaf_count, leaf % leaf_count
            line = rows + inner // in_blocks * 16
            cur = ref[samp, inner % in_blocks, line : line + 16, :].astype(F32)
            cur_ref[place * group + leaf] = jnp.concatenate(
                [cur[:8], -cur[4:8], cur[:4]], axis=0
            ).astype(BF16)
    for leaf in range(leaf_count):
        left = jnp.concatenate(
            [cur_ref[src_ref[leaf, n] - (where - 1) * group] for n in range(near)], axis=1
        )
        out = [
            lax.dot_general(
                left,
                jnp.concatenate([near_ref[leaf, n, r] for n in range(near)], axis=1),
                NT,
                preferred_element_type=F32,
            )
            for r in range(2)
        ]
        out_ref[leaf] = out[0][:8] + out[1][8:]


def receive_kernel(near_ref, rad_ref, *rest):
    far_refs, out_ref = rest[:-1], rest[-1]
    leaf_count = out_ref.shape[0]
    far = far_refs[0][...].astype(F32)
    for ref in far_refs[1:]:
        far = far + ref[...].astype(F32)
    in_blocks = far.shape[0]
    unknowns = rad_ref.shape[4]
    depth = rad_ref.shape[1] * rad_ref.shape[2] * rad_ref.shape[3]
    for leaf in range(leaf_count):
        left = []
        for p in range(2):
            real = [far[b, leaf * 16 + p * 4 : leaf * 16 + p * 4 + 4] for b in range(in_blocks)]
            imag = [
                far[b, leaf * 16 + 8 + p * 4 : leaf * 16 + 12 + p * 4] for b in range(in_blocks)
            ]
            left += [jnp.concatenate(pair, axis=0) for pair in zip(real, imag)]
            left += [jnp.concatenate([i, -r], axis=0) for r, i in zip(real, imag)]
        wide = jnp.concatenate(left, axis=1).astype(BF16)
        right = rad_ref[leaf].reshape(depth, unknowns)
        out_ref[leaf] = near_ref[leaf] + jnp.dot(wide, right, preferred_element_type=F32)


def per_device(
    currents,
    radiation,
    near_blocks,
    near_src,
    leaf_parent,
    leaf_shift,
    shift_table,
    interp_idx,
    interp_val,
    top_src,
    top_disp,
    trans_table,
):
    n_samp = lax.axis_size("samp")
    n_box = lax.axis_size("box")
    leaf_count, comps, unknowns = currents.shape
    group = leaf_parent.shape[0]
    top_count, entries = top_src.shape
    local_blocks, _, block, _ = interp_val.shape
    in_blocks = radiation.shape[3] // block
    leaves = 3 * group
    rows = 16 * leaf_count
    extra = 16 * -(-leaf_count // in_blocks)
    tile = min(16, local_blocks)

    message, phases, moves = pl.pallas_call(
        functools.partial(radiate_kernel, top_count=top_count),
        out_shape=[
            jax.ShapeDtypeStruct((in_blocks, rows + extra, block), BF16),
            pltpu.VMEM(shift_table.shape, BF16),
            pltpu.VMEM(trans_table.shape, BF16),
        ],
        in_specs=[HBM] * 6,
        out_specs=[VMEM] * 3,
        scratch_shapes=[
            pltpu.SMEM(leaf_parent.shape, jnp.int32),
            pltpu.SMEM(leaf_shift.shape, jnp.int32),
            pltpu.VMEM(currents.shape, BF16),
            pltpu.VMEM(radiation.shape, BF16),
            pltpu.SemaphoreType.DMA((leaf_count + 5,)),
        ],
        compiler_params=params(),
        name="radiate",
    )(
        *pinned(
            leaf_parent, leaf_shift, currents, radiation, shift_table, trans_table
        )
    )

    here = lax.all_gather(message, "samp", axis=0)
    last = n_samp - 1
    swap = []
    for box in range(n_box - 1):
        low, high = box * n_samp + last, (box + 1) * n_samp
        swap += [(low, high), (high, low)]
    beyond = lax.ppermute(here, ("box", "samp"), swap)
    shift_rows = phases.astype(F32).reshape(-1, local_blocks, block)
    trans_rows = moves.astype(F32).reshape(-1, local_blocks, block)
    work = 2 * leaves * 16 * in_blocks * block * local_blocks * block
    top_shape = pltpu.VMEM((leaves, 2, local_blocks, 8, block), F32)
    dense, wide_shift, wide_trans, own_top, near_values = pl.pallas_call(
        functools.partial(tables_kernel, rows=rows),
        out_shape=[
            pltpu.VMEM((local_blocks * block, in_blocks * block), BF16),
            pltpu.VMEM((shift_rows.shape[0], local_blocks, 8, block), F32),
            pltpu.VMEM((trans_rows.shape[0] + 2, local_blocks, 8, block), F32),
            top_shape,
            pltpu.VMEM(near_blocks.shape, BF16),
        ],
        in_specs=[SMEM, SMEM, HBM, HBM] + [VMEM] * 3,
        out_specs=[VMEM] * 5,
        scratch_shapes=[pltpu.VMEM(interp_val.shape, BF16), pltpu.SemaphoreType.DMA((2,))],
        compiler_params=params(),
        cost_estimate=pl.CostEstimate(flops=work, bytes_accessed=1 << 24, transcendentals=0),
        name="tables",
    )(interp_idx.T, leaf_shift, *pinned(interp_val, near_blocks), here, shift_rows, trans_rows)
    beyond, dense = lax.optimization_barrier((beyond, dense))
    if n_samp == 2:
        first = beyond
        second = lax.ppermute(beyond, "samp", [(0, 1), (1, 0)])
    else:
        ends = lax.all_gather(beyond, "samp", axis=0)
        first, second = ends[0], ends[n_samp - 1]
    numbers = [pltpu.VMEM((8, block), jnp.int32), pltpu.SMEM((8, block), jnp.int32)]
    sources = (here, first) if n_samp == 2 else (here, first, second)
    near_out = pl.pallas_call(
        functools.partial(near_kernel, rows=rows, n_samp=n_samp),
        out_shape=jax.ShapeDtypeStruct((leaf_count, comps, unknowns), F32),
        in_specs=[SMEM] + [VMEM] * (1 + len(sources)),
        out_specs=VMEM,
        scratch_shapes=[pltpu.VMEM((leaves, 16, block), BF16)],
        compiler_params=params(),
        cost_estimate=pl.CostEstimate(flops=work, bytes_accessed=1 << 22, transcendentals=0),
        name="near",
    )(near_src, near_values, *sources)
    second, near_out = lax.optimization_barrier((second, near_out))

    *fars, _ = pl.pallas_call(
        functools.partial(field_kernel, n_samp=n_samp, leaf_count=leaf_count, tile=tile),
        out_shape=[jax.ShapeDtypeStruct((in_blocks, rows, block), BF16)] * n_samp
        + [top_shape],
        in_specs=[HBM] * 4 + [VMEM] * 7,
        out_specs=[VMEM] * (n_samp + 1),
        scratch_shapes=[
            pltpu.SMEM(leaf_parent.shape, jnp.int32),
            pltpu.SMEM(leaf_shift.shape, jnp.int32),
            pltpu.SMEM(top_src.shape, jnp.int32),
            pltpu.SMEM(top_disp.shape, jnp.int32),
            pltpu.VMEM((group, 2, local_blocks, 8, block), F32),
            pltpu.VMEM((group * 16, local_blocks * block), BF16),
            pltpu.VMEM((group * 16, in_blocks * block), F32),
            *numbers,
            pltpu.SMEM((3 * top_count,), jnp.int32),
            pltpu.SMEM((leaves,), jnp.int32),
            pltpu.SMEM((group,), jnp.int32),
            pltpu.SMEM((group, entries + 1), jnp.int32),
            pltpu.SMEM((group, entries + 1), jnp.int32),
            pltpu.SemaphoreType.DMA((5,)),
        ],
        input_output_aliases={10: n_samp},
        compiler_params=params(),
        name="field",
    )(
        *pinned(leaf_parent, leaf_shift, top_src, top_disp),
        here,
        first,
        second,
        dense,
        wide_shift,
        wide_trans,
        own_top,
    )
    received = [fars[0]] + [
        lax.ppermute(fars[d], "samp", [(i, (i + d) % n_samp) for i in range(n_samp)])
        for d in range(1, n_samp)
    ]
    return pl.pallas_call(
        receive_kernel,
        out_shape=jax.ShapeDtypeStruct((leaf_count, comps, unknowns), F32),
        in_specs=[VMEM] * (2 + n_samp),
        out_specs=VMEM,
        compiler_params=params(),
        name="receive",
    )(near_out, radiation, *received)


def solution(mesh):
    placed = (
        P(("box", "samp"), None, None),
        P(("box", "samp"), None, None, None, None),
        P(("box", "samp"), None, None, None, None),
        P(("box", "samp"), None),
        P("box"),
        P("box"),
        P(None, None, "samp"),
        P("samp", None),
        P("samp", None, None, None),
        P("box", None),
        P("box", None),
        P(None, None, "samp"),
    )
    return jax.shard_map(
        per_device,
        mesh=mesh,
        in_specs=placed,
        out_specs=P(("box", "samp"), None, None),
        check_vma=False,
    )
```
